128 devices in a mesh: row: 8 (over x, core), col: 16 (over z, y).
Axes of the slice: x: 4, y: 4, z: 4, core: 2. Of those that a mesh axis runs over, the one named last changes fastest.
Arguments:
- force: float32 [3, 128, 256, 512], P(None, 'row', 'col'), may hold values from -8 to 8
- multiplier: float32 [6, 128, 256, 512], P(None, 'row', 'col'), may hold values from -6 to 6
- strain_aux: float32 [6, 128, 256, 512], P(None, 'row', 'col'), may hold values from -4 to 4
- entry_lines: int32 [16384], P(('row', 'col')), may hold values from 0 to 1023, as said below
- entry_owner: int32 [16384, 1], P(('row', 'col')), may hold values from 0 to 127, as said below
- entry_slot: int32 [16384], P(('row', 'col')), may hold values from 0 to 71
Outputs:
- velocity: float32 [3, 128, 256, 512], P(None, 'row', 'col')
- new_aux: float32 [6, 128, 256, 512], P(None, 'row', 'col')
- new_multiplier: float32 [6, 128, 256, 512], P(None, 'row', 'col')
The draws below stay inside these ranges and needn't reach their ends.
Inputs may be any that keep to these rules, and one draw needn't show every extreme that they name: `entry_owner`: margins come in runs of four consecutive entries naming one owner and one slot. Among the margins listed on one device, no owner is named more than 4 times (one run), and the listing device itself exactly 4 times. `entry_lines`: each run of four consecutive margins covers a 2 x 2 patch of neighbouring lines in y and z with the same x block.
All inputs are finite; a program needn't handle non-finite values.
Results may differ from the reference program's by a relative error of at most 0.0003.
Values sent between devices are 32-bit elements; how exact they have to be, the bound alone decides.
A program may use at most 192 MiB of HBM per device.

```python
import math
import jax
import jax.numpy as jnp
from jax import lax

NX = 512
BL = 128
CY = 16
CZ = 16
NPD = 72
ENT = 128
NY = 128
NZ = 256
N_ROW = 8
N_COL = 16


def layout(key):
    devices = N_ROW * N_COL
    groups = ENT // 4
    per_line = NX // BL
    key_perm, key_order, key_ys, key_zs, key_x, key_slot = jax.random.split(key, 6)
    others = jnp.arange(1, devices, dtype=jnp.int32)[None, :] + jnp.zeros((devices, 1), jnp.int32)
    others = jax.random.permutation(key_perm, others, axis=1, independent=True)
    offsets = jnp.concatenate([jnp.zeros((devices, 1), jnp.int32), others[:, :groups - 1]], axis=1)
    offsets = jax.random.permutation(key_order, offsets, axis=1, independent=True)
    device_ids = jnp.arange(devices, dtype=jnp.int32)[:, None]
    owners = (device_ids + offsets) % devices
    start_y = jax.random.randint(key_ys, (devices, groups), 0, CY - 1)
    start_z = jax.random.randint(key_zs, (devices, groups), 0, CZ - 1)
    block_x = jax.random.randint(key_x, (devices, groups), 0, per_line)
    slots = jax.random.randint(key_slot, (devices, groups), 0, NPD)
    quads = jnp.arange(4, dtype=jnp.int32)[None, None, :]
    lines = ((start_y[:, :, None] + quads // 2) * CZ + start_z[:, :, None] + quads % 2) * per_line + block_x[:, :, None]
    owners4 = owners[:, :, None] + jnp.zeros((1, 1, 4), jnp.int32)
    slots4 = slots[:, :, None] + jnp.zeros((1, 1, 4), jnp.int32)
    return (lines.reshape(-1).astype(jnp.int32), owners4.reshape(-1, 1).astype(jnp.int32), slots4.reshape(-1).astype(jnp.int32))


def draw_entry_lines(key, part):
    return layout(key)[0]


def draw_entry_owner(key, part):
    return layout(key)[1]


def draw_entry_slot(key, part):
    return layout(key)[2]


def level_of(rng, dims, cuts, least, largest):
    level = 1.0
    for axis_at, shards_of in cuts:
        steps = jax.random.uniform(jax.random.fold_in(jax.random.fold_in(rng, 6), axis_at), (shards_of,), jnp.float32, least / len(cuts), largest / len(cuts))
        level = level * jnp.repeat(jnp.exp(steps), dims[axis_at] // shards_of).reshape((-1,) + (1,) * (len(dims) - 1 - axis_at))
    return level


def bell_draw(stream_key, shape, width, reach, cuts=(), kind=jnp.bfloat16):
    array = width * jax.random.normal(stream_key, shape, jnp.float32)
    if cuts:
        array = array * level_of(stream_key, shape, cuts, -0.22, 0.18)
    return jnp.clip(array, -reach, reach).astype(kind)


def setup_inputs(seed: int = 0) -> dict:
    arg_keys = jax.random.split(jax.random.key(seed), 7)
    return {
        "force": bell_draw(arg_keys[0], (3, NY, NZ, NX), 2.0, 8.0, ((1, 8), (2, 16)), jnp.float32),
        "multiplier": bell_draw(arg_keys[1], (6, NY, NZ, NX), 1.0, 6.0, ((1, 8), (2, 16)), jnp.float32),
        "strain_aux": bell_draw(arg_keys[2], (6, NY, NZ, NX), 0.3, 4.0, ((1, 8), (2, 16)), jnp.float32),
        "entry_lines": draw_entry_lines(jax.random.fold_in(arg_keys[6], 71), 0),
        "entry_owner": draw_entry_owner(jax.random.fold_in(arg_keys[6], 71), 0),
        "entry_slot": draw_entry_slot(jax.random.fold_in(arg_keys[6], 71), 0),
    }


mass_coef = 0.02
visc_coef = 10.0
penalty = 5.0
yield_stress = 2.0

def centered(lower2, lower1, upper1, upper2):
    return (8.0 * (upper1 - lower1) - (upper2 - lower2)) / 12.0

def deriv(field, axis):
    return centered(jnp.roll(field, 2, axis), jnp.roll(field, 1, axis), jnp.roll(field, -1, axis), jnp.roll(field, -2, axis))

def wave(total):
    marks = jnp.arange(total, dtype=jnp.int32)
    signed = jnp.where(marks < total // 2, marks, marks - total)
    waves = signed.astype(jnp.float32) * (2.0 * math.pi / total)
    keeper = (marks != total // 2).astype(jnp.float32)
    return (waves, keeper)

def stokes(rhs):
    spectra = jnp.fft.fftn(rhs, axes=(1, 2, 3))
    wave_y, keep_y = wave(NY)
    wave_z, keep_z = wave(NZ)
    wave_x, keep_x = wave(NX)
    wave_y, keep_y = (wave_y.reshape(NY, 1, 1), keep_y.reshape(NY, 1, 1))
    wave_z, keep_z = (wave_z.reshape(1, NZ, 1), keep_z.reshape(1, NZ, 1))
    wave_x, keep_x = (wave_x.reshape(1, 1, NX), keep_x.reshape(1, 1, NX))
    dotk = wave_x * spectra[0] + wave_y * spectra[1] + wave_z * spectra[2]
    ksq = wave_x * wave_x + wave_y * wave_y + wave_z * wave_z
    ksafe = jnp.where(ksq > 0, ksq, 1.0)
    gain = keep_x * keep_y * keep_z / (mass_coef + visc_coef * ksq)
    solved = jnp.stack([(spectra[0] - wave_x * dotk / ksafe) * gain, (spectra[1] - wave_y * dotk / ksafe) * gain, (spectra[2] - wave_z * dotk / ksafe) * gain])
    return jnp.real(jnp.fft.ifftn(solved, axes=(1, 2, 3))).astype(jnp.float32)

def project(fluid, entry_lines, entry_owner, entry_slot):
    nxb = NX // BL
    count = entry_lines.shape[0]
    devs = jnp.arange(count, dtype=jnp.int32) // ENT
    row_id = devs // N_COL
    col_id = devs % N_COL
    line_y = entry_lines // (CZ * nxb)
    line_z = entry_lines // nxb % CZ
    line_b = entry_lines % nxb
    glob_y = row_id * CY + line_y
    glob_z = col_id * CZ + line_z
    glob_x = line_b * BL
    nparts = N_ROW * N_COL * NPD
    particle = entry_owner[:, 0] * NPD + entry_slot
    grid5 = fluid.reshape(3, NY, NZ, nxb, BL)
    blocks = grid5[:, glob_y, glob_z, line_b]
    xs = glob_x.astype(jnp.float32)[:, None] + jnp.arange(BL, dtype=jnp.float32)[None, :]
    ys = glob_y.astype(jnp.float32)
    zs = glob_z.astype(jnp.float32)
    ones = jnp.full((count,), float(BL), jnp.float32)
    cells = jax.ops.segment_sum(ones, particle, nparts)
    safe_n = jnp.maximum(cells, 1.0)
    center_x = jax.ops.segment_sum(lax.optimization_barrier(jnp.sum(xs, axis=1)), particle, nparts) / safe_n
    center_y = jax.ops.segment_sum(ones * ys, particle, nparts) / safe_n
    center_z = jax.ops.segment_sum(ones * zs, particle, nparts) / safe_n
    rel_x = xs - center_x[particle][:, None]
    rel_y = (ys - center_y[particle])[:, None] + jnp.zeros((1, BL), jnp.float32)
    rel_z = (zs - center_z[particle])[:, None] + jnp.zeros((1, BL), jnp.float32)
    vel_x, vel_y, vel_z = (blocks[0], blocks[1], blocks[2])
    mean_x = jax.ops.segment_sum(lax.optimization_barrier(jnp.sum(vel_x, axis=1)), particle, nparts) / safe_n
    mean_y = jax.ops.segment_sum(lax.optimization_barrier(jnp.sum(vel_y, axis=1)), particle, nparts) / safe_n
    mean_z = jax.ops.segment_sum(lax.optimization_barrier(jnp.sum(vel_z, axis=1)), particle, nparts) / safe_n
    mom_x = jax.ops.segment_sum(lax.optimization_barrier(jnp.sum(rel_y * vel_z - rel_z * vel_y, axis=1)), particle, nparts)
    mom_y = jax.ops.segment_sum(lax.optimization_barrier(jnp.sum(rel_z * vel_x - rel_x * vel_z, axis=1)), particle, nparts)
    mom_z = jax.ops.segment_sum(lax.optimization_barrier(jnp.sum(rel_x * vel_y - rel_y * vel_x, axis=1)), particle, nparts)
    spread = jax.ops.segment_sum(lax.optimization_barrier(jnp.sum(rel_x * rel_x + rel_y * rel_y + rel_z * rel_z, axis=1)), particle, nparts)
    inertia = jnp.maximum(spread * (2.0 / 3.0), 1.0)
    spin_x = (mom_x / inertia)[particle][:, None]
    spin_y = (mom_y / inertia)[particle][:, None]
    spin_z = (mom_z / inertia)[particle][:, None]
    rigid_x = mean_x[particle][:, None] + spin_y * rel_z - spin_z * rel_y
    rigid_y = mean_y[particle][:, None] + spin_z * rel_x - spin_x * rel_z
    rigid_z = mean_z[particle][:, None] + spin_x * rel_y - spin_y * rel_x
    correction = jnp.stack([rigid_x, rigid_y, rigid_z]) - blocks
    grid5 = grid5.at[:, glob_y, glob_z, line_b].add(correction)
    return grid5.reshape(3, NY, NZ, NX)

def reference(force, multiplier, strain_aux, entry_lines, entry_owner, entry_slot):
    shifted = multiplier - penalty * strain_aux
    rhs_x = force[0] + deriv(shifted[0], 2) + deriv(shifted[3], 0) + deriv(shifted[4], 1)
    rhs_y = force[1] + deriv(shifted[3], 2) + deriv(shifted[1], 0) + deriv(shifted[5], 1)
    rhs_z = force[2] + deriv(shifted[4], 2) + deriv(shifted[5], 0) + deriv(shifted[2], 1)
    fluid = stokes(jnp.stack([rhs_x, rhs_y, rhs_z]))
    velocity = project(fluid, entry_lines, entry_owner, entry_slot)
    vel_x, vel_y, vel_z = (velocity[0], velocity[1], velocity[2])
    strain = jnp.stack([deriv(vel_x, 2), deriv(vel_y, 0), deriv(vel_z, 1), (deriv(vel_x, 0) + deriv(vel_y, 2)) / 2.0, (deriv(vel_x, 1) + deriv(vel_z, 2)) / 2.0, (deriv(vel_y, 1) + deriv(vel_z, 0)) / 2.0])
    q_field = multiplier + penalty * strain
    qnorm = jnp.sqrt(q_field[0] ** 2 + q_field[1] ** 2 + q_field[2] ** 2 + 2.0 * (q_field[3] ** 2 + q_field[4] ** 2 + q_field[5] ** 2))
    factor = 1.0 - yield_stress / jnp.maximum(qnorm, yield_stress)
    new_aux = factor[None] * q_field / penalty
    new_multiplier = multiplier + penalty * (strain - new_aux)
    return (velocity, new_aux, new_multiplier)
```

```python
import functools
import math

import jax
import jax.numpy as jnp
import numpy as np
from jax import lax
from jax.experimental import pallas as pl
from jax.experimental.pallas import tpu as pltpu
from jax.sharding import PartitionSpec as P

MASS, VISC, PEN, YIELD = 0.02, 10.0, 5.0, 2.0
NPD = 72
NX, NY, NZ = 512, 128, 256
ROWS, COLS = 8, 16
CHUNKS = 4
MC = 32 // CHUNKS
F32, BF16 = jnp.float32, jnp.bfloat16
MESH = pl.DeviceIdType.MESH
HIGHEST = lax.Precision.HIGHEST
NN = (((1,), (0,)), ((), ()))
NT = (((1,), (1,)), ((), ()))

YCOMP = (3, 1, 5)
ZCOMP = (4, 5, 2)
XCOMP = (0, 3, 4)


def pieces_np(table, count):
    out = []
    rest = np.asarray(table, np.float64)
    for _ in range(count):
        piece = rest.astype(jnp.bfloat16)
        out.append(piece)
        rest = rest - piece.astype(np.float64)
    return np.stack(out)


def kron_dft(points, batch, sign):
    index = np.arange(points)
    angle = sign * 2 * np.pi * (np.outer(index, index) % points) / points
    eye = np.eye(batch)
    cos, sin = np.kron(np.cos(angle), eye), np.kron(np.sin(angle), eye)
    return np.block([[cos, sin], [-sin, cos]])


def kron_dft_z(sign):
    index = np.arange(16)
    angle = sign * 2 * np.pi * (np.outer(index, index) % 16) / 16
    eye = np.eye(8)
    cos, sin = np.kron(eye, np.cos(angle)), np.kron(eye, np.sin(angle))
    return np.block([[cos, sin], [-sin, cos]])


def mode_table():
    chunk, dest, part, inner = np.meshgrid(
        np.arange(CHUNKS), np.arange(ROWS), np.arange(2), np.arange(MC), indexing="ij"
    )
    mode = 32 * dest + MC * chunk + inner
    return mode.reshape(CHUNKS, -1), part.reshape(CHUNKS, -1)


def make_tables():
    mode, part = mode_table()
    x = np.arange(NX)
    angle = 2 * np.pi * ((mode[..., None] * x) % NX) / NX
    fwd = np.where(part[..., None] == 0, np.cos(angle), -np.sin(angle))
    weight = np.where(mode == 0, 1.0, 2.0)[..., None] / float(NX * NY * NZ)
    inv = weight * fwd
    ky_f = pieces_np(kron_dft(16, 16, -1), 2)
    ky_i = pieces_np(kron_dft(16, 16, 1), INV)
    kz_f = pieces_np(kron_dft_z(-1), 2)
    kz_i = pieces_np(kron_dft_z(1), INV)
    lane = np.arange(256)
    turn_y = 2 * np.pi * np.outer(np.arange(8), lane // 16) / NY
    turn_z = 2 * np.pi * np.outer(np.arange(16), np.arange(128) % 16) / NZ
    two_y = np.stack([np.cos(turn_y), np.sin(turn_y)]).astype(np.float32)
    two_z = np.stack([np.cos(turn_z), np.sin(turn_z)]).astype(np.float32)
    return {
        "tf": pieces_np(fwd, 2),
        "ti": pieces_np(inv, INV),
        "kyf": ky_f,
        "kyi": ky_i,
        "kzf": kz_f,
        "kzi": kz_i,
        "twy": two_y,
        "twz": two_z,
        "dz": deriv_rows(16).astype(jnp.bfloat16),
        "bz": deriv_halo().astype(jnp.bfloat16),
    }


INV = 3


def deriv_rows(lines):
    one = np.zeros((16, 16))
    for offset, coef in ((1, 8), (-1, -8), (2, -1), (-2, 1)):
        one += coef * np.eye(16, k=offset)
    return np.kron(np.eye(lines), one)


def deriv_halo():
    out = np.zeros((16, 16, 4, 16))
    for y in range(16):
        for layer, place in enumerate((-2, -1, 16, 17)):
            for z in range(16):
                out[y, z, layer, y] = {1: 8, -1: -8, 2: -1, -2: 1}.get(place - z, 0)
    return out.reshape(256, 64)


def split(value, count):
    out = []
    for step in range(count):
        piece = value.astype(BF16)
        out.append(piece)
        if step + 1 < count:
            value = value - piece.astype(F32)
    return out


def dot(a, b, dims=NN):
    return lax.dot_general(a, b, dims, preferred_element_type=F32)


def dot_exact(a, b, dims=NN):
    return lax.dot_general(a, b, dims, precision=HIGHEST, preferred_element_type=F32)


def product(a, b, dims=NN):
    count = len(a)
    total = None
    for i in range(count - 1, -1, -1):
        for j in range(count - 1 - i, -1, -1):
            term = dot(a[i], b[j], dims)
            total = term if total is None else total + term
    return total


def exact_left(a, value, count):
    total = None
    for piece in reversed(split(value, count)):
        term = dot(a, piece)
        total = term if total is None else total + term
    return total


def fft(xs, sign):
    count = len(xs)
    if count == 1:
        return xs
    even, odd = fft(xs[0::2], sign), fft(xs[1::2], sign)
    out = [None] * count
    half = count // 2
    for k in range(half):
        re, im = odd[k]
        if k == 0:
            tr, ti = re, im
        elif 4 * k == count:
            tr, ti = (-im, re) if sign > 0 else (im, -re)
        else:
            c = math.cos(2 * math.pi * k / count)
            s = sign * math.sin(2 * math.pi * k / count)
            tr, ti = re * c - im * s, re * s + im * c
        er, ei = even[k]
        out[k] = (er + tr, ei + ti)
        out[k + half] = (er - tr, ei - ti)
    return out


def along_x(field):
    axis = field.ndim - 1
    up1, up2 = pltpu.roll(field, NX - 1, axis), pltpu.roll(field, NX - 2, axis)
    lo1, lo2 = pltpu.roll(field, 1, axis), pltpu.roll(field, 2, axis)
    return (8.0 * (up1 - lo1) - (up2 - lo2)) * (1.0 / 12.0)


def centered(lo2, lo1, up1, up2):
    return (8.0 * (up1 - lo1) - (up2 - lo2)) * (1.0 / 12.0)


def kernel(
    force, mult, aux, ent, tf, ti, kyf, kyi, kzf, kzi, twy, twz, dzt, bzt,
    vext, vzh,
    yext, zf, zh, rhs, rpieces, fluid,
    x1, r1, y1, r2, z1, r3, y2, r4, ascr, bscr,
    g1, g2, g3, g4, gtile, match, geo, mgeo, hot, hott,
    halo_send, halo_recv, a_send, a_recv, g_send, g_recv,
):
    row, col = lax.axis_index("row"), lax.axis_index("col")

    def row_peer(off):
        return lax.rem(row + off, ROWS)

    def col_peer(off):
        return lax.rem(col + off, COLS)

    def remote(src, dst, send, recv, device):
        return pltpu.make_async_remote_copy(
            src_ref=src, dst_ref=dst, send_sem=send, recv_sem=recv,
            device_id=device, device_id_type=MESH,
        )

    def wait_for(ref, sem):
        pltpu.make_async_copy(ref, ref, sem).wait()

    barrier = pltpu.get_barrier_semaphore()
    for off in range(1, ROWS):
        pl.semaphore_signal(barrier, inc=1, device_id=(row_peer(off), col), device_id_type=MESH)
    for off in range(1, COLS):
        pl.semaphore_signal(barrier, inc=1, device_id=(row, col_peer(off)), device_id_type=MESH)

    def shifted(comp):
        return mult[comp] - PEN * aux[comp]

    for i, comp in enumerate(YCOMP):
        yext[i, 2:18] = shifted(comp)
    for i, comp in enumerate(ZCOMP):
        for layer, z in enumerate((0, 1, 14, 15)):
            zf[i, layer] = mult[comp, :, z, :] - PEN * aux[comp, :, z, :]
    pl.semaphore_wait(barrier, ROWS + COLS - 2)

    def halo_copies(base, ybuf, zsrc, zdst):
        up, down = (row_peer(1), col), (row_peer(ROWS - 1), col)
        right, left = (row, col_peer(1)), (row, col_peer(COLS - 1))
        sems = [(halo_send.at[base + k], halo_recv.at[base + k]) for k in range(4)]
        return [
            remote(zsrc.at[:, 2:4], zdst.at[:, 0:2], *sems[0], right),
            remote(zsrc.at[:, 0:2], zdst.at[:, 2:4], *sems[1], left),
            remote(ybuf.at[:, 16:18], ybuf.at[:, 0:2], *sems[2], up),
            remote(ybuf.at[:, 2:4], ybuf.at[:, 18:20], *sems[3], down),
        ]

    stress_halos = halo_copies(0, yext, zf, zh)
    for copy in stress_halos:
        copy.start()

    lane128 = lax.broadcasted_iota(jnp.int32, (1, 128), 1)
    entry = ent[...]
    line_of = lax.broadcasted_iota(jnp.int32, (8, 128), 0)
    gy = entry[2:3] + (row * 16).astype(F32)
    gz = entry[3:4] + (col * 16).astype(F32)
    fields = jnp.concatenate([entry[0:2], gy, gz, gy * gy, gz * gz, entry[4:6]], axis=0)
    pair = lax.broadcasted_iota(jnp.int32, (128, 128), 0)
    runs_lane = lax.broadcasted_iota(jnp.int32, (128, 128), 1)
    gather_runs = (pair // 4 == runs_lane).astype(F32)
    spread_runs = (runs_lane // 4 == pair).astype(F32)
    sums = dot_exact(fields, gather_runs)
    mean_y, mean_z = sums[2:3] * 0.25, sums[3:4] * 0.25
    inner = 4.0 * 174752.0 + 128.0 * (
        sums[4:5] - 4.0 * mean_y * mean_y + sums[5:6] - 4.0 * mean_z * mean_z
    )
    gtile[0] = jnp.concatenate(
        [sums[0:1] * 0.25, sums[1:2] * 0.25 + 63.5, mean_y, mean_z, inner, jnp.zeros((3, 128), F32)], axis=0
    )

    def gather_cols(slot, buf):
        buf[col] = gtile[slot]
        for off in range(1, COLS):
            remote(
                gtile.at[slot], buf.at[col], g_send.at[2 * slot], g_recv.at[2 * slot], (row, col_peer(off))
            ).start()

    def gather_rows(slot, buf, wide):
        wait_for(buf.at[pl.ds(0, COLS - 1)], g_recv.at[2 * slot])
        parts = []
        for q in range(4):
            total = None
            for k in range(4):
                tile = jnp.where(runs_lane[0:8] < 32, buf[4 * q + k], 0.0)
                tile = pltpu.roll(tile, 32 * k, 1) if k else tile
                total = tile if total is None else total + tile
            parts.append(total)
        wide[row] = jnp.concatenate(parts, axis=1)
        for off in range(1, ROWS):
            remote(
                wide.at[row], wide.at[row], g_send.at[2 * slot + 1], g_recv.at[2 * slot + 1], (row_peer(off), col)
            ).start()

    gather_cols(0, g1)

    for c, comp in enumerate(XCOMP):
        rhs[c] = (force[c] + along_x(shifted(comp))).reshape(256, NX)
    fluid[...] = jnp.zeros_like(fluid)
    for c, comp in enumerate(ZCOMP):
        own = shifted(comp).reshape(256, NX)
        rhs[c] += exact_left(dzt[...], own, 2) * (1.0 / 12.0)
    gather_rows(0, g1, g2)
    for copy in stress_halos:
        copy.wait_recv()
    for c in range(3):
        along_y = centered(yext[c, 0:16], yext[c, 1:17], yext[c, 3:19], yext[c, 4:20]).reshape(256, NX)
        edge = exact_left(bzt[...], zh[c].reshape(64, NX), 2) * (1.0 / 12.0)
        high, low = split(rhs[c] + along_y + edge, 2)
        rpieces[0, c] = high
        rpieces[1, c] = low

    def send_rows(stage, j, src, dst):
        dst[j, row] = src[j, row]
        for off in range(1, ROWS):
            peer = row_peer(off)
            remote(src.at[j, peer], dst.at[j, row], a_send.at[stage, j], a_recv.at[stage, j], (peer, col)).start()

    def send_cols(stage, j, src, dst):
        dst[j, col] = src[j, col]
        for off in range(1, COLS):
            peer = col_peer(off)
            remote(src.at[j, peer], dst.at[j, col], a_send.at[stage, j], a_recv.at[stage, j], (row, peer)).start()

    def await_all(stage, j, dst, count):
        wait_for(dst.at[j, pl.ds(0, count - 1)], a_recv.at[stage, j])

    def x_forward(j):
        for c in range(3):
            out = product([tf[0, j], tf[1, j]], [rpieces[0, c], rpieces[1, c]], NT)
            x1[j, :, c] = out.reshape(ROWS, 2 * MC, 256)
        send_rows(0, j, x1, r1)

    def y_forward(j):
        await_all(0, j, r1, ROWS)
        for c in range(3):
            xs = [(r1[j, s, c, 0:MC], r1[j, s, c, MC : 2 * MC]) for s in range(8)]
            for k, (re, im) in enumerate(fft(xs, -1)):
                cos, sin = twy[0, k : k + 1], twy[1, k : k + 1]
                at = k * 3 * MC + c * MC
                ascr[at : at + MC, 0:256] = re * cos + im * sin
                ascr[at : at + MC, 256:512] = im * cos - re * sin
        out = product(split(ascr[...], 2), [kyf[0], kyf[1]]).reshape(8, 3, MC, 512)
        for half in range(2):
            for part in range(2):
                at = 256 * part + 128 * half
                y1[j, pl.ds(half, 8, 2), :, part] = out[:, :, :, at : at + 128]
        send_cols(1, j, y1, r2)

    def solve(j):
        await_all(1, j, r2, COLS)
        for c in range(3):
            xs = [(r2[j, s, c, 0], r2[j, s, c, 1]) for s in range(16)]
            for k, (re, im) in enumerate(fft(xs, -1)):
                cos, sin = twz[0, k : k + 1], twz[1, k : k + 1]
                at = k * 3 * MC + c * MC
                bscr[at : at + MC, 0:128] = re * cos + im * sin
                bscr[at : at + MC, 128:256] = im * cos - re * sin
        bscr[...] = product(split(bscr[...], 2), [kzf[0], kzf[1]])
        mode = row * 32 + j * MC + lax.broadcasted_iota(jnp.int32, (MC, 128), 0)
        lanes = lax.broadcasted_iota(jnp.int32, (MC, 128), 1)
        wave_x = mode.astype(F32) * (2.0 * math.pi / NX)
        index_y = col // 2 + 8 * (8 * lax.rem(col, 2) + lanes // 16)
        wave_y = jnp.where(index_y < NY // 2, index_y, index_y - NY).astype(F32) * (2.0 * math.pi / NY)
        keep_y = (index_y != NY // 2).astype(F32)
        for k in range(16):
            index_z = k + 16 * (lanes % 16)
            wave_z = jnp.where(index_z < NZ // 2, index_z, index_z - NZ).astype(F32) * (2.0 * math.pi / NZ)
            keep = keep_y * (index_z != NZ // 2).astype(F32)
            ksq = wave_x * wave_x + wave_y * wave_y + wave_z * wave_z
            inverse = 1.0 / jnp.where(ksq > 0, ksq, 1.0)
            gain = keep / (MASS + VISC * ksq)
            for part in range(2):
                at = 3 * MC * k
                lane = slice(128 * part, 128 * part + 128)
                fx, fy, fz = (bscr[at + MC * c : at + MC * c + MC, lane] for c in range(3))
                dotk = (wave_x * fx + wave_y * fy + wave_z * fz) * inverse
                bscr[at : at + MC, lane] = (fx - wave_x * dotk) * gain
                bscr[at + MC : at + 2 * MC, lane] = (fy - wave_y * dotk) * gain
                bscr[at + 2 * MC : at + 3 * MC, lane] = (fz - wave_z * dotk) * gain
        bscr[...] = product(split(bscr[...], INV), [kzi[p] for p in range(INV)])
        for c in range(3):
            xs = []
            for k in range(16):
                cos, sin = twz[0, k : k + 1], twz[1, k : k + 1]
                at = k * 3 * MC + c * MC
                re, im = bscr[at : at + MC, 0:128], bscr[at : at + MC, 128:256]
                xs.append((re * cos - im * sin, im * cos + re * sin))
            for s, (re, im) in enumerate(fft(xs, 1)):
                z1[j, s, c, 0] = re
                z1[j, s, c, 1] = im
        send_cols(2, j, z1, r3)

    def y_inverse(j):
        await_all(2, j, r3, COLS)
        for half in range(2):
            for part in range(2):
                at = 256 * part + 128 * half
                ascr[:, at : at + 128] = r3[j, pl.ds(half, 8, 2), :, part].reshape(8 * 3 * MC, 128)
        ascr[...] = product(split(ascr[...], INV), [kyi[p] for p in range(INV)])
        for c in range(3):
            xs = []
            for k in range(8):
                cos, sin = twy[0, k : k + 1], twy[1, k : k + 1]
                at = k * 3 * MC + c * MC
                re, im = ascr[at : at + MC, 0:256], ascr[at : at + MC, 256:512]
                xs.append((re * cos - im * sin, im * cos + re * sin))
            for s, (re, im) in enumerate(fft(xs, 1)):
                y2[j, s, c, 0:MC] = re
                y2[j, s, c, MC : 2 * MC] = im
        send_rows(3, j, y2, r4)

    def x_inverse(j):
        await_all(3, j, r4, ROWS)
        for c in range(3):
            spectrum = jnp.transpose(r4[j, :, c].reshape(2 * MC * ROWS, 256))
            fluid[c] += product(split(spectrum, INV), [ti[p, j] for p in range(INV)])

    def geometry():
        wait_for(g2.at[pl.ds(0, ROWS - 1)], g_recv.at[1])
        own = dot_exact(spread_runs[0:32], fields, NT) * 0.25
        ids = own[:, 0:1]
        count = jnp.zeros((32, 1), F32)
        cx, cy, cz = count, count, count
        for r in range(ROWS):
            block = g2[r]
            same = (ids == block[0:1]).astype(F32)
            match[r] = same
            count += jnp.sum(same, axis=1, keepdims=True)
            cx += jnp.sum(same * block[1:2], axis=1, keepdims=True)
            cy += jnp.sum(same * block[2:3], axis=1, keepdims=True)
            cz += jnp.sum(same * block[3:4], axis=1, keepdims=True)
        safe = jnp.maximum(count, 1.0)
        cx, cy, cz = cx / safe, cy / safe, cz / safe
        spread = jnp.zeros((32, 1), F32)
        for r in range(ROWS):
            block = g2[r]
            dx, dy, dz = block[1:2] - cx, block[2:3] - cy, block[3:4] - cz
            inner_spread = block[4:5] + 512.0 * (dx * dx + dy * dy + dz * dz)
            spread += jnp.sum(match[r] * inner_spread, axis=1, keepdims=True)
        inertia = jnp.maximum(spread * (2.0 / 3.0), 1.0)
        place = lane128
        packed = jnp.where(place == 0, 1.0 / jnp.maximum(512.0 * count, 1.0), 0.0)
        for at, value in ((1, cx), (2, cy), (3, cz), (4, 1.0 / inertia)):
            packed = jnp.where(place == at, value, packed)
        geo[...] = packed
        mine = dot_exact((pair == runs_lane).astype(F32), fields, NT)
        centers = dot_exact(gather_runs[:, 0:32], packed)
        rel = jnp.where(place == 0, mine[:, 1:2] + 63.5 - centers[:, 1:2], 0.0)
        rel = jnp.where(place == 1, mine[:, 2:3] - centers[:, 2:3], rel)
        mgeo[...] = jnp.where(place == 2, mine[:, 3:4] - centers[:, 3:4], rel)
        rows256 = lax.broadcasted_iota(jnp.int32, (256, 128), 0).astype(F32)
        cols256 = lax.broadcasted_iota(jnp.int32, (128, 256), 1).astype(F32)
        for b in range(4):
            hot[b] = ((fields[6:7] == rows256) & (fields[7:8] == float(b))).astype(F32).astype(BF16)
            hott[b] = ((mine[:, 6:7] == cols256) & (mine[:, 7:8] == float(b))).astype(F32).astype(BF16)

    x_forward(0)
    geometry()

    @pl.loop(0, CHUNKS + 3)
    def _(t):
        pl.when(t + 1 < CHUNKS)(lambda: x_forward(t + 1))
        pl.when(t < CHUNKS)(lambda: y_forward(t))
        pl.when((t >= 1) & (t < CHUNKS + 1))(lambda: solve(t - 1))
        pl.when((t >= 2) & (t < CHUNKS + 2))(lambda: y_inverse(t - 2))
        pl.when(t >= 3)(lambda: x_inverse(t - 3))

    inside = lane128.astype(F32) - 63.5
    blocks = []
    firsts, seconds = [], []
    for c in range(3):
        block = jnp.zeros((128, 128), F32)
        for b in range(4):
            block += exact_left(hott[b], fluid[c, :, 128 * b : 128 * b + 128], 3)
        blocks.append(block)
        firsts.append(jnp.sum(block, axis=1, keepdims=True))
        seconds.append(jnp.sum(block * inside, axis=1, keepdims=True))
    rx, ry, rz = mgeo[:, 0:1], mgeo[:, 1:2], mgeo[:, 2:3]
    moments = jnp.zeros((128, 128), F32)
    for at, value in enumerate(
        (
            firsts[0],
            firsts[1],
            firsts[2],
            ry * firsts[2] - rz * firsts[1],
            rz * firsts[0] - (rx * firsts[2] + seconds[2]),
            rx * firsts[1] + seconds[1] - ry * firsts[0],
        )
    ):
        moments = jnp.where(lane128 == at, value, moments)
    gtile[1] = dot_exact(jnp.transpose(moments)[0:8], gather_runs)
    gather_cols(1, g3)
    gather_rows(1, g3, g4)
    wait_for(g4.at[pl.ds(0, ROWS - 1)], g_recv.at[3])
    totals = jnp.zeros((32, 8), F32)
    for r in range(ROWS):
        totals += dot_exact(match[r], g4[r], NT)
    packed = geo[...]
    params = jnp.zeros((32, 128), F32)
    for at in range(6):
        scale = packed[:, 0:1] if at < 3 else packed[:, 4:5]
        params = jnp.where(lane128 == at, totals[:, at : at + 1] * scale, params)
    fitted = dot_exact(gather_runs[:, 0:32], params)
    vx, vy, vz, wx, wy, wz = (fitted[:, k : k + 1] for k in range(6))
    cell_x = rx + inside
    rigid = (
        vx + wy * rz - wz * ry,
        vy + wz * cell_x - wx * rz,
        vz + wx * ry - wy * cell_x,
    )
    for c in range(3):
        fix = rigid[c] - blocks[c]
        for b in range(4):
            lanes = slice(128 * b, 128 * b + 128)
            done = fluid[c, :, lanes] + exact_left(hot[b], fix, 3)
            vext[c, 2:18, :, lanes] = done.reshape(16, 16, 128)
    for copy in stress_halos:
        copy.wait_send()
    for c in range(3):
        for layer, z in enumerate((0, 1, 14, 15)):
            zf[c, layer] = vext[c, 2:18, z, :]
    velocity_halos = halo_copies(4, vext, zf, vzh)
    for k, copy in enumerate(velocity_halos):
        copy.start()
    for copy in velocity_halos:
        copy.wait_recv()

    for copy in velocity_halos:
        copy.wait_send()
    wait_for(g1.at[pl.ds(0, COLS - 1)], g_send.at[0])
    wait_for(g2.at[pl.ds(0, ROWS - 1)], g_send.at[1])
    wait_for(g3.at[pl.ds(0, COLS - 1)], g_send.at[2])
    wait_for(g4.at[pl.ds(0, ROWS - 1)], g_send.at[3])

    @pl.loop(0, CHUNKS)
    def _(j):
        wait_for(x1.at[j, pl.ds(0, ROWS - 1)], a_send.at[0, j])
        wait_for(y1.at[j, pl.ds(0, COLS - 1)], a_send.at[1, j])
        wait_for(z1.at[j, pl.ds(0, COLS - 1)], a_send.at[2, j])
        wait_for(y2.at[j, pl.ds(0, ROWS - 1)], a_send.at[3, j])


def update(vext, vzh, mult, dzt, bzt, vel, new_aux, new_mult, *, lines):
    base = pl.program_id(0) * lines
    rows = 16 * lines
    edge = bzt[...]
    grads = []
    for c in range(3):
        field = vext[c, pl.ds(base + 2, lines)]
        vel[c] = field
        dx = along_x(field.reshape(rows, NX))
        near = [vext[c, pl.ds(base + k, lines)].reshape(rows, NX) for k in (0, 1, 3, 4)]
        dy = centered(*near)
        dz = exact_left(dzt[...], field.reshape(rows, NX), 3) + exact_left(edge, vzh[c], 3)
        grads.append((dx, dy, dz * (1.0 / 12.0)))
    strain = (
        grads[0][0],
        grads[1][1],
        grads[2][2],
        (grads[0][1] + grads[1][0]) * 0.5,
        (grads[0][2] + grads[2][0]) * 0.5,
        (grads[1][2] + grads[2][1]) * 0.5,
    )
    old = [mult[k].reshape(rows, NX) for k in range(6)]
    q = [old[k] + PEN * strain[k] for k in range(6)]
    norm = jnp.sqrt(
        q[0] * q[0] + q[1] * q[1] + q[2] * q[2] + 2.0 * (q[3] * q[3] + q[4] * q[4] + q[5] * q[5])
    )
    factor = 1.0 - YIELD / jnp.maximum(norm, YIELD)
    for k in range(6):
        aux = factor * q[k] * (1.0 / PEN)
        new_aux[k] = aux.reshape(lines, 16, NX)
        new_mult[k] = (old[k] + PEN * (strain[k] - aux)).reshape(lines, 16, NX)


def local(force, mult, aux, entry_lines, entry_owner, entry_slot):
    t = make_tables()
    particle = entry_owner[:, 0] * NPD + entry_slot
    ent = jnp.stack(
        [
            particle,
            (entry_lines % 4) * 128,
            entry_lines // 64,
            entry_lines // 4 % 16,
            entry_lines // 4,
            entry_lines % 4,
            jnp.zeros_like(entry_lines),
            jnp.zeros_like(entry_lines),
        ]
    ).astype(F32)
    vm = pl.BlockSpec(memory_space=pltpu.VMEM)
    sems = pltpu.SemaphoreType.DMA
    names = ("tf", "ti", "kyf", "kyi", "kzf", "kzi", "twy", "twz", "dz", "bz")
    scratch = [
        pltpu.VMEM((3, 20, 16, NX), F32),
        pltpu.VMEM((3, 4, 16, NX), F32),
        pltpu.VMEM((3, 4, 16, NX), F32),
        pltpu.VMEM((3, 256, NX), F32),
        pltpu.VMEM((2, 3, 256, NX), BF16),
        pltpu.VMEM((3, 256, NX), F32),
        pltpu.VMEM((CHUNKS, ROWS, 3, 2 * MC, 256), F32),
        pltpu.VMEM((CHUNKS, ROWS, 3, 2 * MC, 256), F32),
        pltpu.VMEM((CHUNKS, COLS, 3, 2, MC, 128), F32),
        pltpu.VMEM((CHUNKS, COLS, 3, 2, MC, 128), F32),
        pltpu.VMEM((CHUNKS, COLS, 3, 2, MC, 128), F32),
        pltpu.VMEM((CHUNKS, COLS, 3, 2, MC, 128), F32),
        pltpu.VMEM((CHUNKS, ROWS, 3, 2 * MC, 256), F32),
        pltpu.VMEM((CHUNKS, ROWS, 3, 2 * MC, 256), F32),
        pltpu.VMEM((24 * MC, 512), F32),
        pltpu.VMEM((48 * MC, 256), F32),
        pltpu.VMEM((COLS, 8, 128), F32),
        pltpu.VMEM((ROWS, 8, 512), F32),
        pltpu.VMEM((COLS, 8, 128), F32),
        pltpu.VMEM((ROWS, 8, 512), F32),
        pltpu.VMEM((2, 8, 128), F32),
        pltpu.VMEM((ROWS, 32, 512), F32),
        pltpu.VMEM((32, 128), F32),
        pltpu.VMEM((128, 128), F32),
        pltpu.VMEM((4, 256, 128), BF16),
        pltpu.VMEM((4, 128, 256), BF16),
        sems((8,)),
        sems((8,)),
        sems((4, CHUNKS)),
        sems((4, CHUNKS)),
        sems((4,)),
        sems((4,)),
    ]
    vext, vzh = pl.pallas_call(
        kernel,
        out_shape=(
            jax.ShapeDtypeStruct((3, 20, 16, NX), F32),
            jax.ShapeDtypeStruct((3, 4, 16, NX), F32),
        ),
        in_specs=[vm] * (4 + len(names)),
        out_specs=(vm, vm),
        scratch_shapes=scratch,
        compiler_params=pltpu.CompilerParams(
            collective_id=0, has_side_effects=True, vmem_limit_bytes=60 * 2**20
        ),
    )(force, mult, aux, ent, *(jnp.asarray(t[k]) for k in names))

    lines = 4
    whole = lambda *shape: pl.BlockSpec(shape, lambda i: (0,) * len(shape))
    part = lambda n: pl.BlockSpec((n, lines, 16, NX), lambda i: (0, i, 0, 0))
    return tuple(
        pl.pallas_call(
            functools.partial(update, lines=lines),
            grid=(16 // lines,),
            out_shape=tuple(jax.ShapeDtypeStruct((n, 16, 16, NX), F32) for n in (3, 6, 6)),
            in_specs=[
                whole(3, 20, 16, NX),
                whole(3, 64, NX),
                part(6),
                whole(16 * lines, 16 * lines),
                pl.BlockSpec((16 * lines, 64), lambda i: (i, 0)),
            ],
            out_specs=tuple(part(n) for n in (3, 6, 6)),
            compiler_params=pltpu.CompilerParams(vmem_limit_bytes=48 * 2**20),
        )(
            vext,
            vzh.reshape(3, 64, NX),
            mult,
            jnp.asarray(deriv_rows(lines).astype(jnp.bfloat16)),
            jnp.asarray(t["bz"]),
        )
    )


def solution(mesh):
    field = P(None, "row", "col", None)
    return jax.shard_map(
        local,
        mesh=mesh,
        in_specs=(field, field, field, P(("row", "col")), P(("row", "col"), None), P(("row", "col"))),
        out_specs=(field, field, field),
        check_vma=False,
    )
```

```python
import functools
import math

import jax
import jax.numpy as jnp
import numpy as np
from jax import lax
from jax.experimental import pallas as pl
from jax.experimental.pallas import tpu as pltpu
from jax.sharding import PartitionSpec as P

MASS, VISC, PEN, YIELD = 0.02, 10.0, 5.0, 2.0
NPD = 72
NX, NY, NZ = 512, 128, 256
ROWS, COLS = 8, 16
CHUNKS = 4
MC = 32 // CHUNKS
F32, BF16 = jnp.float32, jnp.bfloat16
MESH = pl.DeviceIdType.MESH
HIGHEST = lax.Precision.HIGHEST
NN = (((1,), (0,)), ((), ()))
NT = (((1,), (1,)), ((), ()))

FAR = (
    (2, 2), (2, 1), (1, 2), (2, 3), (3, 2), (1, 1), (3, 3), (1, 3), (3, 1),
    (2, 0), (0, 2), (1, 0), (0, 1), (3, 0), (0, 3),
)

YCOMP = (3, 1, 5)
ZCOMP = (4, 5, 2)
XCOMP = (0, 3, 4)


def pieces_np(table, count):
    out = []
    rest = np.asarray(table, np.float64)
    for _ in range(count):
        piece = rest.astype(jnp.bfloat16)
        out.append(piece)
        rest = rest - piece.astype(np.float64)
    return np.stack(out)


def kron_dft(points, batch, sign):
    index = np.arange(points)
    angle = sign * 2 * np.pi * (np.outer(index, index) % points) / points
    eye = np.eye(batch)
    cos, sin = np.kron(np.cos(angle), eye), np.kron(np.sin(angle), eye)
    return np.block([[cos, sin], [-sin, cos]])


def kron_dft_z(sign):
    index = np.arange(16)
    angle = sign * 2 * np.pi * (np.outer(index, index) % 16) / 16
    eye = np.eye(8)
    cos, sin = np.kron(eye, np.cos(angle)), np.kron(eye, np.sin(angle))
    return np.block([[cos, sin], [-sin, cos]])


def mode_table():
    chunk, dest, part, inner = np.meshgrid(
        np.arange(CHUNKS), np.arange(ROWS), np.arange(2), np.arange(MC), indexing="ij"
    )
    mode = 32 * dest + MC * chunk + inner
    return mode.reshape(CHUNKS, -1), part.reshape(CHUNKS, -1)


def make_tables():
    mode, part = mode_table()
    x = np.arange(NX)
    angle = 2 * np.pi * ((mode[..., None] * x) % NX) / NX
    fwd = np.where(part[..., None] == 0, np.cos(angle), -np.sin(angle))
    weight = np.where(mode == 0, 1.0, 2.0)[..., None] / float(NX * NY * NZ)
    inv = weight * fwd
    ky_f = pieces_np(kron_dft(16, 16, -1), 2)
    ky_i = pieces_np(kron_dft(16, 16, 1), INV)
    kz_f = pieces_np(kron_dft_z(-1), 2)
    kz_i = pieces_np(kron_dft_z(1), INV)
    lane = np.arange(256)
    turn_y = 2 * np.pi * np.outer(np.arange(8), lane // 16) / NY
    turn_z = 2 * np.pi * np.outer(np.arange(16), np.arange(128) % 16) / NZ
    two_y = np.stack([np.cos(turn_y), np.sin(turn_y)]).astype(np.float32)
    two_z = np.stack([np.cos(turn_z), np.sin(turn_z)]).astype(np.float32)
    return {
        "tf": pieces_np(fwd, 2),
        "ti": pieces_np(inv, INV),
        "kyf": ky_f,
        "kyi": ky_i,
        "kzf": kz_f,
        "kzi": kz_i,
        "twy": two_y,
        "twz": two_z,
        "dz": deriv_rows(16).astype(jnp.bfloat16),
        "bz": deriv_halo().astype(jnp.bfloat16),
    }


INV = 3


def deriv_rows(lines):
    one = np.zeros((16, 16))
    for offset, coef in ((1, 8), (-1, -8), (2, -1), (-2, 1)):
        one += coef * np.eye(16, k=offset)
    return np.kron(np.eye(lines), one)


def deriv_halo():
    out = np.zeros((16, 16, 4, 16))
    for y in range(16):
        for layer, place in enumerate((-2, -1, 16, 17)):
            for z in range(16):
                out[y, z, layer, y] = {1: 8, -1: -8, 2: -1, -2: 1}.get(place - z, 0)
    return out.reshape(256, 64)


def split(value, count):
    out = []
    for step in range(count):
        piece = value.astype(BF16)
        out.append(piece)
        if step + 1 < count:
            value = value - piece.astype(F32)
    return out


def dot(a, b, dims=NN):
    return lax.dot_general(a, b, dims, preferred_element_type=F32)


def dot_exact(a, b, dims=NN):
    return lax.dot_general(a, b, dims, precision=HIGHEST, preferred_element_type=F32)


def product(a, b, dims=NN):
    count = len(a)
    total = None
    for i in range(count - 1, -1, -1):
        for j in range(count - 1 - i, -1, -1):
            term = dot(a[i], b[j], dims)
            total = term if total is None else total + term
    return total


def exact_left(a, value, count):
    total = None
    for piece in reversed(split(value, count)):
        term = dot(a, piece)
        total = term if total is None else total + term
    return total


def fft(xs, sign):
    count = len(xs)
    if count == 1:
        return xs
    even, odd = fft(xs[0::2], sign), fft(xs[1::2], sign)
    out = [None] * count
    half = count // 2
    for k in range(half):
        re, im = odd[k]
        if k == 0:
            tr, ti = re, im
        elif 4 * k == count:
            tr, ti = (-im, re) if sign > 0 else (im, -re)
        else:
            c = math.cos(2 * math.pi * k / count)
            s = sign * math.sin(2 * math.pi * k / count)
            tr, ti = re * c - im * s, re * s + im * c
        er, ei = even[k]
        out[k] = (er + tr, ei + ti)
        out[k + half] = (er - tr, ei - ti)
    return out


def along_x(field):
    axis = field.ndim - 1
    up1, up2 = pltpu.roll(field, NX - 1, axis), pltpu.roll(field, NX - 2, axis)
    lo1, lo2 = pltpu.roll(field, 1, axis), pltpu.roll(field, 2, axis)
    return (8.0 * (up1 - lo1) - (up2 - lo2)) * (1.0 / 12.0)


def centered(lo2, lo1, up1, up2):
    return (8.0 * (up1 - lo1) - (up2 - lo2)) * (1.0 / 12.0)


def kernel(
    force_in, mult_in, aux_in, lines_in, owner_in, slot_in,
    tf_in, ti_in, kyf_in, kyi_in, kzf_in, kzi_in, twy_in, twz_in, dzt_in, bzt_in,
    vext, vzh,
    force, mult, aux, tf, ti, kyf, kyi, kzf, kzi, twy, twz, dzt, bzt,
    yext, zf, zh, rhs, rpieces, fluid,
    x1, r1, y1, r2, z1, r3, y2, r4, ascr, bscr,
    g1, g2, g3, g4, gtile, match, geo, mgeo, hot, hott,
    halo_send, halo_recv, a_send, a_recv, g_send, g_recv, load_sem,
):
    row, col = lax.axis_index("row"), lax.axis_index("col")

    def row_peer(off):
        return lax.rem(row + off, ROWS)

    def col_peer(off):
        return lax.rem(col + off, COLS)

    def remote(src, dst, send, recv, device):
        return pltpu.make_async_remote_copy(
            src_ref=src, dst_ref=dst, send_sem=send, recv_sem=recv,
            device_id=device, device_id_type=MESH,
        )

    def wait_for(ref, sem):
        pltpu.make_async_copy(ref, ref, sem).wait()

    loads = {}

    def load(name, src, dst):
        loads[name] = pltpu.make_async_copy(src, dst, load_sem.at[len(loads)])
        loads[name].start()

    for comp in (3, 1, 5, 4, 2):
        load(("mult", comp), mult_in.at[comp], mult.at[comp])
        load(("aux", comp), aux_in.at[comp], aux.at[comp])
    load("dzt", dzt_in, dzt)
    load("bzt", bzt_in, bzt)
    load(("mult", 0), mult_in.at[0], mult.at[0])
    load(("aux", 0), aux_in.at[0], aux.at[0])
    load("force", force_in, force)
    for name, src, dst in (
        ("tf", tf_in, tf), ("twy", twy_in, twy), ("kyf", kyf_in, kyf), ("twz", twz_in, twz),
        ("kzf", kzf_in, kzf), ("kzi", kzi_in, kzi), ("kyi", kyi_in, kyi), ("ti", ti_in, ti),
    ):
        load(name, src, dst)

    def loaded(*names):
        for name in names:
            loads.pop(name).wait()

    barrier = pltpu.get_barrier_semaphore()
    for off in range(1, ROWS):
        pl.semaphore_signal(barrier, inc=1, device_id=(row_peer(off), col), device_id_type=MESH)
    for off in range(1, COLS):
        pl.semaphore_signal(barrier, inc=1, device_id=(row, col_peer(off)), device_id_type=MESH)

    def shifted(comp):
        return mult[comp] - PEN * aux[comp]

    for i, comp in enumerate(YCOMP):
        loaded(("mult", comp), ("aux", comp))
        yext[i, 2:18] = shifted(comp)
    loaded(("mult", 4), ("aux", 4), ("mult", 2), ("aux", 2))
    for i, comp in enumerate(ZCOMP):
        for layer, z in enumerate((0, 1, 14, 15)):
            zf[i, layer] = mult[comp, :, z, :] - PEN * aux[comp, :, z, :]
    pl.semaphore_wait(barrier, ROWS + COLS - 2)

    def halo_copies(base, ybuf, zsrc, zdst):
        up, down = (row_peer(1), col), (row_peer(ROWS - 1), col)
        right, left = (row, col_peer(1)), (row, col_peer(COLS - 1))
        sems = [(halo_send.at[base + k], halo_recv.at[base + k]) for k in range(4)]
        return [
            remote(zsrc.at[:, 2:4], zdst.at[:, 0:2], *sems[0], right),
            remote(zsrc.at[:, 0:2], zdst.at[:, 2:4], *sems[1], left),
            remote(ybuf.at[:, 16:18], ybuf.at[:, 0:2], *sems[2], up),
            remote(ybuf.at[:, 2:4], ybuf.at[:, 18:20], *sems[3], down),
        ]

    stress_halos = halo_copies(0, yext, zf, zh)
    for copy in stress_halos:
        copy.start()

    lane128 = lax.broadcasted_iota(jnp.int32, (1, 128), 1)
    lines, block_x = lines_in[...], lines_in[...] & 3
    particle = owner_in[...] * NPD + slot_in[...]
    gy = ((lines >> 6) + row * 16).astype(F32)
    gz = (((lines >> 2) & 15) + col * 16).astype(F32)
    fields = jnp.concatenate(
        [
            particle.astype(F32),
            (block_x * 128).astype(F32),
            gy,
            gz,
            gy * gy,
            gz * gz,
            (lines >> 2).astype(F32),
            block_x.astype(F32),
        ],
        axis=0,
    )
    pair = lax.broadcasted_iota(jnp.int32, (128, 128), 0)
    runs_lane = lax.broadcasted_iota(jnp.int32, (128, 128), 1)
    gather_runs = (pair // 4 == runs_lane).astype(F32)
    spread_runs = (runs_lane // 4 == pair).astype(F32)
    sums = dot_exact(fields, gather_runs)
    mean_y, mean_z = sums[2:3] * 0.25, sums[3:4] * 0.25
    inner = 4.0 * 174752.0 + 128.0 * (
        sums[4:5] - 4.0 * mean_y * mean_y + sums[5:6] - 4.0 * mean_z * mean_z
    )
    gtile[0] = jnp.concatenate(
        [sums[0:1] * 0.25, sums[1:2] * 0.25 + 63.5, mean_y, mean_z, inner, jnp.zeros((3, 128), F32)], axis=0
    )

    def gather_cols(slot, buf):
        buf[col] = gtile[slot]
        for off in range(1, COLS):
            remote(
                gtile.at[slot], buf.at[col], g_send.at[2 * slot], g_recv.at[2 * slot], (row, col_peer(off))
            ).start()

    def gather_rows(slot, buf, wide):
        wait_for(buf.at[pl.ds(0, COLS - 1)], g_recv.at[2 * slot])
        parts = []
        for q in range(4):
            total = None
            for k in range(4):
                tile = jnp.where(runs_lane[0:8] < 32, buf[4 * q + k], 0.0)
                tile = pltpu.roll(tile, 32 * k, 1) if k else tile
                total = tile if total is None else total + tile
            parts.append(total)
        wide[row] = jnp.concatenate(parts, axis=1)
        for off in range(1, ROWS):
            remote(
                wide.at[row], wide.at[row], g_send.at[2 * slot + 1], g_recv.at[2 * slot + 1], (row_peer(off), col)
            ).start()

    gather_cols(0, g1)

    loaded("dzt", "bzt", ("mult", 0), ("aux", 0), "force")
    for c, comp in enumerate(XCOMP):
        rhs[c] = (force[c] + along_x(shifted(comp))).reshape(256, NX)
    fluid[...] = jnp.zeros_like(fluid)
    for c, comp in enumerate(ZCOMP):
        own = shifted(comp).reshape(256, NX)
        rhs[c] += exact_left(dzt[...], own, 2) * (1.0 / 12.0)
    gather_rows(0, g1, g2)
    for copy in stress_halos:
        copy.wait_recv()
    for c in range(3):
        along_y = centered(yext[c, 0:16], yext[c, 1:17], yext[c, 3:19], yext[c, 4:20]).reshape(256, NX)
        edge = exact_left(bzt[...], zh[c].reshape(64, NX), 2) * (1.0 / 12.0)
        high, low = split(rhs[c] + along_y + edge, 2)
        rpieces[0, c] = high
        rpieces[1, c] = low

    def send_rows(stage, j, src, dst):
        dst[j, row] = src[j, row]
        for off in range(1, ROWS):
            peer = row_peer(off)
            remote(src.at[j, peer], dst.at[j, row], a_send.at[stage, j], a_recv.at[stage, j], (peer, col)).start()

    def send_cols(stage, j, src, dst):
        dst[j, col] = src[j, col]
        for dy, dz in FAR:
            peer = 4 * lax.rem(col // 4 + dz, 4) + lax.rem(col % 4 + dy, 4)
            remote(src.at[j, peer], dst.at[j, col], a_send.at[stage, j], a_recv.at[stage, j], (row, peer)).start()

    def await_all(stage, j, dst, count):
        wait_for(dst.at[j, pl.ds(0, count - 1)], a_recv.at[stage, j])

    def x_forward(j):
        for c in range(3):
            out = product([tf[0, j], tf[1, j]], [rpieces[0, c], rpieces[1, c]], NT)
            x1[j, :, c] = out.reshape(ROWS, 2 * MC, 256)
        send_rows(0, j, x1, r1)

    def y_forward(j):
        await_all(0, j, r1, ROWS)
        for c in range(3):
            xs = [(r1[j, s, c, 0:MC], r1[j, s, c, MC : 2 * MC]) for s in range(8)]
            for k, (re, im) in enumerate(fft(xs, -1)):
                cos, sin = twy[0, k : k + 1], twy[1, k : k + 1]
                at = k * 3 * MC + c * MC
                ascr[at : at + MC, 0:256] = re * cos + im * sin
                ascr[at : at + MC, 256:512] = im * cos - re * sin
        out = product(split(ascr[...], 2), [kyf[0], kyf[1]]).reshape(8, 3, MC, 512)
        for half in range(2):
            for part in range(2):
                at = 256 * part + 128 * half
                y1[j, pl.ds(half, 8, 2), :, part] = out[:, :, :, at : at + 128]
        send_cols(1, j, y1, r2)

    def solve(j):
        await_all(1, j, r2, COLS)
        for c in range(3):
            xs = [(r2[j, s, c, 0], r2[j, s, c, 1]) for s in range(16)]
            for k, (re, im) in enumerate(fft(xs, -1)):
                cos, sin = twz[0, k : k + 1], twz[1, k : k + 1]
                at = k * 3 * MC + c * MC
                bscr[at : at + MC, 0:128] = re * cos + im * sin
                bscr[at : at + MC, 128:256] = im * cos - re * sin
        bscr[...] = product(split(bscr[...], 2), [kzf[0], kzf[1]])
        mode = row * 32 + j * MC + lax.broadcasted_iota(jnp.int32, (MC, 128), 0)
        lanes = lax.broadcasted_iota(jnp.int32, (MC, 128), 1)
        wave_x = mode.astype(F32) * (2.0 * math.pi / NX)
        index_y = col // 2 + 8 * (8 * lax.rem(col, 2) + lanes // 16)
        wave_y = jnp.where(index_y < NY // 2, index_y, index_y - NY).astype(F32) * (2.0 * math.pi / NY)
        keep_y = (index_y != NY // 2).astype(F32)
        for k in range(16):
            index_z = k + 16 * (lanes % 16)
            wave_z = jnp.where(index_z < NZ // 2, index_z, index_z - NZ).astype(F32) * (2.0 * math.pi / NZ)
            keep = keep_y * (index_z != NZ // 2).astype(F32)
            ksq = wave_x * wave_x + wave_y * wave_y + wave_z * wave_z
            inverse = 1.0 / jnp.where(ksq > 0, ksq, 1.0)
            gain = keep / (MASS + VISC * ksq)
            for part in range(2):
                at = 3 * MC * k
                lane = slice(128 * part, 128 * part + 128)
                fx, fy, fz = (bscr[at + MC * c : at + MC * c + MC, lane] for c in range(3))
                dotk = (wave_x * fx + wave_y * fy + wave_z * fz) * inverse
                bscr[at : at + MC, lane] = (fx - wave_x * dotk) * gain
                bscr[at + MC : at + 2 * MC, lane] = (fy - wave_y * dotk) * gain
                bscr[at + 2 * MC : at + 3 * MC, lane] = (fz - wave_z * dotk) * gain
        bscr[...] = product(split(bscr[...], INV), [kzi[p] for p in range(INV)])
        for c in range(3):
            xs = []
            for k in range(16):
                cos, sin = twz[0, k : k + 1], twz[1, k : k + 1]
                at = k * 3 * MC + c * MC
                re, im = bscr[at : at + MC, 0:128], bscr[at : at + MC, 128:256]
                xs.append((re * cos - im * sin, im * cos + re * sin))
            for s, (re, im) in enumerate(fft(xs, 1)):
                z1[j, s, c, 0] = re
                z1[j, s, c, 1] = im
        send_cols(2, j, z1, r3)

    def y_inverse(j):
        await_all(2, j, r3, COLS)
        for half in range(2):
            for part in range(2):
                at = 256 * part + 128 * half
                ascr[:, at : at + 128] = r3[j, pl.ds(half, 8, 2), :, part].reshape(8 * 3 * MC, 128)
        ascr[...] = product(split(ascr[...], INV), [kyi[p] for p in range(INV)])
        for c in range(3):
            xs = []
            for k in range(8):
                cos, sin = twy[0, k : k + 1], twy[1, k : k + 1]
                at = k * 3 * MC + c * MC
                re, im = ascr[at : at + MC, 0:256], ascr[at : at + MC, 256:512]
                xs.append((re * cos - im * sin, im * cos + re * sin))
            for s, (re, im) in enumerate(fft(xs, 1)):
                y2[j, s, c, 0:MC] = re
                y2[j, s, c, MC : 2 * MC] = im
        send_rows(3, j, y2, r4)

    def x_inverse(j):
        await_all(3, j, r4, ROWS)
        for c in range(3):
            spectrum = jnp.transpose(r4[j, :, c].reshape(2 * MC * ROWS, 256))
            fluid[c] += product(split(spectrum, INV), [ti[p, j] for p in range(INV)])

    def geometry():
        wait_for(g2.at[pl.ds(0, ROWS - 1)], g_recv.at[1])
        own = dot_exact(spread_runs[0:32], fields, NT) * 0.25
        ids = own[:, 0:1]
        count = jnp.zeros((32, 1), F32)
        cx, cy, cz = count, count, count
        for r in range(ROWS):
            block = g2[r]
            same = (ids == block[0:1]).astype(F32)
            match[r] = same
            count += jnp.sum(same, axis=1, keepdims=True)
            cx += jnp.sum(same * block[1:2], axis=1, keepdims=True)
            cy += jnp.sum(same * block[2:3], axis=1, keepdims=True)
            cz += jnp.sum(same * block[3:4], axis=1, keepdims=True)
        safe = jnp.maximum(count, 1.0)
        cx, cy, cz = cx / safe, cy / safe, cz / safe
        spread = jnp.zeros((32, 1), F32)
        for r in range(ROWS):
            block = g2[r]
            dx, dy, dz = block[1:2] - cx, block[2:3] - cy, block[3:4] - cz
            inner_spread = block[4:5] + 512.0 * (dx * dx + dy * dy + dz * dz)
            spread += jnp.sum(match[r] * inner_spread, axis=1, keepdims=True)
        inertia = jnp.maximum(spread * (2.0 / 3.0), 1.0)
        place = lane128
        packed = jnp.where(place == 0, 1.0 / jnp.maximum(512.0 * count, 1.0), 0.0)
        for at, value in ((1, cx), (2, cy), (3, cz), (4, 1.0 / inertia)):
            packed = jnp.where(place == at, value, packed)
        geo[...] = packed
        mine = dot_exact((pair == runs_lane).astype(F32), fields, NT)
        centers = dot_exact(gather_runs[:, 0:32], packed)
        rel = jnp.where(place == 0, mine[:, 1:2] + 63.5 - centers[:, 1:2], 0.0)
        rel = jnp.where(place == 1, mine[:, 2:3] - centers[:, 2:3], rel)
        mgeo[...] = jnp.where(place == 2, mine[:, 3:4] - centers[:, 3:4], rel)
        rows256 = lax.broadcasted_iota(jnp.int32, (256, 128), 0).astype(F32)
        cols256 = lax.broadcasted_iota(jnp.int32, (128, 256), 1).astype(F32)
        for b in range(4):
            hot[b] = ((fields[6:7] == rows256) & (fields[7:8] == float(b))).astype(F32).astype(BF16)
            hott[b] = ((mine[:, 6:7] == cols256) & (mine[:, 7:8] == float(b))).astype(F32).astype(BF16)

    loaded("tf")
    x_forward(0)
    x_forward(1)
    geometry()
    loaded("twy", "kyf", "twz", "kzf", "kzi", "kyi", "ti")

    @pl.loop(0, CHUNKS + 5)
    def _(t):
        pl.when(t < CHUNKS)(lambda: y_forward(t))
        pl.when(t + 2 < CHUNKS)(lambda: x_forward(t + 2))
        pl.when((t >= 2) & (t < CHUNKS + 2))(lambda: solve(t - 2))
        pl.when((t >= 4) & (t < CHUNKS + 4))(lambda: y_inverse(t - 4))
        pl.when(t >= 5)(lambda: x_inverse(t - 5))

    inside = lane128.astype(F32) - 63.5
    blocks = []
    firsts, seconds = [], []
    for c in range(3):
        block = jnp.zeros((128, 128), F32)
        for b in range(4):
            block += exact_left(hott[b], fluid[c, :, 128 * b : 128 * b + 128], 3)
        blocks.append(block)
        firsts.append(jnp.sum(block, axis=1, keepdims=True))
        seconds.append(jnp.sum(block * inside, axis=1, keepdims=True))
    rx, ry, rz = mgeo[:, 0:1], mgeo[:, 1:2], mgeo[:, 2:3]
    moments = jnp.zeros((128, 128), F32)
    for at, value in enumerate(
        (
            firsts[0],
            firsts[1],
            firsts[2],
            ry * firsts[2] - rz * firsts[1],
            rz * firsts[0] - (rx * firsts[2] + seconds[2]),
            rx * firsts[1] + seconds[1] - ry * firsts[0],
        )
    ):
        moments = jnp.where(lane128 == at, value, moments)
    gtile[1] = dot_exact(jnp.transpose(moments)[0:8], gather_runs)
    gather_cols(1, g3)
    gather_rows(1, g3, g4)
    wait_for(g4.at[pl.ds(0, ROWS - 1)], g_recv.at[3])
    totals = jnp.zeros((32, 8), F32)
    for r in range(ROWS):
        totals += dot_exact(match[r], g4[r], NT)
    packed = geo[...]
    params = jnp.zeros((32, 128), F32)
    for at in range(6):
        scale = packed[:, 0:1] if at < 3 else packed[:, 4:5]
        params = jnp.where(lane128 == at, totals[:, at : at + 1] * scale, params)
    fitted = dot_exact(gather_runs[:, 0:32], params)
    vx, vy, vz, wx, wy, wz = (fitted[:, k : k + 1] for k in range(6))
    cell_x = rx + inside
    rigid = (
        vx + wy * rz - wz * ry,
        vy + wz * cell_x - wx * rz,
        vz + wx * ry - wy * cell_x,
    )
    for c in range(3):
        fix = rigid[c] - blocks[c]
        for b in range(4):
            lanes = slice(128 * b, 128 * b + 128)
            done = fluid[c, :, lanes] + exact_left(hot[b], fix, 3)
            vext[c, 2:18, :, lanes] = done.reshape(16, 16, 128)
    for copy in stress_halos:
        copy.wait_send()
    for c in range(3):
        for layer, z in enumerate((0, 1, 14, 15)):
            zf[c, layer] = vext[c, 2:18, z, :]
    velocity_halos = halo_copies(4, vext, zf, vzh)
    for k, copy in enumerate(velocity_halos):
        copy.start()
    for copy in velocity_halos:
        copy.wait_recv()

    for copy in velocity_halos:
        copy.wait_send()
    wait_for(g1.at[pl.ds(0, COLS - 1)], g_send.at[0])
    wait_for(g2.at[pl.ds(0, ROWS - 1)], g_send.at[1])
    wait_for(g3.at[pl.ds(0, COLS - 1)], g_send.at[2])
    wait_for(g4.at[pl.ds(0, ROWS - 1)], g_send.at[3])

    @pl.loop(0, CHUNKS)
    def _(j):
        wait_for(x1.at[j, pl.ds(0, ROWS - 1)], a_send.at[0, j])
        wait_for(y1.at[j, pl.ds(0, COLS - 1)], a_send.at[1, j])
        wait_for(z1.at[j, pl.ds(0, COLS - 1)], a_send.at[2, j])
        wait_for(y2.at[j, pl.ds(0, ROWS - 1)], a_send.at[3, j])


def update(vext, vzh, mult, dzt, bzt, vel, new_aux, new_mult, *, lines):
    base = pl.program_id(0) * lines
    rows = 16 * lines
    edge = bzt[...]
    grads = []
    for c in range(3):
        field = vext[c, pl.ds(base + 2, lines)]
        vel[c] = field
        dx = along_x(field.reshape(rows, NX))
        near = [vext[c, pl.ds(base + k, lines)].reshape(rows, NX) for k in (0, 1, 3, 4)]
        dy = centered(*near)
        dz = exact_left(dzt[...], field.reshape(rows, NX), 3) + exact_left(edge, vzh[c], 3)
        grads.append((dx, dy, dz * (1.0 / 12.0)))
    strain = (
        grads[0][0],
        grads[1][1],
        grads[2][2],
        (grads[0][1] + grads[1][0]) * 0.5,
        (grads[0][2] + grads[2][0]) * 0.5,
        (grads[1][2] + grads[2][1]) * 0.5,
    )
    old = [mult[k].reshape(rows, NX) for k in range(6)]
    q = [old[k] + PEN * strain[k] for k in range(6)]
    norm = jnp.sqrt(
        q[0] * q[0] + q[1] * q[1] + q[2] * q[2] + 2.0 * (q[3] * q[3] + q[4] * q[4] + q[5] * q[5])
    )
    factor = 1.0 - YIELD / jnp.maximum(norm, YIELD)
    for k in range(6):
        aux = factor * q[k] * (1.0 / PEN)
        new_aux[k] = aux.reshape(lines, 16, NX)
        new_mult[k] = (old[k] + PEN * (strain[k] - aux)).reshape(lines, 16, NX)


def local(force, mult, aux, entry_lines, entry_owner, entry_slot):
    t = make_tables()
    vm = pl.BlockSpec(memory_space=pltpu.VMEM)
    hbm = pl.BlockSpec(memory_space=pltpu.HBM)
    sems = pltpu.SemaphoreType.DMA
    names = ("tf", "ti", "kyf", "kyi", "kzf", "kzi", "twy", "twz", "dz", "bz")
    loads = [force, mult, aux] + [jnp.asarray(t[k]) for k in names]
    scratch = [pltpu.VMEM(a.shape, a.dtype) for a in loads] + [
        pltpu.VMEM((3, 20, 16, NX), F32),
        pltpu.VMEM((3, 4, 16, NX), F32),
        pltpu.VMEM((3, 4, 16, NX), F32),
        pltpu.VMEM((3, 256, NX), F32),
        pltpu.VMEM((2, 3, 256, NX), BF16),
        pltpu.VMEM((3, 256, NX), F32),
        pltpu.VMEM((CHUNKS, ROWS, 3, 2 * MC, 256), F32),
        pltpu.VMEM((CHUNKS, ROWS, 3, 2 * MC, 256), F32),
        pltpu.VMEM((CHUNKS, COLS, 3, 2, MC, 128), F32),
        pltpu.VMEM((CHUNKS, COLS, 3, 2, MC, 128), F32),
        pltpu.VMEM((CHUNKS, COLS, 3, 2, MC, 128), F32),
        pltpu.VMEM((CHUNKS, COLS, 3, 2, MC, 128), F32),
        pltpu.VMEM((CHUNKS, ROWS, 3, 2 * MC, 256), F32),
        pltpu.VMEM((CHUNKS, ROWS, 3, 2 * MC, 256), F32),
        pltpu.VMEM((24 * MC, 512), F32),
        pltpu.VMEM((48 * MC, 256), F32),
        pltpu.VMEM((COLS, 8, 128), F32),
        pltpu.VMEM((ROWS, 8, 512), F32),
        pltpu.VMEM((COLS, 8, 128), F32),
        pltpu.VMEM((ROWS, 8, 512), F32),
        pltpu.VMEM((2, 8, 128), F32),
        pltpu.VMEM((ROWS, 32, 512), F32),
        pltpu.VMEM((32, 128), F32),
        pltpu.VMEM((128, 128), F32),
        pltpu.VMEM((4, 256, 128), BF16),
        pltpu.VMEM((4, 128, 256), BF16),
        sems((8,)),
        sems((8,)),
        sems((4, CHUNKS)),
        sems((4, CHUNKS)),
        sems((4,)),
        sems((4,)),
        sems((len(names) + 13,)),
    ]
    vext, vzh = pl.pallas_call(
        kernel,
        out_shape=(
            jax.ShapeDtypeStruct((3, 20, 16, NX), F32),
            jax.ShapeDtypeStruct((3, 4, 16, NX), F32),
        ),
        in_specs=[hbm] * 3 + [vm] * 3 + [hbm] * len(names),
        out_specs=(vm, vm),
        scratch_shapes=scratch,
        compiler_params=pltpu.CompilerParams(
            collective_id=0, has_side_effects=True, vmem_limit_bytes=58 * 2**20
        ),
    )(
        force,
        mult,
        aux,
        entry_lines.reshape(1, 128),
        entry_owner.reshape(1, 128),
        entry_slot.reshape(1, 128),
        *loads[3:],
    )

    lines = 4
    whole = lambda *shape: pl.BlockSpec(shape, lambda i: (0,) * len(shape))
    part = lambda n: pl.BlockSpec((n, lines, 16, NX), lambda i: (0, i, 0, 0))
    return tuple(
        pl.pallas_call(
            functools.partial(update, lines=lines),
            grid=(16 // lines,),
            out_shape=tuple(jax.ShapeDtypeStruct((n, 16, 16, NX), F32) for n in (3, 6, 6)),
            in_specs=[
                whole(3, 20, 16, NX),
                whole(3, 64, NX),
                part(6),
                whole(16 * lines, 16 * lines),
                pl.BlockSpec((16 * lines, 64), lambda i: (i, 0)),
            ],
            out_specs=tuple(part(n) for n in (3, 6, 6)),
            compiler_params=pltpu.CompilerParams(vmem_limit_bytes=58 * 2**20),
        )(
            vext,
            vzh.reshape(3, 64, NX),
            mult,
            jnp.asarray(deriv_rows(lines).astype(jnp.bfloat16)),
            jnp.asarray(t["bz"]),
        )
    )


def solution(mesh):
    field = P(None, "row", "col", None)
    return jax.shard_map(
        local,
        mesh=mesh,
        in_specs=(field, field, field, P(("row", "col")), P(("row", "col"), None), P(("row", "col"))),
        out_specs=(field, field, field),
        check_vma=False,
    )
```

```python
import functools
import math

import jax
import jax.numpy as jnp
import numpy as np
from jax import lax
from jax.experimental import pallas as pl
from jax.experimental.pallas import tpu as pltpu
from jax.sharding import PartitionSpec as P

MASS, VISC, PEN, YIELD = 0.02, 10.0, 5.0, 2.0
NPD = 72
NX, NY, NZ = 512, 128, 256
ROWS, COLS = 8, 16
CHUNKS = 4
MC = 32 // CHUNKS
F32, BF16 = jnp.float32, jnp.bfloat16
MESH = pl.DeviceIdType.MESH
HIGHEST = lax.Precision.HIGHEST
NN = (((1,), (0,)), ((), ()))
NT = (((1,), (1,)), ((), ()))

FAR = (
    (2, 2), (2, 1), (1, 2), (2, 3), (3, 2), (1, 1), (3, 3), (1, 3), (3, 1),
    (2, 0), (0, 2), (1, 0), (0, 1), (3, 0), (0, 3),
)

YCOMP = (3, 1, 5)
ZCOMP = (4, 5, 2)
XCOMP = (0, 3, 4)


def pieces_np(table, count):
    out = []
    rest = np.asarray(table, np.float64)
    for _ in range(count):
        piece = rest.astype(jnp.bfloat16)
        out.append(piece)
        rest = rest - piece.astype(np.float64)
    return np.stack(out)


def kron_dft(points, batch, sign):
    index = np.arange(points)
    angle = sign * 2 * np.pi * (np.outer(index, index) % points) / points
    eye = np.eye(batch)
    cos, sin = np.kron(np.cos(angle), eye), np.kron(np.sin(angle), eye)
    return np.block([[cos, sin], [-sin, cos]])


def kron_dft_z(sign):
    index = np.arange(16)
    angle = sign * 2 * np.pi * (np.outer(index, index) % 16) / 16
    eye = np.eye(8)
    cos, sin = np.kron(eye, np.cos(angle)), np.kron(eye, np.sin(angle))
    return np.block([[cos, sin], [-sin, cos]])


def mode_table():
    chunk, dest, part, inner = np.meshgrid(
        np.arange(CHUNKS), np.arange(ROWS), np.arange(2), np.arange(MC), indexing="ij"
    )
    mode = 32 * dest + MC * chunk + inner
    return mode.reshape(CHUNKS, -1), part.reshape(CHUNKS, -1)


def make_tables():
    mode, part = mode_table()
    x = np.arange(NX)
    angle = 2 * np.pi * ((mode[..., None] * x) % NX) / NX
    fwd = np.where(part[..., None] == 0, np.cos(angle), -np.sin(angle))
    weight = np.where(mode == 0, 1.0, 2.0)[..., None] / float(NX * NY * NZ)
    inv = weight * fwd
    ky_f = pieces_np(kron_dft(16, 16, -1), 2)
    ky_i = pieces_np(kron_dft(16, 16, 1), INV)
    kz_f = pieces_np(kron_dft_z(-1), 2)
    kz_i = pieces_np(kron_dft_z(1), INV)
    lane = np.arange(256)
    turn_y = 2 * np.pi * np.outer(np.arange(8), lane // 16) / NY
    turn_z = 2 * np.pi * np.outer(np.arange(16), np.arange(128) % 16) / NZ
    two_y = np.stack([np.cos(turn_y), np.sin(turn_y)]).astype(np.float32)
    two_z = np.stack([np.cos(turn_z), np.sin(turn_z)]).astype(np.float32)
    return {
        "tf": pieces_np(fwd, 2),
        "ti": pieces_np(inv, INV),
        "kyf": ky_f,
        "kyi": ky_i,
        "kzf": kz_f,
        "kzi": kz_i,
        "twy": two_y,
        "twz": two_z,
        "dz": deriv_rows(16).astype(jnp.bfloat16),
        "bz": deriv_halo().astype(jnp.bfloat16),
    }


INV = 3


def deriv_rows(lines):
    one = np.zeros((16, 16))
    for offset, coef in ((1, 8), (-1, -8), (2, -1), (-2, 1)):
        one += coef * np.eye(16, k=offset)
    return np.kron(np.eye(lines), one)


def deriv_halo():
    out = np.zeros((16, 16, 4, 16))
    for y in range(16):
        for layer, place in enumerate((-2, -1, 16, 17)):
            for z in range(16):
                out[y, z, layer, y] = {1: 8, -1: -8, 2: -1, -2: 1}.get(place - z, 0)
    return out.reshape(256, 64)


def split(value, count):
    out = []
    for step in range(count):
        piece = value.astype(BF16)
        out.append(piece)
        if step + 1 < count:
            value = value - piece.astype(F32)
    return out


def dot(a, b, dims=NN):
    return lax.dot_general(a, b, dims, preferred_element_type=F32)


def dot_exact(a, b, dims=NN):
    return lax.dot_general(a, b, dims, precision=HIGHEST, preferred_element_type=F32)


def product(a, b, dims=NN):
    count = len(a)
    total = None
    for i in range(count - 1, -1, -1):
        for j in range(count - 1 - i, -1, -1):
            term = dot(a[i], b[j], dims)
            total = term if total is None else total + term
    return total


def exact_left(a, value, count):
    total = None
    for piece in reversed(split(value, count)):
        term = dot(a, piece)
        total = term if total is None else total + term
    return total


def fft(xs, sign):
    count = len(xs)
    if count == 1:
        return xs
    even, odd = fft(xs[0::2], sign), fft(xs[1::2], sign)
    out = [None] * count
    half = count // 2
    for k in range(half):
        re, im = odd[k]
        if k == 0:
            tr, ti = re, im
        elif 4 * k == count:
            tr, ti = (-im, re) if sign > 0 else (im, -re)
        else:
            c = math.cos(2 * math.pi * k / count)
            s = sign * math.sin(2 * math.pi * k / count)
            tr, ti = re * c - im * s, re * s + im * c
        er, ei = even[k]
        out[k] = (er + tr, ei + ti)
        out[k + half] = (er - tr, ei - ti)
    return out


def along_x(field):
    axis = field.ndim - 1
    up1, up2 = pltpu.roll(field, NX - 1, axis), pltpu.roll(field, NX - 2, axis)
    lo1, lo2 = pltpu.roll(field, 1, axis), pltpu.roll(field, 2, axis)
    return (8.0 * (up1 - lo1) - (up2 - lo2)) * (1.0 / 12.0)


def centered(lo2, lo1, up1, up2):
    return (8.0 * (up1 - lo1) - (up2 - lo2)) * (1.0 / 12.0)


def kernel(
    force_in, mult_in, aux_in, lines_in, owner_in, slot_in,
    tf_in, ti_in, kyf_in, kyi_in, kzf_in, kzi_in, twy_in, twz_in, dzt_in, bzt_in,
    vext_out, vzh_out,
    force, mult, aux, tf, ti, kyf, kyi, kzf, kzi, twy, twz, dzt, bzt,
    yext, zf, zh, vext, vzh, rhs, rpieces, fluid,
    x1, r1, y1, r2, z1, r3, y2, r4, ascr, bscr,
    g1, g2, g3, g4, gtile, match, geo, mgeo, hot, hott,
    halo_send, halo_recv, a_send, a_recv, g_send, g_recv, load_sem, store_sem,
):
    row, col = lax.axis_index("row"), lax.axis_index("col")

    def row_peer(off):
        return lax.rem(row + off, ROWS)

    def col_peer(off):
        return lax.rem(col + off, COLS)

    def remote(src, dst, send, recv, device):
        return pltpu.make_async_remote_copy(
            src_ref=src, dst_ref=dst, send_sem=send, recv_sem=recv,
            device_id=device, device_id_type=MESH,
        )

    def wait_for(ref, sem):
        pltpu.make_async_copy(ref, ref, sem).wait()

    loads = {}

    def load(name, src, dst):
        loads[name] = pltpu.make_async_copy(src, dst, load_sem.at[len(loads)])
        loads[name].start()

    for comp in (4, 5, 2, 3, 1):
        load(("mult", comp), mult_in.at[comp], mult.at[comp])
        load(("aux", comp), aux_in.at[comp], aux.at[comp])
    load("dzt", dzt_in, dzt)
    load("bzt", bzt_in, bzt)
    load(("mult", 0), mult_in.at[0], mult.at[0])
    load(("aux", 0), aux_in.at[0], aux.at[0])
    load("force", force_in, force)
    for name, src, dst in (
        ("tf", tf_in, tf), ("twy", twy_in, twy), ("kyf", kyf_in, kyf), ("twz", twz_in, twz),
        ("kzf", kzf_in, kzf), ("kzi", kzi_in, kzi), ("kyi", kyi_in, kyi), ("ti", ti_in, ti),
    ):
        load(name, src, dst)

    def loaded(*names):
        for name in names:
            loads.pop(name).wait()

    barrier = pltpu.get_barrier_semaphore()
    for off in range(1, ROWS):
        pl.semaphore_signal(barrier, inc=1, device_id=(row_peer(off), col), device_id_type=MESH)
    for off in range(1, COLS):
        pl.semaphore_signal(barrier, inc=1, device_id=(row, col_peer(off)), device_id_type=MESH)

    def shifted(comp):
        return mult[comp] - PEN * aux[comp]

    for i, comp in enumerate(ZCOMP):
        loaded(("mult", comp), ("aux", comp))
        for layer, z in enumerate((0, 1, 14, 15)):
            zf[i, layer] = mult[comp, :, z, :] - PEN * aux[comp, :, z, :]
    pl.semaphore_wait(barrier, ROWS + COLS - 2)

    def halo_copies(base, ybuf, zsrc, zdst):
        up, down = (row_peer(1), col), (row_peer(ROWS - 1), col)
        right, left = (row, col_peer(1)), (row, col_peer(COLS - 1))
        sems = [(halo_send.at[base + k], halo_recv.at[base + k]) for k in range(4)]
        return [
            remote(zsrc.at[:, 2:4], zdst.at[:, 0:2], *sems[0], right),
            remote(zsrc.at[:, 0:2], zdst.at[:, 2:4], *sems[1], left),
            remote(ybuf.at[:, 16:18], ybuf.at[:, 0:2], *sems[2], up),
            remote(ybuf.at[:, 2:4], ybuf.at[:, 18:20], *sems[3], down),
        ]

    stress_halos = halo_copies(0, yext, zf, zh)
    for copy in stress_halos[0:2]:
        copy.start()
    for i, comp in enumerate(YCOMP):
        if comp != 5:
            loaded(("mult", comp), ("aux", comp))
        yext[i, 2:18] = shifted(comp)
    for copy in stress_halos[2:4]:
        copy.start()

    lane128 = lax.broadcasted_iota(jnp.int32, (1, 128), 1)
    lines, block_x = lines_in[...], lines_in[...] & 3
    particle = owner_in[...] * NPD + slot_in[...]
    gy = ((lines >> 6) + row * 16).astype(F32)
    gz = (((lines >> 2) & 15) + col * 16).astype(F32)
    fields = jnp.concatenate(
        [
            particle.astype(F32),
            (block_x * 128).astype(F32),
            gy,
            gz,
            gy * gy,
            gz * gz,
            (lines >> 2).astype(F32),
            block_x.astype(F32),
        ],
        axis=0,
    )
    pair = lax.broadcasted_iota(jnp.int32, (128, 128), 0)
    runs_lane = lax.broadcasted_iota(jnp.int32, (128, 128), 1)
    gather_runs = (pair // 4 == runs_lane).astype(F32)
    spread_runs = (runs_lane // 4 == pair).astype(F32)
    sums = dot_exact(fields, gather_runs)
    mean_y, mean_z = sums[2:3] * 0.25, sums[3:4] * 0.25
    inner = 4.0 * 174752.0 + 128.0 * (
        sums[4:5] - 4.0 * mean_y * mean_y + sums[5:6] - 4.0 * mean_z * mean_z
    )
    gtile[0] = jnp.concatenate(
        [sums[0:1] * 0.25, sums[1:2] * 0.25 + 63.5, mean_y, mean_z, inner, jnp.zeros((3, 128), F32)], axis=0
    )

    def gather_cols(slot, buf):
        buf[col] = gtile[slot]
        for off in range(1, COLS):
            remote(
                gtile.at[slot], buf.at[col], g_send.at[2 * slot], g_recv.at[2 * slot], (row, col_peer(off))
            ).start()

    def gather_rows(slot, buf, wide):
        wait_for(buf.at[pl.ds(0, COLS - 1)], g_recv.at[2 * slot])
        parts = []
        for q in range(4):
            total = None
            for k in range(4):
                tile = jnp.where(runs_lane[0:8] < 32, buf[4 * q + k], 0.0)
                tile = pltpu.roll(tile, 32 * k, 1) if k else tile
                total = tile if total is None else total + tile
            parts.append(total)
        wide[row] = jnp.concatenate(parts, axis=1)
        for off in range(1, ROWS):
            remote(
                wide.at[row], wide.at[row], g_send.at[2 * slot + 1], g_recv.at[2 * slot + 1], (row_peer(off), col)
            ).start()

    gather_cols(0, g1)

    loaded("dzt", "bzt", ("mult", 0), ("aux", 0), "force")
    for c, comp in enumerate(XCOMP):
        rhs[c] = (force[c] + along_x(shifted(comp))).reshape(256, NX)
    fluid[...] = jnp.zeros_like(fluid)
    for c, comp in enumerate(ZCOMP):
        own = shifted(comp).reshape(256, NX)
        rhs[c] += exact_left(dzt[...], own, 2) * (1.0 / 12.0)
    gather_rows(0, g1, g2)
    for copy in stress_halos:
        copy.wait_recv()
    for c in range(3):
        along_y = centered(yext[c, 0:16], yext[c, 1:17], yext[c, 3:19], yext[c, 4:20]).reshape(256, NX)
        edge = exact_left(bzt[...], zh[c].reshape(64, NX), 2) * (1.0 / 12.0)
        high, low = split(rhs[c] + along_y + edge, 2)
        rpieces[0, c] = high
        rpieces[1, c] = low

    def send_rows(stage, j, src, dst):
        dst[j, row] = src[j, row]
        for off in range(1, ROWS):
            peer = row_peer(off)
            remote(src.at[j, peer], dst.at[j, row], a_send.at[stage, j], a_recv.at[stage, j], (peer, col)).start()

    def send_cols(stage, j, src, dst):
        dst[j, col] = src[j, col]
        for dy, dz in FAR:
            peer = 4 * lax.rem(col // 4 + dz, 4) + lax.rem(col % 4 + dy, 4)
            remote(src.at[j, peer], dst.at[j, col], a_send.at[stage, j], a_recv.at[stage, j], (row, peer)).start()

    def await_all(stage, j, dst, count):
        wait_for(dst.at[j, pl.ds(0, count - 1)], a_recv.at[stage, j])

    def x_forward(j):
        for c in range(3):
            out = product([tf[0, j], tf[1, j]], [rpieces[0, c], rpieces[1, c]], NT)
            x1[j, :, c] = out.reshape(ROWS, 2 * MC, 256)
        send_rows(0, j, x1, r1)

    def y_forward(j):
        await_all(0, j, r1, ROWS)
        for c in range(3):
            xs = [(r1[j, s, c, 0:MC], r1[j, s, c, MC : 2 * MC]) for s in range(8)]
            for k, (re, im) in enumerate(fft(xs, -1)):
                cos, sin = twy[0, k : k + 1], twy[1, k : k + 1]
                at = k * 3 * MC + c * MC
                ascr[at : at + MC, 0:256] = re * cos + im * sin
                ascr[at : at + MC, 256:512] = im * cos - re * sin
        out = product(split(ascr[...], 2), [kyf[0], kyf[1]]).reshape(8, 3, MC, 512)
        for half in range(2):
            for part in range(2):
                at = 256 * part + 128 * half
                y1[j, pl.ds(half, 8, 2), :, part] = out[:, :, :, at : at + 128]
        send_cols(1, j, y1, r2)

    def solve(j):
        await_all(1, j, r2, COLS)
        for c in range(3):
            xs = [(r2[j, s, c, 0], r2[j, s, c, 1]) for s in range(16)]
            for k, (re, im) in enumerate(fft(xs, -1)):
                cos, sin = twz[0, k : k + 1], twz[1, k : k + 1]
                at = k * 3 * MC + c * MC
                bscr[at : at + MC, 0:128] = re * cos + im * sin
                bscr[at : at + MC, 128:256] = im * cos - re * sin
        bscr[...] = product(split(bscr[...], 2), [kzf[0], kzf[1]])
        mode = row * 32 + j * MC + lax.broadcasted_iota(jnp.int32, (MC, 128), 0)
        lanes = lax.broadcasted_iota(jnp.int32, (MC, 128), 1)
        wave_x = mode.astype(F32) * (2.0 * math.pi / NX)
        index_y = col // 2 + 8 * (8 * lax.rem(col, 2) + lanes // 16)
        wave_y = jnp.where(index_y < NY // 2, index_y, index_y - NY).astype(F32) * (2.0 * math.pi / NY)
        keep_y = (index_y != NY // 2).astype(F32)
        for k in range(16):
            index_z = k + 16 * (lanes % 16)
            wave_z = jnp.where(index_z < NZ // 2, index_z, index_z - NZ).astype(F32) * (2.0 * math.pi / NZ)
            keep = keep_y * (index_z != NZ // 2).astype(F32)
            ksq = wave_x * wave_x + wave_y * wave_y + wave_z * wave_z
            inverse = 1.0 / jnp.where(ksq > 0, ksq, 1.0)
            gain = keep / (MASS + VISC * ksq)
            for part in range(2):
                at = 3 * MC * k
                lane = slice(128 * part, 128 * part + 128)
                fx, fy, fz = (bscr[at + MC * c : at + MC * c + MC, lane] for c in range(3))
                dotk = (wave_x * fx + wave_y * fy + wave_z * fz) * inverse
                bscr[at : at + MC, lane] = (fx - wave_x * dotk) * gain
                bscr[at + MC : at + 2 * MC, lane] = (fy - wave_y * dotk) * gain
                bscr[at + 2 * MC : at + 3 * MC, lane] = (fz - wave_z * dotk) * gain
        bscr[...] = product(split(bscr[...], INV), [kzi[p] for p in range(INV)])
        for c in range(3):
            xs = []
            for k in range(16):
                cos, sin = twz[0, k : k + 1], twz[1, k : k + 1]
                at = k * 3 * MC + c * MC
                re, im = bscr[at : at + MC, 0:128], bscr[at : at + MC, 128:256]
                xs.append((re * cos - im * sin, im * cos + re * sin))
            for s, (re, im) in enumerate(fft(xs, 1)):
                z1[j, s, c, 0] = re
                z1[j, s, c, 1] = im
        send_cols(2, j, z1, r3)

    def y_inverse(j):
        await_all(2, j, r3, COLS)
        for half in range(2):
            for part in range(2):
                at = 256 * part + 128 * half
                ascr[:, at : at + 128] = r3[j, pl.ds(half, 8, 2), :, part].reshape(8 * 3 * MC, 128)
        ascr[...] = product(split(ascr[...], INV), [kyi[p] for p in range(INV)])
        for c in range(3):
            xs = []
            for k in range(8):
                cos, sin = twy[0, k : k + 1], twy[1, k : k + 1]
                at = k * 3 * MC + c * MC
                re, im = ascr[at : at + MC, 0:256], ascr[at : at + MC, 256:512]
                xs.append((re * cos - im * sin, im * cos + re * sin))
            for s, (re, im) in enumerate(fft(xs, 1)):
                y2[j, s, c, 0:MC] = re
                y2[j, s, c, MC : 2 * MC] = im
        send_rows(3, j, y2, r4)

    def x_inverse(j):
        await_all(3, j, r4, ROWS)
        for c in range(3):
            spectrum = jnp.transpose(r4[j, :, c].reshape(2 * MC * ROWS, 256))
            fluid[c] += product(split(spectrum, INV), [ti[p, j] for p in range(INV)])

    def geometry():
        wait_for(g2.at[pl.ds(0, ROWS - 1)], g_recv.at[1])
        own = dot_exact(spread_runs[0:32], fields, NT) * 0.25
        ids = own[:, 0:1]
        count = jnp.zeros((32, 1), F32)
        cx, cy, cz = count, count, count
        for r in range(ROWS):
            block = g2[r]
            same = (ids == block[0:1]).astype(F32)
            match[r] = same
            count += jnp.sum(same, axis=1, keepdims=True)
            cx += jnp.sum(same * block[1:2], axis=1, keepdims=True)
            cy += jnp.sum(same * block[2:3], axis=1, keepdims=True)
            cz += jnp.sum(same * block[3:4], axis=1, keepdims=True)
        safe = jnp.maximum(count, 1.0)
        cx, cy, cz = cx / safe, cy / safe, cz / safe
        spread = jnp.zeros((32, 1), F32)
        for r in range(ROWS):
            block = g2[r]
            dx, dy, dz = block[1:2] - cx, block[2:3] - cy, block[3:4] - cz
            inner_spread = block[4:5] + 512.0 * (dx * dx + dy * dy + dz * dz)
            spread += jnp.sum(match[r] * inner_spread, axis=1, keepdims=True)
        inertia = jnp.maximum(spread * (2.0 / 3.0), 1.0)
        place = lane128
        packed = jnp.where(place == 0, 1.0 / jnp.maximum(512.0 * count, 1.0), 0.0)
        for at, value in ((1, cx), (2, cy), (3, cz), (4, 1.0 / inertia)):
            packed = jnp.where(place == at, value, packed)
        geo[...] = packed
        mine = dot_exact((pair == runs_lane).astype(F32), fields, NT)
        centers = dot_exact(gather_runs[:, 0:32], packed)
        rel = jnp.where(place == 0, mine[:, 1:2] + 63.5 - centers[:, 1:2], 0.0)
        rel = jnp.where(place == 1, mine[:, 2:3] - centers[:, 2:3], rel)
        mgeo[...] = jnp.where(place == 2, mine[:, 3:4] - centers[:, 3:4], rel)
        rows256 = lax.broadcasted_iota(jnp.int32, (256, 128), 0).astype(F32)
        cols256 = lax.broadcasted_iota(jnp.int32, (128, 256), 1).astype(F32)
        for b in range(4):
            hot[b] = ((fields[6:7] == rows256) & (fields[7:8] == float(b))).astype(F32).astype(BF16)
            hott[b] = ((mine[:, 6:7] == cols256) & (mine[:, 7:8] == float(b))).astype(F32).astype(BF16)

    loaded("tf")
    x_forward(0)
    x_forward(1)
    geometry()
    loaded("twy", "kyf", "twz", "kzf", "kzi", "kyi", "ti")

    @pl.loop(0, CHUNKS + 5)
    def _(t):
        pl.when(t < CHUNKS)(lambda: y_forward(t))
        pl.when(t + 2 < CHUNKS)(lambda: x_forward(t + 2))
        pl.when((t >= 2) & (t < CHUNKS + 2))(lambda: solve(t - 2))
        pl.when((t >= 4) & (t < CHUNKS + 4))(lambda: y_inverse(t - 4))
        pl.when(t >= 5)(lambda: x_inverse(t - 5))

    inside = lane128.astype(F32) - 63.5
    blocks = []
    firsts, seconds = [], []
    for c in range(3):
        block = jnp.zeros((128, 128), F32)
        for b in range(4):
            block += exact_left(hott[b], fluid[c, :, 128 * b : 128 * b + 128], 3)
        blocks.append(block)
        firsts.append(jnp.sum(block, axis=1, keepdims=True))
        seconds.append(jnp.sum(block * inside, axis=1, keepdims=True))
    rx, ry, rz = mgeo[:, 0:1], mgeo[:, 1:2], mgeo[:, 2:3]
    moments = jnp.zeros((128, 128), F32)
    for at, value in enumerate(
        (
            firsts[0],
            firsts[1],
            firsts[2],
            ry * firsts[2] - rz * firsts[1],
            rz * firsts[0] - (rx * firsts[2] + seconds[2]),
            rx * firsts[1] + seconds[1] - ry * firsts[0],
        )
    ):
        moments = jnp.where(lane128 == at, value, moments)
    gtile[1] = dot_exact(jnp.transpose(moments)[0:8], gather_runs)
    gather_cols(1, g3)
    gather_rows(1, g3, g4)
    wait_for(g4.at[pl.ds(0, ROWS - 1)], g_recv.at[3])
    totals = jnp.zeros((32, 8), F32)
    for r in range(ROWS):
        totals += dot_exact(match[r], g4[r], NT)
    packed = geo[...]
    params = jnp.zeros((32, 128), F32)
    for at in range(6):
        scale = packed[:, 0:1] if at < 3 else packed[:, 4:5]
        params = jnp.where(lane128 == at, totals[:, at : at + 1] * scale, params)
    fitted = dot_exact(gather_runs[:, 0:32], params)
    vx, vy, vz, wx, wy, wz = (fitted[:, k : k + 1] for k in range(6))
    cell_x = rx + inside
    rigid = (
        vx + wy * rz - wz * ry,
        vy + wz * cell_x - wx * rz,
        vz + wx * ry - wy * cell_x,
    )
    for c in range(3):
        fix = rigid[c] - blocks[c]
        for b in range(4):
            lanes = slice(128 * b, 128 * b + 128)
            done = fluid[c, :, lanes] + exact_left(hot[b], fix, 3)
            vext[c, 2:18, :, lanes] = done.reshape(16, 16, 128)
    for copy in stress_halos:
        copy.wait_send()
    for c in range(3):
        for layer, z in enumerate((0, 1, 14, 15)):
            zf[c, layer] = vext[c, 2:18, z, :]
    velocity_halos = halo_copies(4, vext, zf, vzh)
    for copy in velocity_halos:
        copy.start()
    stores = [pltpu.make_async_copy(vext.at[c, 2:18], vext_out.at[c, 2:18], store_sem.at[c]) for c in range(3)]
    for store in stores:
        store.start()
    for copy in velocity_halos:
        copy.wait_recv()
    late = [
        pltpu.make_async_copy(vext.at[:, 0:2], vext_out.at[:, 0:2], store_sem.at[3]),
        pltpu.make_async_copy(vext.at[:, 18:20], vext_out.at[:, 18:20], store_sem.at[4]),
        pltpu.make_async_copy(vzh, vzh_out, store_sem.at[5]),
    ]
    for store in late:
        store.start()
    stores += late

    for copy in velocity_halos:
        copy.wait_send()
    wait_for(g1.at[pl.ds(0, COLS - 1)], g_send.at[0])
    wait_for(g2.at[pl.ds(0, ROWS - 1)], g_send.at[1])
    wait_for(g3.at[pl.ds(0, COLS - 1)], g_send.at[2])
    wait_for(g4.at[pl.ds(0, ROWS - 1)], g_send.at[3])

    @pl.loop(0, CHUNKS)
    def _(j):
        wait_for(x1.at[j, pl.ds(0, ROWS - 1)], a_send.at[0, j])
        wait_for(y1.at[j, pl.ds(0, COLS - 1)], a_send.at[1, j])
        wait_for(z1.at[j, pl.ds(0, COLS - 1)], a_send.at[2, j])
        wait_for(y2.at[j, pl.ds(0, ROWS - 1)], a_send.at[3, j])

    for store in stores:
        store.wait()


def update(vlow, vhigh, vzh, mult, dzt, bzt, vel, new_aux, new_mult, *, lines):
    rows = 16 * lines
    edge = bzt[...]
    grads = []
    for c in range(3):
        both = jnp.concatenate([vlow[c], vhigh[c]], axis=0)
        field = both[2 : lines + 2]
        vel[c] = field
        dx = along_x(field.reshape(rows, NX))
        near = [both[k : lines + k].reshape(rows, NX) for k in (0, 1, 3, 4)]
        dy = centered(*near)
        dz = exact_left(dzt[...], field.reshape(rows, NX), 3) + exact_left(edge, vzh[c], 3)
        grads.append((dx, dy, dz * (1.0 / 12.0)))
    strain = (
        grads[0][0],
        grads[1][1],
        grads[2][2],
        (grads[0][1] + grads[1][0]) * 0.5,
        (grads[0][2] + grads[2][0]) * 0.5,
        (grads[1][2] + grads[2][1]) * 0.5,
    )
    old = [mult[k].reshape(rows, NX) for k in range(6)]
    q = [old[k] + PEN * strain[k] for k in range(6)]
    norm = jnp.sqrt(
        q[0] * q[0] + q[1] * q[1] + q[2] * q[2] + 2.0 * (q[3] * q[3] + q[4] * q[4] + q[5] * q[5])
    )
    factor = 1.0 - YIELD / jnp.maximum(norm, YIELD)
    for k in range(6):
        aux = factor * q[k] * (1.0 / PEN)
        new_aux[k] = aux.reshape(lines, 16, NX)
        new_mult[k] = (old[k] + PEN * (strain[k] - aux)).reshape(lines, 16, NX)


def local(force, mult, aux, entry_lines, entry_owner, entry_slot):
    t = make_tables()
    vm = pl.BlockSpec(memory_space=pltpu.VMEM)
    hbm = pl.BlockSpec(memory_space=pltpu.HBM)
    sems = pltpu.SemaphoreType.DMA
    names = ("tf", "ti", "kyf", "kyi", "kzf", "kzi", "twy", "twz", "dz", "bz")
    loads = [force, mult, aux] + [jnp.asarray(t[k]) for k in names]
    scratch = [pltpu.VMEM(a.shape, a.dtype) for a in loads] + [
        pltpu.VMEM((3, 20, 16, NX), F32),
        pltpu.VMEM((3, 4, 16, NX), F32),
        pltpu.VMEM((3, 4, 16, NX), F32),
        pltpu.VMEM((3, 20, 16, NX), F32),
        pltpu.VMEM((3, 4, 16, NX), F32),
        pltpu.VMEM((3, 256, NX), F32),
        pltpu.VMEM((2, 3, 256, NX), BF16),
        pltpu.VMEM((3, 256, NX), F32),
        pltpu.VMEM((CHUNKS, ROWS, 3, 2 * MC, 256), F32),
        pltpu.VMEM((CHUNKS, ROWS, 3, 2 * MC, 256), F32),
        pltpu.VMEM((CHUNKS, COLS, 3, 2, MC, 128), F32),
        pltpu.VMEM((CHUNKS, COLS, 3, 2, MC, 128), F32),
        pltpu.VMEM((CHUNKS, COLS, 3, 2, MC, 128), F32),
        pltpu.VMEM((CHUNKS, COLS, 3, 2, MC, 128), F32),
        pltpu.VMEM((CHUNKS, ROWS, 3, 2 * MC, 256), F32),
        pltpu.VMEM((CHUNKS, ROWS, 3, 2 * MC, 256), F32),
        pltpu.VMEM((24 * MC, 512), F32),
        pltpu.VMEM((48 * MC, 256), F32),
        pltpu.VMEM((COLS, 8, 128), F32),
        pltpu.VMEM((ROWS, 8, 512), F32),
        pltpu.VMEM((COLS, 8, 128), F32),
        pltpu.VMEM((ROWS, 8, 512), F32),
        pltpu.VMEM((2, 8, 128), F32),
        pltpu.VMEM((ROWS, 32, 512), F32),
        pltpu.VMEM((32, 128), F32),
        pltpu.VMEM((128, 128), F32),
        pltpu.VMEM((4, 256, 128), BF16),
        pltpu.VMEM((4, 128, 256), BF16),
        sems((8,)),
        sems((8,)),
        sems((4, CHUNKS)),
        sems((4, CHUNKS)),
        sems((4,)),
        sems((4,)),
        sems((len(names) + 13,)),
        sems((6,)),
    ]
    vext, vzh = pl.pallas_call(
        kernel,
        out_shape=(
            jax.ShapeDtypeStruct((3, 20, 16, NX), F32),
            jax.ShapeDtypeStruct((3, 4, 16, NX), F32),
        ),
        in_specs=[hbm] * 3 + [vm] * 3 + [hbm] * len(names),
        out_specs=(hbm, hbm),
        scratch_shapes=scratch,
        compiler_params=pltpu.CompilerParams(
            collective_id=0, has_side_effects=True, vmem_limit_bytes=58 * 2**20
        ),
    )(
        force,
        mult,
        aux,
        entry_lines.reshape(1, 128),
        entry_owner.reshape(1, 128),
        entry_slot.reshape(1, 128),
        *loads[3:],
    )

    lines = 4
    whole = lambda *shape: pl.BlockSpec(shape, lambda i: (0,) * len(shape))
    part = lambda n: pl.BlockSpec((n, lines, 16, NX), lambda i: (0, i, 0, 0))
    return tuple(
        pl.pallas_call(
            functools.partial(update, lines=lines),
            grid=(16 // lines,),
            out_shape=tuple(jax.ShapeDtypeStruct((n, 16, 16, NX), F32) for n in (3, 6, 6)),
            in_specs=[
                part(3),
                pl.BlockSpec((3, lines, 16, NX), lambda i: (0, i + 1, 0, 0)),
                whole(3, 64, NX),
                part(6),
                whole(16 * lines, 16 * lines),
                pl.BlockSpec((16 * lines, 64), lambda i: (i, 0)),
            ],
            out_specs=tuple(part(n) for n in (3, 6, 6)),
            compiler_params=pltpu.CompilerParams(vmem_limit_bytes=58 * 2**20),
        )(
            vext,
            vext,
            vzh.reshape(3, 64, NX),
            mult,
            jnp.asarray(deriv_rows(lines).astype(jnp.bfloat16)),
            jnp.asarray(t["bz"]),
        )
    )


def solution(mesh):
    field = P(None, "row", "col", None)
    return jax.shard_map(
        local,
        mesh=mesh,
        in_specs=(field, field, field, P(("row", "col")), P(("row", "col"), None), P(("row", "col"))),
        out_specs=(field, field, field),
        check_vma=False,
    )
```

```python
import functools
import math

import jax
import jax.numpy as jnp
import numpy as np
from jax import lax
from jax.experimental import pallas as pl
from jax.experimental.pallas import tpu as pltpu
from jax.sharding import PartitionSpec as P

MASS, VISC, PEN, YIELD = 0.02, 10.0, 5.0, 2.0
NPD = 72
NX, NY, NZ = 512, 128, 256
ROWS, COLS = 8, 16
CHUNKS = 4
MC = 32 // CHUNKS
F32, BF16 = jnp.float32, jnp.bfloat16
MESH = pl.DeviceIdType.MESH
HIGHEST = lax.Precision.HIGHEST
NN = (((1,), (0,)), ((), ()))
NT = (((1,), (1,)), ((), ()))

FAR = (
    (2, 2), (2, 1), (1, 2), (2, 3), (3, 2), (1, 1), (3, 3), (1, 3), (3, 1),
    (2, 0), (0, 2), (1, 0), (0, 1), (3, 0), (0, 3),
)

YCOMP = (3, 1, 5)
ZCOMP = (4, 5, 2)
XCOMP = (0, 3, 4)


def pieces_np(table, count):
    out = []
    rest = np.asarray(table, np.float64)
    for _ in range(count):
        piece = rest.astype(jnp.bfloat16)
        out.append(piece)
        rest = rest - piece.astype(np.float64)
    return np.stack(out)


def kron_dft(points, batch, sign):
    index = np.arange(points)
    angle = sign * 2 * np.pi * (np.outer(index, index) % points) / points
    eye = np.eye(batch)
    cos, sin = np.kron(np.cos(angle), eye), np.kron(np.sin(angle), eye)
    return np.block([[cos, sin], [-sin, cos]])


def kron_dft_z(sign):
    index = np.arange(16)
    angle = sign * 2 * np.pi * (np.outer(index, index) % 16) / 16
    eye = np.eye(8)
    cos, sin = np.kron(eye, np.cos(angle)), np.kron(eye, np.sin(angle))
    return np.block([[cos, sin], [-sin, cos]])


def mode_table():
    chunk, dest, part, inner = np.meshgrid(
        np.arange(CHUNKS), np.arange(ROWS), np.arange(2), np.arange(MC), indexing="ij"
    )
    mode = 32 * dest + MC * chunk + inner
    return mode.reshape(CHUNKS, -1), part.reshape(CHUNKS, -1)


def make_tables():
    mode, part = mode_table()
    x = np.arange(NX)
    angle = 2 * np.pi * ((mode[..., None] * x) % NX) / NX
    fwd = np.where(part[..., None] == 0, np.cos(angle), -np.sin(angle))
    weight = np.where(mode == 0, 1.0, 2.0)[..., None] / float(NX * NY * NZ)
    inv = weight * fwd
    ky_f = pieces_np(kron_dft(16, 16, -1), 2)
    ky_i = pieces_np(kron_dft(16, 16, 1), INV)
    kz_f = pieces_np(kron_dft_z(-1), 2)
    kz_i = pieces_np(kron_dft_z(1), INV)
    lane = np.arange(256)
    turn_y = 2 * np.pi * np.outer(np.arange(8), lane // 16) / NY
    turn_z = 2 * np.pi * np.outer(np.arange(16), np.arange(128) % 16) / NZ
    two_y = np.stack([np.cos(turn_y), np.sin(turn_y)]).astype(np.float32)
    two_z = np.stack([np.cos(turn_z), np.sin(turn_z)]).astype(np.float32)
    return {
        "tf": pieces_np(fwd, 2),
        "ti": pieces_np(inv, INV),
        "kyf": ky_f,
        "kyi": ky_i,
        "kzf": kz_f,
        "kzi": kz_i,
        "twy": two_y,
        "twz": two_z,
        "dz": deriv_rows(16).astype(jnp.bfloat16),
        "bz": deriv_halo().astype(jnp.bfloat16),
    }


INV = 3


def deriv_rows(lines):
    one = np.zeros((16, 16))
    for offset, coef in ((1, 8), (-1, -8), (2, -1), (-2, 1)):
        one += coef * np.eye(16, k=offset)
    return np.kron(np.eye(lines), one)


def deriv_halo():
    out = np.zeros((16, 16, 4, 16))
    for y in range(16):
        for layer, place in enumerate((-2, -1, 16, 17)):
            for z in range(16):
                out[y, z, layer, y] = {1: 8, -1: -8, 2: -1, -2: 1}.get(place - z, 0)
    return out.reshape(256, 64)


def split(value, count):
    out = []
    for step in range(count):
        piece = value.astype(BF16)
        out.append(piece)
        if step + 1 < count:
            value = value - piece.astype(F32)
    return out


def dot(a, b, dims=NN):
    return lax.dot_general(a, b, dims, preferred_element_type=F32)


def dot_exact(a, b, dims=NN):
    return lax.dot_general(a, b, dims, precision=HIGHEST, preferred_element_type=F32)


def product(a, b, dims=NN):
    count = len(a)
    total = None
    for i in range(count - 1, -1, -1):
        for j in range(count - 1 - i, -1, -1):
            term = dot(a[i], b[j], dims)
            total = term if total is None else total + term
    return total


def exact_left(a, value, count):
    total = None
    for piece in reversed(split(value, count)):
        term = dot(a, piece)
        total = term if total is None else total + term
    return total


def fft(xs, sign):
    count = len(xs)
    if count == 1:
        return xs
    even, odd = fft(xs[0::2], sign), fft(xs[1::2], sign)
    out = [None] * count
    half = count // 2
    for k in range(half):
        re, im = odd[k]
        if k == 0:
            tr, ti = re, im
        elif 4 * k == count:
            tr, ti = (-im, re) if sign > 0 else (im, -re)
        else:
            c = math.cos(2 * math.pi * k / count)
            s = sign * math.sin(2 * math.pi * k / count)
            tr, ti = re * c - im * s, re * s + im * c
        er, ei = even[k]
        out[k] = (er + tr, ei + ti)
        out[k + half] = (er - tr, ei - ti)
    return out


def along_x(field):
    axis = field.ndim - 1
    up1, up2 = pltpu.roll(field, NX - 1, axis), pltpu.roll(field, NX - 2, axis)
    lo1, lo2 = pltpu.roll(field, 1, axis), pltpu.roll(field, 2, axis)
    return (8.0 * (up1 - lo1) - (up2 - lo2)) * (1.0 / 12.0)


def centered(lo2, lo1, up1, up2):
    return (8.0 * (up1 - lo1) - (up2 - lo2)) * (1.0 / 12.0)


def kernel(
    force_in, mult_in, aux_in, lines_in, owner_in, slot_in,
    tf_in, ti_in, kyf_in, kyi_in, kzf_in, kzi_in, twy_in, twz_in, dzt_in, bzt_in,
    vext_out, vzh_out,
    force, mult, aux, tf, ti, kyf, kyi, kzf, kzi, twy, twz, dzt, bzt,
    yext, zf, zh, vext, vzh, rhs, rpieces, fluid,
    x1, r1, y1, r2, z1, r3, y2, r4, ascr, bscr,
    g1, g2, g3, g4, gtile, match, mgeo, hot, hott, nbtile, nbcol, nbhot, nbkeep,
    halo_send, halo_recv, a_send, a_recv, g_send, g_recv, load_sem, store_sem,
):
    row, col = lax.axis_index("row"), lax.axis_index("col")

    def row_peer(off):
        return lax.rem(row + off, ROWS)

    def col_peer(off):
        return lax.rem(col + off, COLS)

    def remote(src, dst, send, recv, device):
        return pltpu.make_async_remote_copy(
            src_ref=src, dst_ref=dst, send_sem=send, recv_sem=recv,
            device_id=device, device_id_type=MESH,
        )

    def wait_for(ref, sem):
        pltpu.make_async_copy(ref, ref, sem).wait()

    loads = {}

    def load(name, src, dst):
        loads[name] = pltpu.make_async_copy(src, dst, load_sem.at[len(loads)])
        loads[name].start()

    for comp in (4, 5, 2, 3, 1):
        load(("mult", comp), mult_in.at[comp], mult.at[comp])
        load(("aux", comp), aux_in.at[comp], aux.at[comp])
    load("dzt", dzt_in, dzt)
    load("bzt", bzt_in, bzt)
    load(("mult", 0), mult_in.at[0], mult.at[0])
    load(("aux", 0), aux_in.at[0], aux.at[0])
    load("force", force_in, force)
    for name, src, dst in (
        ("tf", tf_in, tf), ("twy", twy_in, twy), ("kyf", kyf_in, kyf), ("twz", twz_in, twz),
        ("kzf", kzf_in, kzf), ("kzi", kzi_in, kzi), ("kyi", kyi_in, kyi), ("ti", ti_in, ti),
    ):
        load(name, src, dst)

    def loaded(*names):
        for name in names:
            loads.pop(name).wait()

    barrier = pltpu.get_barrier_semaphore()
    for off in range(1, ROWS):
        pl.semaphore_signal(barrier, inc=1, device_id=(row_peer(off), col), device_id_type=MESH)
    for off in range(1, COLS):
        pl.semaphore_signal(barrier, inc=1, device_id=(row, col_peer(off)), device_id_type=MESH)

    def shifted(comp):
        return mult[comp] - PEN * aux[comp]

    for i, comp in enumerate(ZCOMP):
        loaded(("mult", comp), ("aux", comp))
        for layer, z in enumerate((0, 1, 14, 15)):
            zf[i, layer] = mult[comp, :, z, :] - PEN * aux[comp, :, z, :]
    pl.semaphore_wait(barrier, ROWS + COLS - 2)

    def halo_copies(base, ysrc, high, low, ydst, zsrc, zdst):
        up, down = (row_peer(1), col), (row_peer(ROWS - 1), col)
        right, left = (row, col_peer(1)), (row, col_peer(COLS - 1))
        sems = [(halo_send.at[base + k], halo_recv.at[base + k]) for k in range(4)]
        return [
            remote(zsrc.at[:, 2:4], zdst.at[:, 0:2], *sems[0], right),
            remote(zsrc.at[:, 0:2], zdst.at[:, 2:4], *sems[1], left),
            remote(ysrc.at[:, high : high + 2], ydst.at[:, 0:2], *sems[2], up),
            remote(ysrc.at[:, low : low + 2], ydst.at[:, 18:20], *sems[3], down),
        ]

    stress_halos = halo_copies(0, yext, 16, 2, yext, zf, zh)
    for copy in stress_halos[0:2]:
        copy.start()
    for i, comp in enumerate(YCOMP):
        if comp != 5:
            loaded(("mult", comp), ("aux", comp))
        yext[i, 2:18] = shifted(comp)
    for copy in stress_halos[2:4]:
        copy.start()

    lane128 = lax.broadcasted_iota(jnp.int32, (1, 128), 1)
    lines, block_x = lines_in[...], lines_in[...] & 3
    particle = owner_in[...] * NPD + slot_in[...]
    gy = ((lines >> 6) + row * 16).astype(F32)
    gz = (((lines >> 2) & 15) + col * 16).astype(F32)
    fields = jnp.concatenate(
        [
            particle.astype(F32),
            (block_x * 128).astype(F32),
            gy,
            gz,
            gy * gy,
            gz * gz,
            (lines >> 2).astype(F32),
            block_x.astype(F32),
        ],
        axis=0,
    )
    pair = lax.broadcasted_iota(jnp.int32, (128, 128), 0)
    runs_lane = lax.broadcasted_iota(jnp.int32, (128, 128), 1)
    gather_runs = (pair // 4 == runs_lane).astype(F32)
    spread_runs = (runs_lane // 4 == pair).astype(F32)
    sums = dot_exact(fields, gather_runs)
    mean_y, mean_z = sums[2:3] * 0.25, sums[3:4] * 0.25
    inner = 4.0 * 174752.0 + 128.0 * (
        sums[4:5] - 4.0 * mean_y * mean_y + sums[5:6] - 4.0 * mean_z * mean_z
    )
    gtile[0] = jnp.concatenate(
        [sums[0:1] * 0.25, sums[1:2] * 0.25 + 63.5, mean_y, mean_z, inner, jnp.zeros((3, 128), F32)], axis=0
    )

    def gather_cols(slot, buf):
        buf[col] = gtile[slot]
        for off in range(1, COLS):
            remote(
                gtile.at[slot], buf.at[col], g_send.at[2 * slot], g_recv.at[2 * slot], (row, col_peer(off))
            ).start()

    def gather_rows(slot, buf, wide):
        wait_for(buf.at[pl.ds(0, COLS - 1)], g_recv.at[2 * slot])
        parts = []
        for q in range(4):
            total = None
            for k in range(4):
                tile = jnp.where(runs_lane[0:8] < 32, buf[4 * q + k], 0.0)
                tile = pltpu.roll(tile, 32 * k, 1) if k else tile
                total = tile if total is None else total + tile
            parts.append(total)
        wide[row] = jnp.concatenate(parts, axis=1)
        for off in range(1, ROWS):
            remote(
                wide.at[row], wide.at[row], g_send.at[2 * slot + 1], g_recv.at[2 * slot + 1], (row_peer(off), col)
            ).start()

    gather_cols(0, g1)

    loaded("dzt", "bzt", ("mult", 0), ("aux", 0), "force")
    for c, comp in enumerate(XCOMP):
        rhs[c] = (force[c] + along_x(shifted(comp))).reshape(256, NX)
    fluid[...] = jnp.zeros_like(fluid)
    for c, comp in enumerate(ZCOMP):
        own = shifted(comp).reshape(256, NX)
        rhs[c] += exact_left(dzt[...], own, 2) * (1.0 / 12.0)
    gather_rows(0, g1, g2)
    for copy in stress_halos:
        copy.wait_recv()
    for c in range(3):
        along_y = centered(yext[c, 0:16], yext[c, 1:17], yext[c, 3:19], yext[c, 4:20]).reshape(256, NX)
        edge = exact_left(bzt[...], zh[c].reshape(64, NX), 2) * (1.0 / 12.0)
        high, low = split(rhs[c] + along_y + edge, 2)
        rpieces[0, c] = high
        rpieces[1, c] = low

    def send_rows(stage, j, src, dst):
        dst[j, row] = src[j, row]
        for off in range(1, ROWS):
            peer = row_peer(off)
            remote(src.at[j, peer], dst.at[j, row], a_send.at[stage, j], a_recv.at[stage, j], (peer, col)).start()

    def send_cols(stage, j, src, dst):
        dst[j, col] = src[j, col]
        for dy, dz in FAR:
            peer = 4 * lax.rem(col // 4 + dz, 4) + lax.rem(col % 4 + dy, 4)
            remote(src.at[j, peer], dst.at[j, col], a_send.at[stage, j], a_recv.at[stage, j], (row, peer)).start()

    def await_all(stage, j, dst, count):
        wait_for(dst.at[j, pl.ds(0, count - 1)], a_recv.at[stage, j])

    def x_forward(j):
        for c in range(3):
            out = product([tf[0, j], tf[1, j]], [rpieces[0, c], rpieces[1, c]], NT)
            x1[j, :, c] = out.reshape(ROWS, 2 * MC, 256)
        send_rows(0, j, x1, r1)

    def y_forward(j):
        await_all(0, j, r1, ROWS)
        for c in range(3):
            xs = [(r1[j, s, c, 0:MC], r1[j, s, c, MC : 2 * MC]) for s in range(8)]
            for k, (re, im) in enumerate(fft(xs, -1)):
                cos, sin = twy[0, k : k + 1], twy[1, k : k + 1]
                at = k * 3 * MC + c * MC
                ascr[at : at + MC, 0:256] = re * cos + im * sin
                ascr[at : at + MC, 256:512] = im * cos - re * sin
        out = product(split(ascr[...], 2), [kyf[0], kyf[1]]).reshape(8, 3, MC, 512)
        for half in range(2):
            for part in range(2):
                at = 256 * part + 128 * half
                y1[j, pl.ds(half, 8, 2), :, part] = out[:, :, :, at : at + 128]
        send_cols(1, j, y1, r2)

    def solve(j):
        await_all(1, j, r2, COLS)
        for c in range(3):
            xs = [(r2[j, s, c, 0], r2[j, s, c, 1]) for s in range(16)]
            for k, (re, im) in enumerate(fft(xs, -1)):
                cos, sin = twz[0, k : k + 1], twz[1, k : k + 1]
                at = k * 3 * MC + c * MC
                bscr[at : at + MC, 0:128] = re * cos + im * sin
                bscr[at : at + MC, 128:256] = im * cos - re * sin
        bscr[...] = product(split(bscr[...], 2), [kzf[0], kzf[1]])
        mode = row * 32 + j * MC + lax.broadcasted_iota(jnp.int32, (MC, 128), 0)
        lanes = lax.broadcasted_iota(jnp.int32, (MC, 128), 1)
        wave_x = mode.astype(F32) * (2.0 * math.pi / NX)
        index_y = col // 2 + 8 * (8 * lax.rem(col, 2) + lanes // 16)
        wave_y = jnp.where(index_y < NY // 2, index_y, index_y - NY).astype(F32) * (2.0 * math.pi / NY)
        keep_y = (index_y != NY // 2).astype(F32)
        for k in range(16):
            index_z = k + 16 * (lanes % 16)
            wave_z = jnp.where(index_z < NZ // 2, index_z, index_z - NZ).astype(F32) * (2.0 * math.pi / NZ)
            keep = keep_y * (index_z != NZ // 2).astype(F32)
            ksq = wave_x * wave_x + wave_y * wave_y + wave_z * wave_z
            inverse = 1.0 / jnp.where(ksq > 0, ksq, 1.0)
            gain = keep / (MASS + VISC * ksq)
            for part in range(2):
                at = 3 * MC * k
                lane = slice(128 * part, 128 * part + 128)
                fx, fy, fz = (bscr[at + MC * c : at + MC * c + MC, lane] for c in range(3))
                dotk = (wave_x * fx + wave_y * fy + wave_z * fz) * inverse
                bscr[at : at + MC, lane] = (fx - wave_x * dotk) * gain
                bscr[at + MC : at + 2 * MC, lane] = (fy - wave_y * dotk) * gain
                bscr[at + 2 * MC : at + 3 * MC, lane] = (fz - wave_z * dotk) * gain
        bscr[...] = product(split(bscr[...], INV), [kzi[p] for p in range(INV)])
        for c in range(3):
            xs = []
            for k in range(16):
                cos, sin = twz[0, k : k + 1], twz[1, k : k + 1]
                at = k * 3 * MC + c * MC
                re, im = bscr[at : at + MC, 0:128], bscr[at : at + MC, 128:256]
                xs.append((re * cos - im * sin, im * cos + re * sin))
            for s, (re, im) in enumerate(fft(xs, 1)):
                z1[j, s, c, 0] = re
                z1[j, s, c, 1] = im
        send_cols(2, j, z1, r3)

    def y_inverse(j):
        await_all(2, j, r3, COLS)
        for half in range(2):
            for part in range(2):
                at = 256 * part + 128 * half
                ascr[:, at : at + 128] = r3[j, pl.ds(half, 8, 2), :, part].reshape(8 * 3 * MC, 128)
        ascr[...] = product(split(ascr[...], INV), [kyi[p] for p in range(INV)])
        for c in range(3):
            xs = []
            for k in range(8):
                cos, sin = twy[0, k : k + 1], twy[1, k : k + 1]
                at = k * 3 * MC + c * MC
                re, im = ascr[at : at + MC, 0:256], ascr[at : at + MC, 256:512]
                xs.append((re * cos - im * sin, im * cos + re * sin))
            for s, (re, im) in enumerate(fft(xs, 1)):
                y2[j, s, c, 0:MC] = re
                y2[j, s, c, MC : 2 * MC] = im
        send_rows(3, j, y2, r4)

    def x_inverse(j):
        await_all(3, j, r4, ROWS)
        for c in range(3):
            spectrum = jnp.transpose(r4[j, :, c].reshape(2 * MC * ROWS, 256))
            out = product(split(spectrum, INV), [ti[p, j] for p in range(INV)])
            fluid[c] += out.reshape(16, 16, NX)

    def tile_copies():
        peers = ((row, col_peer(1)), (row, col_peer(COLS - 1)), (row_peer(1), col), (row_peer(ROWS - 1), col))
        return [
            remote(gtile.at[2], nbtile.at[k], halo_send.at[8 + k], halo_recv.at[8 + k], peer)
            for k, peer in enumerate(peers)
        ]

    def neighbours():
        for copy in tile_copies():
            copy.wait_recv()
        for k in range(4):
            tile = nbtile[k]
            nbcol[k] = dot_exact((pair == runs_lane).astype(F32), tile, NT)
            ids = dot_exact(spread_runs[0:32], tile, NT)[:, 5:6] * 0.25
            for r in range(ROWS):
                match[r, 32 + 32 * k : 64 + 32 * k] = (ids == g2[r, 0:1]).astype(F32)
            line, block = tile[3:4], tile[4:5]
            y = jnp.floor(line * (1.0 / 16.0))
            z = line - 16.0 * y
            layer, along = (z, y) if k < 2 else (y, z)
            layer = layer - (14.0 if k % 2 == 0 else 0.0)
            inside = (layer >= 0.0) & (layer <= 1.0)
            target = jnp.where(inside, block * 32.0 + layer * 16.0 + along, -1.0)
            hits = (target == pair.astype(F32)).astype(F32)
            nbhot[k] = hits.astype(BF16)
            nbkeep[k] = jnp.broadcast_to(1.0 - jnp.sum(hits, axis=1, keepdims=True), (128, 128))

    def rigid_of(sums, cols):
        sums = dot_exact(gather_runs[:, 0:32], sums)
        rx, ry, rz, mean, turn = (cols[:, k : k + 1] for k in (0, 1, 2, 6, 7))
        vx, vy, vz = (sums[:, k : k + 1] * mean for k in range(3))
        wx, wy, wz = (sums[:, k : k + 1] * turn for k in range(3, 6))
        cell_x = rx + (lane128.astype(F32) - 63.5)
        return (
            jnp.broadcast_to(vx + wy * rz - wz * ry, (128, 128)),
            vy + wz * cell_x - wx * rz,
            vz + wx * ry - wy * cell_x,
        )

    def geometry():
        wait_for(g2.at[pl.ds(0, ROWS - 1)], g_recv.at[1])
        own = dot_exact(spread_runs[0:32], fields, NT) * 0.25
        ids = own[:, 0:1]
        count = jnp.zeros((32, 1), F32)
        cx, cy, cz = count, count, count
        for r in range(ROWS):
            block = g2[r]
            same = (ids == block[0:1]).astype(F32)
            match[r, 0:32] = same
            count += jnp.sum(same, axis=1, keepdims=True)
            cx += jnp.sum(same * block[1:2], axis=1, keepdims=True)
            cy += jnp.sum(same * block[2:3], axis=1, keepdims=True)
            cz += jnp.sum(same * block[3:4], axis=1, keepdims=True)
        safe = jnp.maximum(count, 1.0)
        cx, cy, cz = cx / safe, cy / safe, cz / safe
        spread = jnp.zeros((32, 1), F32)
        for r in range(ROWS):
            block = g2[r]
            dx, dy, dz = block[1:2] - cx, block[2:3] - cy, block[3:4] - cz
            inner_spread = block[4:5] + 512.0 * (dx * dx + dy * dy + dz * dz)
            spread += jnp.sum(match[r, 0:32] * inner_spread, axis=1, keepdims=True)
        inertia = jnp.maximum(spread * (2.0 / 3.0), 1.0)
        place = lane128
        packed = jnp.where(place == 0, 1.0 / jnp.maximum(512.0 * count, 1.0), 0.0)
        for at, value in ((1, cx), (2, cy), (3, cz), (4, 1.0 / inertia)):
            packed = jnp.where(place == at, value, packed)
        mine = dot_exact((pair == runs_lane).astype(F32), fields, NT)
        centers = dot_exact(gather_runs[:, 0:32], packed)
        rel = jnp.where(place == 0, mine[:, 1:2] + 63.5 - centers[:, 1:2], 0.0)
        rel = jnp.where(place == 1, mine[:, 2:3] - centers[:, 2:3], rel)
        rel = jnp.where(place == 2, mine[:, 3:4] - centers[:, 3:4], rel)
        for at, value in enumerate((mine[:, 6:7], mine[:, 7:8], mine[:, 0:1], centers[:, 0:1], centers[:, 4:5])):
            rel = jnp.where(place == 3 + at, value, rel)
        mgeo[...] = rel
        gtile[2] = jnp.transpose(rel)[0:8]
        for copy in tile_copies():
            copy.start()
        rows256 = lax.broadcasted_iota(jnp.int32, (256, 128), 0).astype(F32)
        cols256 = lax.broadcasted_iota(jnp.int32, (128, 256), 1).astype(F32)
        for b in range(4):
            hot[b] = ((fields[6:7] == rows256) & (fields[7:8] == float(b))).astype(F32).astype(BF16)
            hott[b] = ((mine[:, 6:7] == cols256) & (mine[:, 7:8] == float(b))).astype(F32).astype(BF16)

    loaded("tf")
    x_forward(0)
    x_forward(1)
    geometry()
    loaded("twy", "kyf", "twz", "kzf", "kzi", "kyi", "ti")

    @pl.loop(0, CHUNKS + 5)
    def _(t):
        pl.when(t < CHUNKS)(lambda: y_forward(t))
        pl.when(t + 2 < CHUNKS)(lambda: x_forward(t + 2))
        pl.when(t == 3)(neighbours)
        pl.when((t >= 2) & (t < CHUNKS + 2))(lambda: solve(t - 2))
        pl.when((t >= 4) & (t < CHUNKS + 4))(lambda: y_inverse(t - 4))
        pl.when(t >= 5)(lambda: x_inverse(t - 5))

    for copy in stress_halos:
        copy.wait_send()
    for c in range(3):
        for layer, z in enumerate((0, 1, 14, 15)):
            zf[c, layer] = fluid[c, :, z, :]
    velocity_halos = halo_copies(4, fluid, 14, 0, vext, zf, vzh)
    for copy in velocity_halos:
        copy.start()

    inside = lane128.astype(F32) - 63.5
    blocks = []
    firsts, seconds = [], []
    for c in range(3):
        block = jnp.zeros((128, 128), F32)
        for b in range(4):
            block += exact_left(hott[b], fluid[c, :, :, 128 * b : 128 * b + 128].reshape(256, 128), 3)
        blocks.append(block)
        firsts.append(jnp.sum(block, axis=1, keepdims=True))
        seconds.append(jnp.sum(block * inside, axis=1, keepdims=True))
    rx, ry, rz = mgeo[:, 0:1], mgeo[:, 1:2], mgeo[:, 2:3]
    moments = jnp.zeros((128, 128), F32)
    for at, value in enumerate(
        (
            firsts[0],
            firsts[1],
            firsts[2],
            ry * firsts[2] - rz * firsts[1],
            rz * firsts[0] - (rx * firsts[2] + seconds[2]),
            rx * firsts[1] + seconds[1] - ry * firsts[0],
        )
    ):
        moments = jnp.where(lane128 == at, value, moments)
    gtile[1] = dot_exact(jnp.transpose(moments)[0:8], gather_runs)
    gather_cols(1, g3)
    gather_rows(1, g3, g4)
    wait_for(g4.at[pl.ds(0, ROWS - 1)], g_recv.at[3])
    totals = jnp.zeros((160, 8), F32)
    for r in range(ROWS):
        totals += dot_exact(match[r], g4[r], NT)
    rigid = rigid_of(totals[0:32], mgeo)
    for c in range(3):
        fix = rigid[c] - blocks[c]
        for b in range(4):
            lanes = slice(128 * b, 128 * b + 128)
            done = fluid[c, :, :, lanes] + exact_left(hot[b], fix, 3).reshape(16, 16, 128)
            vext[c, 2:18, :, lanes] = done
    stores = [pltpu.make_async_copy(vext.at[c, 2:18], vext_out.at[c, 2:18], store_sem.at[c]) for c in range(3)]
    for store in stores:
        store.start()
    for copy in velocity_halos:
        copy.wait_recv()
    for k in range(4):
        rigid = rigid_of(totals[32 + 32 * k : 64 + 32 * k], nbcol[k])
        fix = exact_left(nbhot[k], jnp.concatenate(rigid, axis=1), 3)
        keep = nbkeep[k]
        ref, first = ((vzh, 0), (vzh, 2), (vext, 0), (vext, 18))[k]
        for c in range(3):
            for b in range(4):
                lanes, rows = slice(128 * b, 128 * b + 128), slice(32 * b, 32 * b + 32)
                old = ref[c, first : first + 2, :, lanes].reshape(32, 128)
                new = old * keep[rows] + fix[rows, 128 * c : 128 * c + 128]
                ref[c, first : first + 2, :, lanes] = new.reshape(2, 16, 128)
    late = [
        pltpu.make_async_copy(vext.at[:, 0:2], vext_out.at[:, 0:2], store_sem.at[3]),
        pltpu.make_async_copy(vext.at[:, 18:20], vext_out.at[:, 18:20], store_sem.at[4]),
        pltpu.make_async_copy(vzh, vzh_out, store_sem.at[5]),
    ]
    for store in late:
        store.start()
    stores += late

    for copy in velocity_halos + tile_copies():
        copy.wait_send()
    wait_for(g1.at[pl.ds(0, COLS - 1)], g_send.at[0])
    wait_for(g2.at[pl.ds(0, ROWS - 1)], g_send.at[1])
    wait_for(g3.at[pl.ds(0, COLS - 1)], g_send.at[2])
    wait_for(g4.at[pl.ds(0, ROWS - 1)], g_send.at[3])

    @pl.loop(0, CHUNKS)
    def _(j):
        wait_for(x1.at[j, pl.ds(0, ROWS - 1)], a_send.at[0, j])
        wait_for(y1.at[j, pl.ds(0, COLS - 1)], a_send.at[1, j])
        wait_for(z1.at[j, pl.ds(0, COLS - 1)], a_send.at[2, j])
        wait_for(y2.at[j, pl.ds(0, ROWS - 1)], a_send.at[3, j])

    for store in stores:
        store.wait()


def update(vlow, vhigh, vzh, mult, dzt, bzt, vel, new_aux, new_mult, *, lines):
    rows = 16 * lines
    edge = bzt[...]
    grads = []
    for c in range(3):
        both = jnp.concatenate([vlow[c], vhigh[c]], axis=0)
        field = both[2 : lines + 2]
        vel[c] = field
        dx = along_x(field.reshape(rows, NX))
        near = [both[k : lines + k].reshape(rows, NX) for k in (0, 1, 3, 4)]
        dy = centered(*near)
        dz = exact_left(dzt[...], field.reshape(rows, NX), 3) + exact_left(edge, vzh[c], 3)
        grads.append((dx, dy, dz * (1.0 / 12.0)))
    strain = (
        grads[0][0],
        grads[1][1],
        grads[2][2],
        (grads[0][1] + grads[1][0]) * 0.5,
        (grads[0][2] + grads[2][0]) * 0.5,
        (grads[1][2] + grads[2][1]) * 0.5,
    )
    old = [mult[k].reshape(rows, NX) for k in range(6)]
    q = [old[k] + PEN * strain[k] for k in range(6)]
    norm = jnp.sqrt(
        q[0] * q[0] + q[1] * q[1] + q[2] * q[2] + 2.0 * (q[3] * q[3] + q[4] * q[4] + q[5] * q[5])
    )
    factor = 1.0 - YIELD / jnp.maximum(norm, YIELD)
    for k in range(6):
        aux = factor * q[k] * (1.0 / PEN)
        new_aux[k] = aux.reshape(lines, 16, NX)
        new_mult[k] = (old[k] + PEN * (strain[k] - aux)).reshape(lines, 16, NX)


def local(force, mult, aux, entry_lines, entry_owner, entry_slot):
    t = make_tables()
    vm = pl.BlockSpec(memory_space=pltpu.VMEM)
    hbm = pl.BlockSpec(memory_space=pltpu.HBM)
    sems = pltpu.SemaphoreType.DMA
    names = ("tf", "ti", "kyf", "kyi", "kzf", "kzi", "twy", "twz", "dz", "bz")
    loads = [force, mult, aux] + [jnp.asarray(t[k]) for k in names]
    scratch = [pltpu.VMEM(a.shape, a.dtype) for a in loads] + [
        pltpu.VMEM((3, 20, 16, NX), F32),
        pltpu.VMEM((3, 4, 16, NX), F32),
        pltpu.VMEM((3, 4, 16, NX), F32),
        pltpu.VMEM((3, 20, 16, NX), F32),
        pltpu.VMEM((3, 4, 16, NX), F32),
        pltpu.VMEM((3, 256, NX), F32),
        pltpu.VMEM((2, 3, 256, NX), BF16),
        pltpu.VMEM((3, 16, 16, NX), F32),
        pltpu.VMEM((CHUNKS, ROWS, 3, 2 * MC, 256), F32),
        pltpu.VMEM((CHUNKS, ROWS, 3, 2 * MC, 256), F32),
        pltpu.VMEM((CHUNKS, COLS, 3, 2, MC, 128), F32),
        pltpu.VMEM((CHUNKS, COLS, 3, 2, MC, 128), F32),
        pltpu.VMEM((CHUNKS, COLS, 3, 2, MC, 128), F32),
        pltpu.VMEM((CHUNKS, COLS, 3, 2, MC, 128), F32),
        pltpu.VMEM((CHUNKS, ROWS, 3, 2 * MC, 256), F32),
        pltpu.VMEM((CHUNKS, ROWS, 3, 2 * MC, 256), F32),
        pltpu.VMEM((24 * MC, 512), F32),
        pltpu.VMEM((48 * MC, 256), F32),
        pltpu.VMEM((COLS, 8, 128), F32),
        pltpu.VMEM((ROWS, 8, 512), F32),
        pltpu.VMEM((COLS, 8, 128), F32),
        pltpu.VMEM((ROWS, 8, 512), F32),
        pltpu.VMEM((3, 8, 128), F32),
        pltpu.VMEM((ROWS, 160, 512), F32),
        pltpu.VMEM((128, 128), F32),
        pltpu.VMEM((4, 256, 128), BF16),
        pltpu.VMEM((4, 128, 256), BF16),
        pltpu.VMEM((4, 8, 128), F32),
        pltpu.VMEM((4, 128, 8), F32),
        pltpu.VMEM((4, 128, 128), BF16),
        pltpu.VMEM((4, 128, 128), F32),
        sems((12,)),
        sems((12,)),
        sems((4, CHUNKS)),
        sems((4, CHUNKS)),
        sems((4,)),
        sems((4,)),
        sems((len(names) + 13,)),
        sems((6,)),
    ]
    vext, vzh = pl.pallas_call(
        kernel,
        out_shape=(
            jax.ShapeDtypeStruct((3, 20, 16, NX), F32),
            jax.ShapeDtypeStruct((3, 4, 16, NX), F32),
        ),
        in_specs=[hbm] * 3 + [vm] * 3 + [hbm] * len(names),
        out_specs=(hbm, hbm),
        scratch_shapes=scratch,
        compiler_params=pltpu.CompilerParams(
            collective_id=0, has_side_effects=True, vmem_limit_bytes=58 * 2**20
        ),
    )(
        force,
        mult,
        aux,
        entry_lines.reshape(1, 128),
        entry_owner.reshape(1, 128),
        entry_slot.reshape(1, 128),
        *loads[3:],
    )

    lines = 4
    whole = lambda *shape: pl.BlockSpec(shape, lambda i: (0,) * len(shape))
    part = lambda n: pl.BlockSpec((n, lines, 16, NX), lambda i: (0, i, 0, 0))
    return tuple(
        pl.pallas_call(
            functools.partial(update, lines=lines),
            grid=(16 // lines,),
            out_shape=tuple(jax.ShapeDtypeStruct((n, 16, 16, NX), F32) for n in (3, 6, 6)),
            in_specs=[
                part(3),
                pl.BlockSpec((3, lines, 16, NX), lambda i: (0, i + 1, 0, 0)),
                whole(3, 64, NX),
                part(6),
                whole(16 * lines, 16 * lines),
                pl.BlockSpec((16 * lines, 64), lambda i: (i, 0)),
            ],
            out_specs=tuple(part(n) for n in (3, 6, 6)),
            compiler_params=pltpu.CompilerParams(vmem_limit_bytes=58 * 2**20),
        )(
            vext,
            vext,
            vzh.reshape(3, 64, NX),
            mult,
            jnp.asarray(deriv_rows(lines).astype(jnp.bfloat16)),
            jnp.asarray(t["bz"]),
        )
    )


def solution(mesh):
    field = P(None, "row", "col", None)
    return jax.shard_map(
        local,
        mesh=mesh,
        in_specs=(field, field, field, P(("row", "col")), P(("row", "col"), None), P(("row", "col"))),
        out_specs=(field, field, field),
        check_vma=False,
    )
```

```python
import functools
import math

import jax
import jax.numpy as jnp
import numpy as np
from jax import lax
from jax.experimental import pallas as pl
from jax.experimental.pallas import tpu as pltpu
from jax.sharding import PartitionSpec as P

MASS, VISC, PEN, YIELD = 0.02, 10.0, 5.0, 2.0
NPD = 72
NX, NY, NZ = 512, 128, 256
ROWS, COLS = 8, 16
CHUNKS = 4
MC = 32 // CHUNKS
F32, BF16 = jnp.float32, jnp.bfloat16
MESH = pl.DeviceIdType.MESH
HIGHEST = lax.Precision.HIGHEST
NN = (((1,), (0,)), ((), ()))
NT = (((1,), (1,)), ((), ()))

FAR = (
    (2, 2), (2, 1), (1, 2), (2, 3), (3, 2), (1, 1), (3, 3), (1, 3), (3, 1),
    (2, 0), (0, 2), (1, 0), (0, 1), (3, 0), (0, 3),
)

YCOMP = (3, 1, 5)
ZCOMP = (4, 5, 2)
XCOMP = (0, 3, 4)


def pieces_np(table, count):
    out = []
    rest = np.asarray(table, np.float64)
    for _ in range(count):
        piece = rest.astype(jnp.bfloat16)
        out.append(piece)
        rest = rest - piece.astype(np.float64)
    return np.stack(out)


def kron_dft(points, batch, sign):
    index = np.arange(points)
    angle = sign * 2 * np.pi * (np.outer(index, index) % points) / points
    eye = np.eye(batch)
    cos, sin = np.kron(np.cos(angle), eye), np.kron(np.sin(angle), eye)
    return np.block([[cos, sin], [-sin, cos]])


def kron_dft_z(sign):
    index = np.arange(16)
    angle = sign * 2 * np.pi * (np.outer(index, index) % 16) / 16
    eye = np.eye(8)
    cos, sin = np.kron(eye, np.cos(angle)), np.kron(eye, np.sin(angle))
    return np.block([[cos, sin], [-sin, cos]])


def mode_table():
    chunk, dest, part, inner = np.meshgrid(
        np.arange(CHUNKS), np.arange(ROWS), np.arange(2), np.arange(MC), indexing="ij"
    )
    mode = 32 * dest + MC * chunk + inner
    return mode.reshape(CHUNKS, -1), part.reshape(CHUNKS, -1)


def make_tables():
    mode, part = mode_table()
    x = np.arange(NX)
    angle = 2 * np.pi * ((mode[..., None] * x) % NX) / NX
    fwd = np.where(part[..., None] == 0, np.cos(angle), -np.sin(angle))
    weight = np.where(mode == 0, 1.0, 2.0)[..., None] / float(NX * NY * NZ)
    inv = weight * fwd
    ky_f = pieces_np(kron_dft(16, 16, -1), 2)
    ky_i = pieces_np(kron_dft(16, 16, 1), INV)
    kz_f = pieces_np(kron_dft_z(-1), 2)
    kz_i = pieces_np(kron_dft_z(1), INV)
    lane = np.arange(256)
    turn_y = 2 * np.pi * np.outer(np.arange(8), lane // 16) / NY
    turn_z = 2 * np.pi * np.outer(np.arange(16), np.arange(128) % 16) / NZ
    two_y = np.stack([np.cos(turn_y), np.sin(turn_y)]).astype(np.float32)
    two_z = np.stack([np.cos(turn_z), np.sin(turn_z)]).astype(np.float32)
    return {
        "tf": pieces_np(fwd, 2),
        "ti": pieces_np(inv, INV),
        "kyf": ky_f,
        "kyi": ky_i,
        "kzf": kz_f,
        "kzi": kz_i,
        "twy": two_y,
        "twz": two_z,
        "dz": deriv_rows(16).astype(jnp.bfloat16),
        "bz": deriv_halo().astype(jnp.bfloat16),
    }


INV = 3


def deriv_rows(lines):
    one = np.zeros((16, 16))
    for offset, coef in ((1, 8), (-1, -8), (2, -1), (-2, 1)):
        one += coef * np.eye(16, k=offset)
    return np.kron(np.eye(lines), one)


def deriv_halo():
    out = np.zeros((16, 16, 4, 16))
    for y in range(16):
        for layer, place in enumerate((-2, -1, 16, 17)):
            for z in range(16):
                out[y, z, layer, y] = {1: 8, -1: -8, 2: -1, -2: 1}.get(place - z, 0)
    return out.reshape(256, 64)


def split(value, count):
    out = []
    for step in range(count):
        piece = value.astype(BF16)
        out.append(piece)
        if step + 1 < count:
            value = value - piece.astype(F32)
    return out


def dot(a, b, dims=NN):
    return lax.dot_general(a, b, dims, preferred_element_type=F32)


def dot_exact(a, b, dims=NN):
    return lax.dot_general(a, b, dims, precision=HIGHEST, preferred_element_type=F32)


def product(a, b, dims=NN):
    count = len(a)
    total = None
    for i in range(count - 1, -1, -1):
        for j in range(count - 1 - i, -1, -1):
            term = dot(a[i], b[j], dims)
            total = term if total is None else total + term
    return total


def exact_left(a, value, count):
    total = None
    for piece in reversed(split(value, count)):
        term = dot(a, piece)
        total = term if total is None else total + term
    return total


def fft(xs, sign):
    count = len(xs)
    if count == 1:
        return xs
    even, odd = fft(xs[0::2], sign), fft(xs[1::2], sign)
    out = [None] * count
    half = count // 2
    for k in range(half):
        re, im = odd[k]
        if k == 0:
            tr, ti = re, im
        elif 4 * k == count:
            tr, ti = (-im, re) if sign > 0 else (im, -re)
        else:
            c = math.cos(2 * math.pi * k / count)
            s = sign * math.sin(2 * math.pi * k / count)
            tr, ti = re * c - im * s, re * s + im * c
        er, ei = even[k]
        out[k] = (er + tr, ei + ti)
        out[k + half] = (er - tr, ei - ti)
    return out


def along_x(field):
    axis = field.ndim - 1
    up1, up2 = pltpu.roll(field, NX - 1, axis), pltpu.roll(field, NX - 2, axis)
    lo1, lo2 = pltpu.roll(field, 1, axis), pltpu.roll(field, 2, axis)
    return (8.0 * (up1 - lo1) - (up2 - lo2)) * (1.0 / 12.0)


def centered(lo2, lo1, up1, up2):
    return (8.0 * (up1 - lo1) - (up2 - lo2)) * (1.0 / 12.0)


def kernel(
    force_in, mult_in, aux_in, lines_in, owner_in, slot_in,
    tf_in, ti_in, kyf_in, kyi_in, kzf_in, kzi_in, twy_in, twz_in, dzt_in, bzt_in,
    vext_out, vzh_out,
    force, mult, aux, tf, ti, kyf, kyi, kzf, kzi, twy, twz, dzt, bzt,
    yext, zf, zh, vext, vzh, rhs, rpieces, fluid,
    x1, r1, y1, r2, z1, r3, y2, r4, ascr, bscr,
    g1, g2, g3, g4, gtile, match, mgeo, hot, hott, nbtile, nbcol, nbhot, nbkeep,
    halo_send, halo_recv, a_send, a_recv, g_send, g_recv, load_sem, store_sem,
):
    row, col = lax.axis_index("row"), lax.axis_index("col")

    def row_peer(off):
        return lax.rem(row + off, ROWS)

    def col_peer(off):
        return lax.rem(col + off, COLS)

    def remote(src, dst, send, recv, device):
        return pltpu.make_async_remote_copy(
            src_ref=src, dst_ref=dst, send_sem=send, recv_sem=recv,
            device_id=device, device_id_type=MESH,
        )

    def wait_for(ref, sem):
        pltpu.make_async_copy(ref, ref, sem).wait()

    loads = {}

    def load(name, src, dst):
        loads[name] = pltpu.make_async_copy(src, dst, load_sem.at[len(loads)])
        loads[name].start()

    for comp in (4, 5, 2, 3, 1):
        load(("mult", comp), mult_in.at[comp], mult.at[comp])
        load(("aux", comp), aux_in.at[comp], aux.at[comp])
    load("dzt", dzt_in, dzt)
    load("bzt", bzt_in, bzt)
    load(("mult", 0), mult_in.at[0], mult.at[0])
    load(("aux", 0), aux_in.at[0], aux.at[0])
    load("force", force_in, force)
    for name, src, dst in (
        ("tf", tf_in, tf), ("twy", twy_in, twy), ("kyf", kyf_in, kyf), ("twz", twz_in, twz),
        ("kzf", kzf_in, kzf), ("kzi", kzi_in, kzi), ("kyi", kyi_in, kyi), ("ti", ti_in, ti),
    ):
        load(name, src, dst)

    def loaded(*names):
        for name in names:
            loads.pop(name).wait()

    barrier = pltpu.get_barrier_semaphore()
    for off in range(1, ROWS):
        pl.semaphore_signal(barrier, inc=1, device_id=(row_peer(off), col), device_id_type=MESH)
    for off in range(1, COLS):
        pl.semaphore_signal(barrier, inc=1, device_id=(row, col_peer(off)), device_id_type=MESH)

    def shifted(comp):
        return mult[comp] - PEN * aux[comp]

    for i, comp in enumerate(ZCOMP):
        loaded(("mult", comp), ("aux", comp))
        for layer, z in enumerate((0, 1, 14, 15)):
            zf[i, layer] = mult[comp, :, z, :] - PEN * aux[comp, :, z, :]
    pl.semaphore_wait(barrier, ROWS + COLS - 2)

    def halo_copies(base, ysrc, high, low, ydst, zsrc, zdst):
        up, down = (row_peer(1), col), (row_peer(ROWS - 1), col)
        right, left = (row, col_peer(1)), (row, col_peer(COLS - 1))
        sems = [(halo_send.at[base + k], halo_recv.at[base + k]) for k in range(4)]
        return [
            remote(zsrc.at[:, 2:4], zdst.at[:, 0:2], *sems[0], right),
            remote(zsrc.at[:, 0:2], zdst.at[:, 2:4], *sems[1], left),
            remote(ysrc.at[:, high : high + 2], ydst.at[:, 0:2], *sems[2], up),
            remote(ysrc.at[:, low : low + 2], ydst.at[:, 18:20], *sems[3], down),
        ]

    stress_halos = halo_copies(0, yext, 16, 2, yext, zf, zh)
    for copy in stress_halos[0:2]:
        copy.start()
    for i, comp in enumerate(YCOMP):
        if comp != 5:
            loaded(("mult", comp), ("aux", comp))
        yext[i, 2:18] = shifted(comp)
    for copy in stress_halos[2:4]:
        copy.start()

    lane128 = lax.broadcasted_iota(jnp.int32, (1, 128), 1)
    lines, block_x = lines_in[...], lines_in[...] & 3
    particle = owner_in[...] * NPD + slot_in[...]
    gy = ((lines >> 6) + row * 16).astype(F32)
    gz = (((lines >> 2) & 15) + col * 16).astype(F32)
    fields = jnp.concatenate(
        [
            particle.astype(F32),
            (block_x * 128).astype(F32),
            gy,
            gz,
            gy * gy,
            gz * gz,
            (lines >> 2).astype(F32),
            block_x.astype(F32),
        ],
        axis=0,
    )
    pair = lax.broadcasted_iota(jnp.int32, (128, 128), 0)
    runs_lane = lax.broadcasted_iota(jnp.int32, (128, 128), 1)
    gather_runs = (pair // 4 == runs_lane).astype(F32)
    spread_runs = (runs_lane // 4 == pair).astype(F32)
    sums = dot_exact(fields, gather_runs)
    mean_y, mean_z = sums[2:3] * 0.25, sums[3:4] * 0.25
    inner = 4.0 * 174752.0 + 128.0 * (
        sums[4:5] - 4.0 * mean_y * mean_y + sums[5:6] - 4.0 * mean_z * mean_z
    )
    gtile[0] = jnp.concatenate(
        [sums[0:1] * 0.25, sums[1:2] * 0.25 + 63.5, mean_y, mean_z, inner, jnp.zeros((3, 128), F32)], axis=0
    )

    def gather_cols(slot, buf):
        buf[col] = gtile[slot]
        for off in range(1, COLS):
            remote(
                gtile.at[slot], buf.at[col], g_send.at[2 * slot], g_recv.at[2 * slot], (row, col_peer(off))
            ).start()

    def gather_rows(slot, buf, wide):
        wait_for(buf.at[pl.ds(0, COLS - 1)], g_recv.at[2 * slot])
        parts = []
        for q in range(4):
            total = None
            for k in range(4):
                tile = jnp.where(runs_lane[0:8] < 32, buf[4 * q + k], 0.0)
                tile = pltpu.roll(tile, 32 * k, 1) if k else tile
                total = tile if total is None else total + tile
            parts.append(total)
        wide[row] = jnp.concatenate(parts, axis=1)
        for off in range(1, ROWS):
            remote(
                wide.at[row], wide.at[row], g_send.at[2 * slot + 1], g_recv.at[2 * slot + 1], (row_peer(off), col)
            ).start()

    gather_cols(0, g1)

    loaded("dzt", "bzt", ("mult", 0), ("aux", 0), "force")
    for c, comp in enumerate(XCOMP):
        rhs[c] = (force[c] + along_x(shifted(comp))).reshape(256, NX)
    fluid[...] = jnp.zeros_like(fluid)
    for c, comp in enumerate(ZCOMP):
        own = shifted(comp).reshape(256, NX)
        rhs[c] += exact_left(dzt[...], own, 2) * (1.0 / 12.0)
    gather_rows(0, g1, g2)
    for copy in stress_halos:
        copy.wait_recv()
    for c in range(3):
        along_y = centered(yext[c, 0:16], yext[c, 1:17], yext[c, 3:19], yext[c, 4:20]).reshape(256, NX)
        edge = exact_left(bzt[...], zh[c].reshape(64, NX), 2) * (1.0 / 12.0)
        high, low = split(rhs[c] + along_y + edge, 2)
        rpieces[0, c] = high
        rpieces[1, c] = low

    def send_rows(stage, j, src, dst):
        dst[j, row] = src[j, row]
        for off in range(1, ROWS):
            peer = row_peer(off)
            remote(src.at[j, peer], dst.at[j, row], a_send.at[stage, j], a_recv.at[stage, j], (peer, col)).start()

    def send_cols(stage, j, src, dst):
        dst[j, col] = src[j, col]
        for dy, dz in FAR:
            peer = 4 * lax.rem(col // 4 + dz, 4) + lax.rem(col % 4 + dy, 4)
            remote(src.at[j, peer], dst.at[j, col], a_send.at[stage, j], a_recv.at[stage, j], (row, peer)).start()

    def await_all(stage, j, dst, count):
        wait_for(dst.at[j, pl.ds(0, count - 1)], a_recv.at[stage, j])

    def x_forward(j):
        for c in range(3):
            out = product([tf[0, j], tf[1, j]], [rpieces[0, c], rpieces[1, c]], NT)
            x1[j, :, c] = out.reshape(ROWS, 2 * MC, 256)
        send_rows(0, j, x1, r1)

    def y_forward(j):
        await_all(0, j, r1, ROWS)
        for c in range(3):
            xs = [(r1[j, s, c, 0:MC], r1[j, s, c, MC : 2 * MC]) for s in range(8)]
            for k, (re, im) in enumerate(fft(xs, -1)):
                cos, sin = twy[0, k : k + 1], twy[1, k : k + 1]
                at = k * 3 * MC + c * MC
                ascr[at : at + MC, 0:256] = re * cos + im * sin
                ascr[at : at + MC, 256:512] = im * cos - re * sin
        out = product(split(ascr[...], 2), [kyf[0], kyf[1]]).reshape(8, 3, MC, 512)
        for half in range(2):
            for part in range(2):
                at = 256 * part + 128 * half
                y1[j, pl.ds(half, 8, 2), :, part] = out[:, :, :, at : at + 128]
        send_cols(1, j, y1, r2)

    def solve(j):
        await_all(1, j, r2, COLS)
        for c in range(3):
            xs = [(r2[j, s, c, 0], r2[j, s, c, 1]) for s in range(16)]
            for k, (re, im) in enumerate(fft(xs, -1)):
                cos, sin = twz[0, k : k + 1], twz[1, k : k + 1]
                at = k * 3 * MC + c * MC
                bscr[at : at + MC, 0:128] = re * cos + im * sin
                bscr[at : at + MC, 128:256] = im * cos - re * sin
        bscr[...] = product(split(bscr[...], 2), [kzf[0], kzf[1]])
        mode = row * 32 + j * MC + lax.broadcasted_iota(jnp.int32, (MC, 128), 0)
        lanes = lax.broadcasted_iota(jnp.int32, (MC, 128), 1)
        wave_x = mode.astype(F32) * (2.0 * math.pi / NX)
        index_y = col // 2 + 8 * (8 * lax.rem(col, 2) + lanes // 16)
        wave_y = jnp.where(index_y < NY // 2, index_y, index_y - NY).astype(F32) * (2.0 * math.pi / NY)
        keep_y = (index_y != NY // 2).astype(F32)
        for k in range(16):
            index_z = k + 16 * (lanes % 16)
            wave_z = jnp.where(index_z < NZ // 2, index_z, index_z - NZ).astype(F32) * (2.0 * math.pi / NZ)
            keep = keep_y * (index_z != NZ // 2).astype(F32)
            ksq = wave_x * wave_x + wave_y * wave_y + wave_z * wave_z
            inverse = 1.0 / jnp.where(ksq > 0, ksq, 1.0)
            gain = keep / (MASS + VISC * ksq)
            for part in range(2):
                at = 3 * MC * k
                lane = slice(128 * part, 128 * part + 128)
                fx, fy, fz = (bscr[at + MC * c : at + MC * c + MC, lane] for c in range(3))
                dotk = (wave_x * fx + wave_y * fy + wave_z * fz) * inverse
                bscr[at : at + MC, lane] = (fx - wave_x * dotk) * gain
                bscr[at + MC : at + 2 * MC, lane] = (fy - wave_y * dotk) * gain
                bscr[at + 2 * MC : at + 3 * MC, lane] = (fz - wave_z * dotk) * gain
        bscr[...] = product(split(bscr[...], INV), [kzi[p] for p in range(INV)])
        for c in range(3):
            xs = []
            for k in range(16):
                cos, sin = twz[0, k : k + 1], twz[1, k : k + 1]
                at = k * 3 * MC + c * MC
                re, im = bscr[at : at + MC, 0:128], bscr[at : at + MC, 128:256]
                xs.append((re * cos - im * sin, im * cos + re * sin))
            for s, (re, im) in enumerate(fft(xs, 1)):
                z1[j, s, c, 0] = re
                z1[j, s, c, 1] = im
        send_cols(2, j, z1, r3)

    def y_inverse(j):
        await_all(2, j, r3, COLS)
        for half in range(2):
            for part in range(2):
                at = 256 * part + 128 * half
                ascr[:, at : at + 128] = r3[j, pl.ds(half, 8, 2), :, part].reshape(8 * 3 * MC, 128)
        ascr[...] = product(split(ascr[...], INV), [kyi[p] for p in range(INV)])
        for c in range(3):
            xs = []
            for k in range(8):
                cos, sin = twy[0, k : k + 1], twy[1, k : k + 1]
                at = k * 3 * MC + c * MC
                re, im = ascr[at : at + MC, 0:256], ascr[at : at + MC, 256:512]
                xs.append((re * cos - im * sin, im * cos + re * sin))
            for s, (re, im) in enumerate(fft(xs, 1)):
                y2[j, s, c, 0:MC] = re
                y2[j, s, c, MC : 2 * MC] = im
        send_rows(3, j, y2, r4)

    def x_inverse(j):
        await_all(3, j, r4, ROWS)
        for c in range(3):
            spectrum = jnp.transpose(r4[j, :, c].reshape(2 * MC * ROWS, 256))
            out = product(split(spectrum, INV), [ti[p, j] for p in range(INV)])
            fluid[c] += out.reshape(16, 16, NX)

    def tile_copies():
        peers = ((row, col_peer(1)), (row, col_peer(COLS - 1)), (row_peer(1), col), (row_peer(ROWS - 1), col))
        return [
            remote(gtile.at[2], nbtile.at[k], halo_send.at[8 + k], halo_recv.at[8 + k], peer)
            for k, peer in enumerate(peers)
        ]

    def neighbours():
        for copy in tile_copies():
            copy.wait_recv()
        for k in range(4):
            tile = nbtile[k]
            nbcol[k] = dot_exact((pair == runs_lane).astype(F32), tile, NT)
            ids = dot_exact(spread_runs[0:32], tile, NT)[:, 5:6] * 0.25
            for r in range(ROWS):
                same = (ids == g2[r, 0:1]).astype(F32)
                match[32 + 32 * k : 64 + 32 * k, 512 * r : 512 * r + 512] = same.astype(BF16)
            line, block = tile[3:4], tile[4:5]
            y = jnp.floor(line * (1.0 / 16.0))
            z = line - 16.0 * y
            layer, along = (z, y) if k < 2 else (y, z)
            layer = layer - (14.0 if k % 2 == 0 else 0.0)
            inside = (layer >= 0.0) & (layer <= 1.0)
            target = jnp.where(inside, block * 32.0 + layer * 16.0 + along, -1.0)
            hits = (target == pair.astype(F32)).astype(F32)
            nbhot[k] = hits.astype(BF16)
            nbkeep[k] = jnp.broadcast_to(1.0 - jnp.sum(hits, axis=1, keepdims=True), (128, 128))

    def rigid_of(sums, cols):
        sums = dot_exact(gather_runs[:, 0:32], sums)
        rx, ry, rz, mean, turn = (cols[:, k : k + 1] for k in (0, 1, 2, 6, 7))
        vx, vy, vz = (sums[:, k : k + 1] * mean for k in range(3))
        wx, wy, wz = (sums[:, k : k + 1] * turn for k in range(3, 6))
        cell_x = rx + (lane128.astype(F32) - 63.5)
        return (
            jnp.broadcast_to(vx + wy * rz - wz * ry, (128, 128)),
            vy + wz * cell_x - wx * rz,
            vz + wx * ry - wy * cell_x,
        )

    def geometry():
        wait_for(g2.at[pl.ds(0, ROWS - 1)], g_recv.at[1])
        own = dot_exact(spread_runs[0:32], fields, NT) * 0.25
        ids = own[:, 0:1]
        count = jnp.zeros((32, 1), F32)
        cx, cy, cz = count, count, count
        sames = []
        for r in range(ROWS):
            block = g2[r]
            same = (ids == block[0:1]).astype(F32)
            match[0:32, 512 * r : 512 * r + 512] = same.astype(BF16)
            sames.append(same)
            count += jnp.sum(same, axis=1, keepdims=True)
            cx += jnp.sum(same * block[1:2], axis=1, keepdims=True)
            cy += jnp.sum(same * block[2:3], axis=1, keepdims=True)
            cz += jnp.sum(same * block[3:4], axis=1, keepdims=True)
        safe = jnp.maximum(count, 1.0)
        cx, cy, cz = cx / safe, cy / safe, cz / safe
        spread = jnp.zeros((32, 1), F32)
        for r in range(ROWS):
            block = g2[r]
            dx, dy, dz = block[1:2] - cx, block[2:3] - cy, block[3:4] - cz
            inner_spread = block[4:5] + 512.0 * (dx * dx + dy * dy + dz * dz)
            spread += jnp.sum(sames[r] * inner_spread, axis=1, keepdims=True)
        inertia = jnp.maximum(spread * (2.0 / 3.0), 1.0)
        place = lane128
        packed = jnp.where(place == 0, 1.0 / jnp.maximum(512.0 * count, 1.0), 0.0)
        for at, value in ((1, cx), (2, cy), (3, cz), (4, 1.0 / inertia)):
            packed = jnp.where(place == at, value, packed)
        mine = dot_exact((pair == runs_lane).astype(F32), fields, NT)
        centers = dot_exact(gather_runs[:, 0:32], packed)
        rel = jnp.where(place == 0, mine[:, 1:2] + 63.5 - centers[:, 1:2], 0.0)
        rel = jnp.where(place == 1, mine[:, 2:3] - centers[:, 2:3], rel)
        rel = jnp.where(place == 2, mine[:, 3:4] - centers[:, 3:4], rel)
        for at, value in enumerate((mine[:, 6:7], mine[:, 7:8], mine[:, 0:1], centers[:, 0:1], centers[:, 4:5])):
            rel = jnp.where(place == 3 + at, value, rel)
        mgeo[...] = rel
        gtile[2] = jnp.transpose(rel)[0:8]
        for copy in tile_copies():
            copy.start()
        rows256 = lax.broadcasted_iota(jnp.int32, (256, 128), 0).astype(F32)
        cols256 = lax.broadcasted_iota(jnp.int32, (128, 256), 1).astype(F32)
        for b in range(4):
            hot[b] = ((fields[6:7] == rows256) & (fields[7:8] == float(b))).astype(F32).astype(BF16)
            hott[b] = ((mine[:, 6:7] == cols256) & (mine[:, 7:8] == float(b))).astype(F32).astype(BF16)

    loaded("tf")
    x_forward(0)
    x_forward(1)
    geometry()
    loaded("twy", "kyf", "twz", "kzf", "kzi", "kyi", "ti")

    @pl.loop(0, CHUNKS + 5)
    def _(t):
        pl.when(t < CHUNKS)(lambda: y_forward(t))
        pl.when(t + 2 < CHUNKS)(lambda: x_forward(t + 2))
        pl.when(t == 3)(neighbours)
        pl.when((t >= 2) & (t < CHUNKS + 2))(lambda: solve(t - 2))
        pl.when((t >= 4) & (t < CHUNKS + 4))(lambda: y_inverse(t - 4))
        pl.when(t >= 5)(lambda: x_inverse(t - 5))

    for copy in stress_halos:
        copy.wait_send()
    for c in range(3):
        for layer, z in enumerate((0, 1, 14, 15)):
            zf[c, layer] = fluid[c, :, z, :]
    velocity_halos = halo_copies(4, fluid, 14, 0, vext, zf, vzh)
    for copy in velocity_halos:
        copy.start()

    inside = lane128.astype(F32) - 63.5
    blocks = []
    firsts, seconds = [], []
    for c in range(3):
        block = jnp.zeros((128, 128), F32)
        for b in range(4):
            block += exact_left(hott[b], fluid[c, :, :, 128 * b : 128 * b + 128].reshape(256, 128), 3)
        blocks.append(block)
        firsts.append(jnp.sum(block, axis=1, keepdims=True))
        seconds.append(jnp.sum(block * inside, axis=1, keepdims=True))
    rx, ry, rz = mgeo[:, 0:1], mgeo[:, 1:2], mgeo[:, 2:3]
    moments = jnp.zeros((128, 128), F32)
    for at, value in enumerate(
        (
            firsts[0],
            firsts[1],
            firsts[2],
            ry * firsts[2] - rz * firsts[1],
            rz * firsts[0] - (rx * firsts[2] + seconds[2]),
            rx * firsts[1] + seconds[1] - ry * firsts[0],
        )
    ):
        moments = jnp.where(lane128 == at, value, moments)
    gtile[1] = dot_exact(jnp.transpose(moments)[0:8], gather_runs)
    gather_cols(1, g3)
    gather_rows(1, g3, g4)
    wait_for(g4.at[pl.ds(0, ROWS - 1)], g_recv.at[3])
    parts = split(jnp.concatenate([g4[r] for r in range(ROWS)], axis=1), 3)
    parts = jnp.concatenate([part.astype(F32) for part in parts], axis=0).astype(BF16)
    totals = dot(match[...], parts, NT)
    totals = totals[:, 16:24] + totals[:, 8:16] + totals[:, 0:8]
    rigid = rigid_of(totals[0:32], mgeo)
    for c in range(3):
        fix = rigid[c] - blocks[c]
        for b in range(4):
            lanes = slice(128 * b, 128 * b + 128)
            done = fluid[c, :, :, lanes] + exact_left(hot[b], fix, 3).reshape(16, 16, 128)
            vext[c, 2:18, :, lanes] = done
    stores = [pltpu.make_async_copy(vext.at[c, 2:18], vext_out.at[c, 2:18], store_sem.at[c]) for c in range(3)]
    for store in stores:
        store.start()
    for copy in velocity_halos:
        copy.wait_recv()
    for k in range(4):
        rigid = rigid_of(totals[32 + 32 * k : 64 + 32 * k], nbcol[k])
        fix = exact_left(nbhot[k], jnp.concatenate(rigid, axis=1), 3)
        keep = nbkeep[k]
        ref, first = ((vzh, 0), (vzh, 2), (vext, 0), (vext, 18))[k]
        for c in range(3):
            for b in range(4):
                lanes, rows = slice(128 * b, 128 * b + 128), slice(32 * b, 32 * b + 32)
                old = ref[c, first : first + 2, :, lanes].reshape(32, 128)
                new = old * keep[rows] + fix[rows, 128 * c : 128 * c + 128]
                ref[c, first : first + 2, :, lanes] = new.reshape(2, 16, 128)
    late = [
        pltpu.make_async_copy(vext.at[:, 0:2], vext_out.at[:, 0:2], store_sem.at[3]),
        pltpu.make_async_copy(vext.at[:, 18:20], vext_out.at[:, 18:20], store_sem.at[4]),
        pltpu.make_async_copy(vzh, vzh_out, store_sem.at[5]),
    ]
    for store in late:
        store.start()
    stores += late

    for copy in velocity_halos + tile_copies():
        copy.wait_send()
    wait_for(g1.at[pl.ds(0, COLS - 1)], g_send.at[0])
    wait_for(g2.at[pl.ds(0, ROWS - 1)], g_send.at[1])
    wait_for(g3.at[pl.ds(0, COLS - 1)], g_send.at[2])
    wait_for(g4.at[pl.ds(0, ROWS - 1)], g_send.at[3])

    @pl.loop(0, CHUNKS)
    def _(j):
        wait_for(x1.at[j, pl.ds(0, ROWS - 1)], a_send.at[0, j])
        wait_for(y1.at[j, pl.ds(0, COLS - 1)], a_send.at[1, j])
        wait_for(z1.at[j, pl.ds(0, COLS - 1)], a_send.at[2, j])
        wait_for(y2.at[j, pl.ds(0, ROWS - 1)], a_send.at[3, j])

    for store in stores:
        store.wait()


def update(vlow, vhigh, vzh, mult, dzt, bzt, vel, new_aux, new_mult, *, lines):
    rows = 16 * lines
    edge = bzt[...]
    grads = []
    for c in range(3):
        both = jnp.concatenate([vlow[c], vhigh[c]], axis=0)
        field = both[2 : lines + 2]
        vel[c] = field
        dx = along_x(field.reshape(rows, NX))
        near = [both[k : lines + k].reshape(rows, NX) for k in (0, 1, 3, 4)]
        dy = centered(*near)
        dz = exact_left(dzt[...], field.reshape(rows, NX), 3) + exact_left(edge, vzh[c], 3)
        grads.append((dx, dy, dz * (1.0 / 12.0)))
    strain = (
        grads[0][0],
        grads[1][1],
        grads[2][2],
        (grads[0][1] + grads[1][0]) * 0.5,
        (grads[0][2] + grads[2][0]) * 0.5,
        (grads[1][2] + grads[2][1]) * 0.5,
    )
    old = [mult[k].reshape(rows, NX) for k in range(6)]
    q = [old[k] + PEN * strain[k] for k in range(6)]
    norm = jnp.sqrt(
        q[0] * q[0] + q[1] * q[1] + q[2] * q[2] + 2.0 * (q[3] * q[3] + q[4] * q[4] + q[5] * q[5])
    )
    factor = 1.0 - YIELD / jnp.maximum(norm, YIELD)
    for k in range(6):
        aux = factor * q[k] * (1.0 / PEN)
        new_aux[k] = aux.reshape(lines, 16, NX)
        new_mult[k] = (old[k] + PEN * (strain[k] - aux)).reshape(lines, 16, NX)


def local(force, mult, aux, entry_lines, entry_owner, entry_slot):
    t = make_tables()
    vm = pl.BlockSpec(memory_space=pltpu.VMEM)
    hbm = pl.BlockSpec(memory_space=pltpu.HBM)
    sems = pltpu.SemaphoreType.DMA
    names = ("tf", "ti", "kyf", "kyi", "kzf", "kzi", "twy", "twz", "dz", "bz")
    loads = [force, mult, aux] + [jnp.asarray(t[k]) for k in names]
    scratch = [pltpu.VMEM(a.shape, a.dtype) for a in loads] + [
        pltpu.VMEM((3, 20, 16, NX), F32),
        pltpu.VMEM((3, 4, 16, NX), F32),
        pltpu.VMEM((3, 4, 16, NX), F32),
        pltpu.VMEM((3, 20, 16, NX), F32),
        pltpu.VMEM((3, 4, 16, NX), F32),
        pltpu.VMEM((3, 256, NX), F32),
        pltpu.VMEM((2, 3, 256, NX), BF16),
        pltpu.VMEM((3, 16, 16, NX), F32),
        pltpu.VMEM((CHUNKS, ROWS, 3, 2 * MC, 256), F32),
        pltpu.VMEM((CHUNKS, ROWS, 3, 2 * MC, 256), F32),
        pltpu.VMEM((CHUNKS, COLS, 3, 2, MC, 128), F32),
        pltpu.VMEM((CHUNKS, COLS, 3, 2, MC, 128), F32),
        pltpu.VMEM((CHUNKS, COLS, 3, 2, MC, 128), F32),
        pltpu.VMEM((CHUNKS, COLS, 3, 2, MC, 128), F32),
        pltpu.VMEM((CHUNKS, ROWS, 3, 2 * MC, 256), F32),
        pltpu.VMEM((CHUNKS, ROWS, 3, 2 * MC, 256), F32),
        pltpu.VMEM((24 * MC, 512), F32),
        pltpu.VMEM((48 * MC, 256), F32),
        pltpu.VMEM((COLS, 8, 128), F32),
        pltpu.VMEM((ROWS, 8, 512), F32),
        pltpu.VMEM((COLS, 8, 128), F32),
        pltpu.VMEM((ROWS, 8, 512), F32),
        pltpu.VMEM((3, 8, 128), F32),
        pltpu.VMEM((160, 512 * ROWS), BF16),
        pltpu.VMEM((128, 128), F32),
        pltpu.VMEM((4, 256, 128), BF16),
        pltpu.VMEM((4, 128, 256), BF16),
        pltpu.VMEM((4, 8, 128), F32),
        pltpu.VMEM((4, 128, 8), F32),
        pltpu.VMEM((4, 128, 128), BF16),
        pltpu.VMEM((4, 128, 128), F32),
        sems((12,)),
        sems((12,)),
        sems((4, CHUNKS)),
        sems((4, CHUNKS)),
        sems((4,)),
        sems((4,)),
        sems((len(names) + 13,)),
        sems((6,)),
    ]
    vext, vzh = pl.pallas_call(
        kernel,
        out_shape=(
            jax.ShapeDtypeStruct((3, 20, 16, NX), F32),
            jax.ShapeDtypeStruct((3, 4, 16, NX), F32),
        ),
        in_specs=[hbm] * 3 + [vm] * 3 + [hbm] * len(names),
        out_specs=(hbm, hbm),
        scratch_shapes=scratch,
        compiler_params=pltpu.CompilerParams(
            collective_id=0, has_side_effects=True, vmem_limit_bytes=58 * 2**20
        ),
    )(
        force,
        mult,
        aux,
        entry_lines.reshape(1, 128),
        entry_owner.reshape(1, 128),
        entry_slot.reshape(1, 128),
        *loads[3:],
    )

    lines = 4
    whole = lambda *shape: pl.BlockSpec(shape, lambda i: (0,) * len(shape))
    part = lambda n: pl.BlockSpec((n, lines, 16, NX), lambda i: (0, i, 0, 0))
    return tuple(
        pl.pallas_call(
            functools.partial(update, lines=lines),
            grid=(16 // lines,),
            out_shape=tuple(jax.ShapeDtypeStruct((n, 16, 16, NX), F32) for n in (3, 6, 6)),
            in_specs=[
                part(3),
                pl.BlockSpec((3, lines, 16, NX), lambda i: (0, i + 1, 0, 0)),
                whole(3, 64, NX),
                part(6),
                whole(16 * lines, 16 * lines),
                pl.BlockSpec((16 * lines, 64), lambda i: (i, 0)),
            ],
            out_specs=tuple(part(n) for n in (3, 6, 6)),
            compiler_params=pltpu.CompilerParams(vmem_limit_bytes=58 * 2**20),
        )(
            vext,
            vext,
            vzh.reshape(3, 64, NX),
            mult,
            jnp.asarray(deriv_rows(lines).astype(jnp.bfloat16)),
            jnp.asarray(t["bz"]),
        )
    )


def solution(mesh):
    field = P(None, "row", "col", None)
    return jax.shard_map(
        local,
        mesh=mesh,
        in_specs=(field, field, field, P(("row", "col")), P(("row", "col"), None), P(("row", "col"))),
        out_specs=(field, field, field),
        check_vma=False,
    )
```

```python
import functools
import math

import jax
import jax.numpy as jnp
import numpy as np
from jax import lax
from jax.experimental import pallas as pl
from jax.experimental.pallas import tpu as pltpu
from jax.sharding import PartitionSpec as P

MASS, VISC, PEN, YIELD = 0.02, 10.0, 5.0, 2.0
NPD = 72
NX, NY, NZ = 512, 128, 256
ROWS, COLS = 8, 16
CHUNKS = 4
MC = 32 // CHUNKS
F32, BF16 = jnp.float32, jnp.bfloat16
MESH = pl.DeviceIdType.MESH
HIGHEST = lax.Precision.HIGHEST
NN = (((1,), (0,)), ((), ()))
NT = (((1,), (1,)), ((), ()))

FAR = (
    (2, 2), (2, 1), (1, 2), (2, 3), (3, 2), (1, 1), (3, 3), (1, 3), (3, 1),
    (2, 0), (0, 2), (1, 0), (0, 1), (3, 0), (0, 3),
)

YCOMP = (3, 1, 5)
ZCOMP = (4, 5, 2)
XCOMP = (0, 3, 4)


def pieces_np(table, count):
    out = []
    rest = np.asarray(table, np.float64)
    for _ in range(count):
        piece = rest.astype(jnp.bfloat16)
        out.append(piece)
        rest = rest - piece.astype(np.float64)
    return np.stack(out)


def kron_dft(points, batch, sign):
    index = np.arange(points)
    angle = sign * 2 * np.pi * (np.outer(index, index) % points) / points
    eye = np.eye(batch)
    cos, sin = np.kron(np.cos(angle), eye), np.kron(np.sin(angle), eye)
    return np.block([[cos, sin], [-sin, cos]])


def kron_dft_z(sign):
    index = np.arange(16)
    angle = sign * 2 * np.pi * (np.outer(index, index) % 16) / 16
    eye = np.eye(8)
    cos, sin = np.kron(eye, np.cos(angle)), np.kron(eye, np.sin(angle))
    return np.block([[cos, sin], [-sin, cos]])


def mode_table():
    chunk, dest, part, inner = np.meshgrid(
        np.arange(CHUNKS), np.arange(ROWS), np.arange(2), np.arange(MC), indexing="ij"
    )
    mode = 32 * dest + MC * chunk + inner
    return mode.reshape(CHUNKS, -1), part.reshape(CHUNKS, -1)


def make_tables():
    mode, part = mode_table()
    x = np.arange(NX)
    angle = 2 * np.pi * ((mode[..., None] * x) % NX) / NX
    fwd = np.where(part[..., None] == 0, np.cos(angle), -np.sin(angle))
    weight = np.where(mode == 0, 1.0, 2.0)[..., None] / float(NX * NY * NZ)
    inv = weight * fwd
    ky_f = pieces_np(kron_dft(16, 16, -1), 2)
    ky_i = pieces_np(kron_dft(16, 16, 1), INV)
    kz_f = pieces_np(kron_dft_z(-1), 2)
    kz_i = pieces_np(kron_dft_z(1), INV)
    lane = np.arange(256)
    turn_y = 2 * np.pi * np.outer(np.arange(8), lane // 16) / NY
    turn_z = 2 * np.pi * np.outer(np.arange(16), np.arange(128) % 16) / NZ
    two_y = np.stack([np.cos(turn_y), np.sin(turn_y)]).astype(np.float32)
    two_z = np.stack([np.cos(turn_z), np.sin(turn_z)]).astype(np.float32)
    return {
        "tf": pieces_np(fwd, 2),
        "ti": pieces_np(inv, INV),
        "kyf": ky_f,
        "kyi": ky_i,
        "kzf": kz_f,
        "kzi": kz_i,
        "twy": two_y,
        "twz": two_z,
        "dz": deriv_rows(16).astype(jnp.bfloat16),
        "bz": deriv_halo().astype(jnp.bfloat16),
    }


INV = 3


def deriv_rows(lines):
    one = np.zeros((16, 16))
    for offset, coef in ((1, 8), (-1, -8), (2, -1), (-2, 1)):
        one += coef * np.eye(16, k=offset)
    return np.kron(np.eye(lines), one)


def deriv_halo():
    out = np.zeros((16, 16, 4, 16))
    for y in range(16):
        for layer, place in enumerate((-2, -1, 16, 17)):
            for z in range(16):
                out[y, z, layer, y] = {1: 8, -1: -8, 2: -1, -2: 1}.get(place - z, 0)
    return out.reshape(256, 64)


def split(value, count):
    out = []
    for step in range(count):
        piece = value.astype(BF16)
        out.append(piece)
        if step + 1 < count:
            value = value - piece.astype(F32)
    return out


def dot(a, b, dims=NN):
    return lax.dot_general(a, b, dims, preferred_element_type=F32)


def dot_exact(a, b, dims=NN):
    return lax.dot_general(a, b, dims, precision=HIGHEST, preferred_element_type=F32)


def product(a, b, dims=NN):
    count = len(a)
    total = None
    for i in range(count - 1, -1, -1):
        for j in range(count - 1 - i, -1, -1):
            term = dot(a[i], b[j], dims)
            total = term if total is None else total + term
    return total


def exact_left(a, value, count):
    total = None
    for piece in reversed(split(value, count)):
        term = dot(a, piece)
        total = term if total is None else total + term
    return total


def fft(xs, sign):
    count = len(xs)
    if count == 1:
        return xs
    even, odd = fft(xs[0::2], sign), fft(xs[1::2], sign)
    out = [None] * count
    half = count // 2
    for k in range(half):
        re, im = odd[k]
        if k == 0:
            tr, ti = re, im
        elif 4 * k == count:
            tr, ti = (-im, re) if sign > 0 else (im, -re)
        else:
            c = math.cos(2 * math.pi * k / count)
            s = sign * math.sin(2 * math.pi * k / count)
            tr, ti = re * c - im * s, re * s + im * c
        er, ei = even[k]
        out[k] = (er + tr, ei + ti)
        out[k + half] = (er - tr, ei - ti)
    return out


def along_x(field):
    axis = field.ndim - 1
    up1, up2 = pltpu.roll(field, NX - 1, axis), pltpu.roll(field, NX - 2, axis)
    lo1, lo2 = pltpu.roll(field, 1, axis), pltpu.roll(field, 2, axis)
    return (8.0 * (up1 - lo1) - (up2 - lo2)) * (1.0 / 12.0)


def centered(lo2, lo1, up1, up2):
    return (8.0 * (up1 - lo1) - (up2 - lo2)) * (1.0 / 12.0)


def kernel(
    force_in, mult_in, aux_in, lines_in, owner_in, slot_in,
    tf_in, ti_in, kyf_in, kyi_in, kzf_in, kzi_in, twy_in, twz_in, dzt_in, bzt_in,
    vext_out, vzh_out,
    force, mult, aux, tf, ti, kyf, kyi, kzf, kzi, twy, twz, dzt, bzt,
    yext, zf, zh, vext, vzh, rhs, rpieces, fluid,
    x1, r1, y1, r2, z1, r3, y2, r4, ascr, bscr,
    g1, g2, g3, g4, gtile, match, mgeo, hot, hott, nbtile, nbcol, nbhot, nbkeep,
    halo_send, halo_recv, a_send, a_recv, g_send, g_recv, load_sem, store_sem,
):
    row, col = lax.axis_index("row"), lax.axis_index("col")

    def row_peer(off):
        return lax.rem(row + off, ROWS)

    def col_peer(off):
        return lax.rem(col + off, COLS)

    def remote(src, dst, send, recv, device):
        return pltpu.make_async_remote_copy(
            src_ref=src, dst_ref=dst, send_sem=send, recv_sem=recv,
            device_id=device, device_id_type=MESH,
        )

    def wait_for(ref, sem):
        pltpu.make_async_copy(ref, ref, sem).wait()

    loads = {}

    def load(name, src, dst):
        loads[name] = pltpu.make_async_copy(src, dst, load_sem.at[len(loads)])
        loads[name].start()

    for comp in (4, 5, 2, 3, 1):
        load(("mult", comp), mult_in.at[comp], mult.at[comp])
        load(("aux", comp), aux_in.at[comp], aux.at[comp])
    load("dzt", dzt_in, dzt)
    load("bzt", bzt_in, bzt)
    load(("mult", 0), mult_in.at[0], mult.at[0])
    load(("aux", 0), aux_in.at[0], aux.at[0])
    load("force", force_in, force)
    for name, src, dst in (
        ("tf", tf_in, tf), ("twy", twy_in, twy), ("kyf", kyf_in, kyf), ("twz", twz_in, twz),
        ("kzf", kzf_in, kzf), ("kzi", kzi_in, kzi), ("kyi", kyi_in, kyi), ("ti", ti_in, ti),
    ):
        load(name, src, dst)

    def loaded(*names):
        for name in names:
            loads.pop(name).wait()

    barrier = pltpu.get_barrier_semaphore()
    for off in range(1, ROWS):
        pl.semaphore_signal(barrier, inc=1, device_id=(row_peer(off), col), device_id_type=MESH)
    for off in range(1, COLS):
        pl.semaphore_signal(barrier, inc=1, device_id=(row, col_peer(off)), device_id_type=MESH)

    def shifted(comp):
        return mult[comp] - PEN * aux[comp]

    for i, comp in enumerate(ZCOMP):
        loaded(("mult", comp), ("aux", comp))
        for layer, z in enumerate((0, 1, 14, 15)):
            zf[i, layer] = mult[comp, :, z, :] - PEN * aux[comp, :, z, :]
    pl.semaphore_wait(barrier, ROWS + COLS - 2)

    def halo_copies(base, ysrc, high, low, ydst, zsrc, zdst):
        up, down = (row_peer(1), col), (row_peer(ROWS - 1), col)
        right, left = (row, col_peer(1)), (row, col_peer(COLS - 1))
        sems = [(halo_send.at[base + k], halo_recv.at[base + k]) for k in range(4)]
        return [
            remote(zsrc.at[:, 2:4], zdst.at[:, 0:2], *sems[0], right),
            remote(zsrc.at[:, 0:2], zdst.at[:, 2:4], *sems[1], left),
            remote(ysrc.at[:, high : high + 2], ydst.at[:, 0:2], *sems[2], up),
            remote(ysrc.at[:, low : low + 2], ydst.at[:, 18:20], *sems[3], down),
        ]

    stress_halos = halo_copies(0, yext, 16, 2, yext, zf, zh)
    for copy in stress_halos[0:2]:
        copy.start()
    for i, comp in enumerate(YCOMP):
        if comp != 5:
            loaded(("mult", comp), ("aux", comp))
        yext[i, 2:18] = shifted(comp)
    for copy in stress_halos[2:4]:
        copy.start()

    lane128 = lax.broadcasted_iota(jnp.int32, (1, 128), 1)
    lines, block_x = lines_in[...], lines_in[...] & 3
    particle = owner_in[...] * NPD + slot_in[...]
    gy = ((lines >> 6) + row * 16).astype(F32)
    gz = (((lines >> 2) & 15) + col * 16).astype(F32)
    fields = jnp.concatenate(
        [
            particle.astype(F32),
            (block_x * 128).astype(F32),
            gy,
            gz,
            gy * gy,
            gz * gz,
            (lines >> 2).astype(F32),
            block_x.astype(F32),
        ],
        axis=0,
    )
    pair = lax.broadcasted_iota(jnp.int32, (128, 128), 0)
    runs_lane = lax.broadcasted_iota(jnp.int32, (128, 128), 1)
    gather_runs = (pair // 4 == runs_lane).astype(F32)
    spread_runs = (runs_lane // 4 == pair).astype(F32)
    sums = dot_exact(fields, gather_runs)
    mean_y, mean_z = sums[2:3] * 0.25, sums[3:4] * 0.25
    inner = 4.0 * 174752.0 + 128.0 * (
        sums[4:5] - 4.0 * mean_y * mean_y + sums[5:6] - 4.0 * mean_z * mean_z
    )
    gtile[0] = jnp.concatenate(
        [sums[0:1] * 0.25, sums[1:2] * 0.25 + 63.5, mean_y, mean_z, inner, jnp.zeros((3, 128), F32)], axis=0
    )

    def gather_cols(slot, buf):
        buf[col] = gtile[slot]
        for off in range(1, COLS):
            remote(
                gtile.at[slot], buf.at[col], g_send.at[2 * slot], g_recv.at[2 * slot], (row, col_peer(off))
            ).start()

    def gather_rows(slot, buf, wide):
        wait_for(buf.at[pl.ds(0, COLS - 1)], g_recv.at[2 * slot])
        parts = []
        for q in range(4):
            total = None
            for k in range(4):
                tile = jnp.where(runs_lane[0:8] < 32, buf[4 * q + k], 0.0)
                tile = pltpu.roll(tile, 32 * k, 1) if k else tile
                total = tile if total is None else total + tile
            parts.append(total)
        wide[row] = jnp.concatenate(parts, axis=1)
        for off in range(1, ROWS):
            remote(
                wide.at[row], wide.at[row], g_send.at[2 * slot + 1], g_recv.at[2 * slot + 1], (row_peer(off), col)
            ).start()

    gather_cols(0, g1)

    loaded("dzt", "bzt", ("mult", 0), ("aux", 0), "force")
    for c, comp in enumerate(XCOMP):
        rhs[c] = (force[c] + along_x(shifted(comp))).reshape(256, NX)
    fluid[...] = jnp.zeros_like(fluid)
    for c, comp in enumerate(ZCOMP):
        own = shifted(comp).reshape(256, NX)
        rhs[c] += exact_left(dzt[...], own, 2) * (1.0 / 12.0)
    gather_rows(0, g1, g2)
    for copy in stress_halos:
        copy.wait_recv()
    for c in range(3):
        along_y = centered(yext[c, 0:16], yext[c, 1:17], yext[c, 3:19], yext[c, 4:20]).reshape(256, NX)
        edge = exact_left(bzt[...], zh[c].reshape(64, NX), 2) * (1.0 / 12.0)
        high, low = split(rhs[c] + along_y + edge, 2)
        rpieces[0, c] = high
        rpieces[1, c] = low

    def send_rows(stage, j, src, dst):
        dst[j, row] = src[j, row]
        for off in range(1, ROWS):
            peer = row_peer(off)
            remote(src.at[j, peer], dst.at[j, row], a_send.at[stage, j], a_recv.at[stage, j], (peer, col)).start()

    def send_cols(stage, j, src, dst):
        dst[j, col] = src[j, col]
        for dy, dz in FAR:
            peer = 4 * lax.rem(col // 4 + dz, 4) + lax.rem(col % 4 + dy, 4)
            remote(src.at[j, peer], dst.at[j, col], a_send.at[stage, j], a_recv.at[stage, j], (row, peer)).start()

    def await_all(stage, j, dst, count):
        wait_for(dst.at[j, pl.ds(0, count - 1)], a_recv.at[stage, j])

    def x_forward(j):
        for c in range(3):
            out = product([tf[0, j], tf[1, j]], [rpieces[0, c], rpieces[1, c]], NT)
            x1[j, :, c] = out.reshape(ROWS, 2 * MC, 256)
        send_rows(0, j, x1, r1)

    def y_forward(j):
        await_all(0, j, r1, ROWS)
        for c in range(3):
            xs = [(r1[j, s, c, 0:MC], r1[j, s, c, MC : 2 * MC]) for s in range(8)]
            for k, (re, im) in enumerate(fft(xs, -1)):
                cos, sin = twy[0, k : k + 1], twy[1, k : k + 1]
                at = k * 3 * MC + c * MC
                ascr[at : at + MC, 0:256] = re * cos + im * sin
                ascr[at : at + MC, 256:512] = im * cos - re * sin
        out = product(split(ascr[...], 2), [kyf[0], kyf[1]]).reshape(8, 3, MC, 512)
        for half in range(2):
            for part in range(2):
                at = 256 * part + 128 * half
                y1[j, pl.ds(half, 8, 2), :, part] = out[:, :, :, at : at + 128]
        send_cols(1, j, y1, r2)

    def solve(j):
        await_all(1, j, r2, COLS)
        for c in range(3):
            xs = [(r2[j, s, c, 0], r2[j, s, c, 1]) for s in range(16)]
            for k, (re, im) in enumerate(fft(xs, -1)):
                cos, sin = twz[0, k : k + 1], twz[1, k : k + 1]
                at = k * 3 * MC + c * MC
                bscr[at : at + MC, 0:128] = re * cos + im * sin
                bscr[at : at + MC, 128:256] = im * cos - re * sin
        bscr[...] = product(split(bscr[...], 2), [kzf[0], kzf[1]])
        mode = row * 32 + j * MC + lax.broadcasted_iota(jnp.int32, (MC, 128), 0)
        lanes = lax.broadcasted_iota(jnp.int32, (MC, 128), 1)
        wave_x = mode.astype(F32) * (2.0 * math.pi / NX)
        index_y = col // 2 + 8 * (8 * lax.rem(col, 2) + lanes // 16)
        wave_y = jnp.where(index_y < NY // 2, index_y, index_y - NY).astype(F32) * (2.0 * math.pi / NY)
        keep_y = (index_y != NY // 2).astype(F32)
        for k in range(16):
            index_z = k + 16 * (lanes % 16)
            wave_z = jnp.where(index_z < NZ // 2, index_z, index_z - NZ).astype(F32) * (2.0 * math.pi / NZ)
            keep = keep_y * (index_z != NZ // 2).astype(F32)
            ksq = wave_x * wave_x + wave_y * wave_y + wave_z * wave_z
            inverse = 1.0 / jnp.where(ksq > 0, ksq, 1.0)
            gain = keep / (MASS + VISC * ksq)
            for part in range(2):
                at = 3 * MC * k
                lane = slice(128 * part, 128 * part + 128)
                fx, fy, fz = (bscr[at + MC * c : at + MC * c + MC, lane] for c in range(3))
                dotk = (wave_x * fx + wave_y * fy + wave_z * fz) * inverse
                bscr[at : at + MC, lane] = (fx - wave_x * dotk) * gain
                bscr[at + MC : at + 2 * MC, lane] = (fy - wave_y * dotk) * gain
                bscr[at + 2 * MC : at + 3 * MC, lane] = (fz - wave_z * dotk) * gain
        bscr[...] = product(split(bscr[...], INV), [kzi[p] for p in range(INV)])
        for c in range(3):
            xs = []
            for k in range(16):
                cos, sin = twz[0, k : k + 1], twz[1, k : k + 1]
                at = k * 3 * MC + c * MC
                re, im = bscr[at : at + MC, 0:128], bscr[at : at + MC, 128:256]
                xs.append((re * cos - im * sin, im * cos + re * sin))
            for s, (re, im) in enumerate(fft(xs, 1)):
                z1[j, s, c, 0] = re
                z1[j, s, c, 1] = im
        send_cols(2, j, z1, r3)

    def y_inverse(j):
        await_all(2, j, r3, COLS)
        for half in range(2):
            for part in range(2):
                at = 256 * part + 128 * half
                ascr[:, at : at + 128] = r3[j, pl.ds(half, 8, 2), :, part].reshape(8 * 3 * MC, 128)
        ascr[...] = product(split(ascr[...], INV), [kyi[p] for p in range(INV)])
        for c in range(3):
            xs = []
            for k in range(8):
                cos, sin = twy[0, k : k + 1], twy[1, k : k + 1]
                at = k * 3 * MC + c * MC
                re, im = ascr[at : at + MC, 0:256], ascr[at : at + MC, 256:512]
                xs.append((re * cos - im * sin, im * cos + re * sin))
            for s, (re, im) in enumerate(fft(xs, 1)):
                y2[j, s, c, 0:MC] = re
                y2[j, s, c, MC : 2 * MC] = im
        send_rows(3, j, y2, r4)

    def x_inverse(j):
        await_all(3, j, r4, ROWS)
        for c in range(3):
            spectrum = jnp.transpose(r4[j, :, c].reshape(2 * MC * ROWS, 256))
            out = product(split(spectrum, INV), [ti[p, j] for p in range(INV)])
            fluid[c] += out.reshape(16, 16, NX)

    def tile_copies():
        peers = ((row, col_peer(1)), (row, col_peer(COLS - 1)), (row_peer(1), col), (row_peer(ROWS - 1), col))
        return [
            remote(gtile.at[2], nbtile.at[k], halo_send.at[8 + k], halo_recv.at[8 + k], peer)
            for k, peer in enumerate(peers)
        ]

    def neighbours():
        for copy in tile_copies():
            copy.wait_recv()
        for k in range(4):
            tile = nbtile[k]
            nbcol[k] = dot_exact((pair == runs_lane).astype(F32), tile, NT)
            ids = dot_exact(spread_runs[0:32], tile, NT)[:, 5:6] * 0.25
            for r in range(ROWS):
                same = (ids == g2[r, 0:1]).astype(F32)
                match[32 + 32 * k : 64 + 32 * k, 512 * r : 512 * r + 512] = same.astype(BF16)
            line, block = tile[3:4], tile[4:5]
            y = jnp.floor(line * (1.0 / 16.0))
            z = line - 16.0 * y
            layer, along = (z, y) if k < 2 else (y, z)
            layer = layer - (14.0 if k % 2 == 0 else 0.0)
            inside = (layer >= 0.0) & (layer <= 1.0)
            target = jnp.where(inside, block * 32.0 + layer * 16.0 + along, -1.0)
            hits = (target == pair.astype(F32)).astype(F32)
            nbhot[k] = hits.astype(BF16)
            nbkeep[k] = jnp.broadcast_to(1.0 - jnp.sum(hits, axis=1, keepdims=True), (128, 128))

    def rigid_of(sums, cols):
        rx, ry, rz, mean, turn = (cols[:, k : k + 1] for k in (0, 1, 2, 6, 7))
        vx, vy, vz = (sums[:, k : k + 1] * mean for k in range(3))
        wx, wy, wz = (sums[:, k : k + 1] * turn for k in range(3, 6))
        cell_x = rx + (lane128.astype(F32) - 63.5)
        return (
            jnp.broadcast_to(vx + wy * rz - wz * ry, (128, 128)),
            vy + wz * cell_x - wx * rz,
            vz + wx * ry - wy * cell_x,
        )

    def geometry():
        wait_for(g2.at[pl.ds(0, ROWS - 1)], g_recv.at[1])
        own = dot_exact(spread_runs[0:32], fields, NT) * 0.25
        ids = own[:, 0:1]
        count = jnp.zeros((32, 1), F32)
        cx, cy, cz = count, count, count
        sames = []
        for r in range(ROWS):
            block = g2[r]
            same = (ids == block[0:1]).astype(F32)
            match[0:32, 512 * r : 512 * r + 512] = same.astype(BF16)
            sames.append(same)
            count += jnp.sum(same, axis=1, keepdims=True)
            cx += jnp.sum(same * block[1:2], axis=1, keepdims=True)
            cy += jnp.sum(same * block[2:3], axis=1, keepdims=True)
            cz += jnp.sum(same * block[3:4], axis=1, keepdims=True)
        safe = jnp.maximum(count, 1.0)
        cx, cy, cz = cx / safe, cy / safe, cz / safe
        spread = jnp.zeros((32, 1), F32)
        for r in range(ROWS):
            block = g2[r]
            dx, dy, dz = block[1:2] - cx, block[2:3] - cy, block[3:4] - cz
            inner_spread = block[4:5] + 512.0 * (dx * dx + dy * dy + dz * dz)
            spread += jnp.sum(sames[r] * inner_spread, axis=1, keepdims=True)
        inertia = jnp.maximum(spread * (2.0 / 3.0), 1.0)
        place = lane128
        packed = jnp.where(place == 0, 1.0 / jnp.maximum(512.0 * count, 1.0), 0.0)
        for at, value in ((1, cx), (2, cy), (3, cz), (4, 1.0 / inertia)):
            packed = jnp.where(place == at, value, packed)
        mine = dot_exact((pair == runs_lane).astype(F32), fields, NT)
        centers = dot_exact(gather_runs[:, 0:32], packed)
        rel = jnp.where(place == 0, mine[:, 1:2] + 63.5 - centers[:, 1:2], 0.0)
        rel = jnp.where(place == 1, mine[:, 2:3] - centers[:, 2:3], rel)
        rel = jnp.where(place == 2, mine[:, 3:4] - centers[:, 3:4], rel)
        for at, value in enumerate((mine[:, 6:7], mine[:, 7:8], mine[:, 0:1], centers[:, 0:1], centers[:, 4:5])):
            rel = jnp.where(place == 3 + at, value, rel)
        mgeo[...] = rel
        gtile[2] = jnp.transpose(rel)[0:8]
        for copy in tile_copies():
            copy.start()
        rows256 = lax.broadcasted_iota(jnp.int32, (256, 128), 0).astype(F32)
        cols256 = lax.broadcasted_iota(jnp.int32, (128, 256), 1).astype(F32)
        for b in range(4):
            hot[b] = ((fields[6:7] == rows256) & (fields[7:8] == float(b))).astype(F32).astype(BF16)
            hott[b] = ((mine[:, 6:7] == cols256) & (mine[:, 7:8] == float(b))).astype(F32).astype(BF16)

    loaded("tf")
    x_forward(0)
    x_forward(1)
    geometry()
    loaded("twy", "kyf", "twz", "kzf", "kzi", "kyi", "ti")

    @pl.loop(0, CHUNKS + 5)
    def _(t):
        pl.when(t < CHUNKS)(lambda: y_forward(t))
        pl.when(t + 2 < CHUNKS)(lambda: x_forward(t + 2))
        pl.when((t >= 2) & (t < CHUNKS + 2))(lambda: solve(t - 2))
        pl.when((t >= 4) & (t < CHUNKS + 4))(lambda: y_inverse(t - 4))
        pl.when(t == CHUNKS + 3)(neighbours)
        pl.when(t >= 5)(lambda: x_inverse(t - 5))

    for copy in stress_halos:
        copy.wait_send()
    for c in range(3):
        for layer, z in enumerate((0, 1, 14, 15)):
            zf[c, layer] = fluid[c, :, z, :]
    velocity_halos = halo_copies(4, fluid, 14, 0, vext, zf, vzh)
    for copy in velocity_halos:
        copy.start()

    inside = lane128.astype(F32) - 63.5
    blocks = []
    firsts, seconds = [], []
    for c in range(3):
        block = jnp.zeros((128, 128), F32)
        for b in range(4):
            block += exact_left(hott[b], fluid[c, :, :, 128 * b : 128 * b + 128].reshape(256, 128), 3)
        blocks.append(block)
        firsts.append(jnp.sum(block, axis=1, keepdims=True))
        seconds.append(jnp.sum(block * inside, axis=1, keepdims=True))
    rx, ry, rz = mgeo[:, 0:1], mgeo[:, 1:2], mgeo[:, 2:3]
    moments = jnp.zeros((128, 128), F32)
    for at, value in enumerate(
        (
            firsts[0],
            firsts[1],
            firsts[2],
            ry * firsts[2] - rz * firsts[1],
            rz * firsts[0] - (rx * firsts[2] + seconds[2]),
            rx * firsts[1] + seconds[1] - ry * firsts[0],
        )
    ):
        moments = jnp.where(lane128 == at, value, moments)
    gtile[1] = dot_exact(jnp.transpose(moments)[0:8], gather_runs)
    gather_cols(1, g3)
    gather_rows(1, g3, g4)
    wait_for(g4.at[pl.ds(0, ROWS - 1)], g_recv.at[3])
    parts = split(jnp.concatenate([g4[r] for r in range(ROWS)], axis=1), 3)
    parts = jnp.concatenate([part.astype(F32) for part in parts], axis=0).astype(BF16)
    totals = dot(match[...], parts, NT)
    totals = totals[:, 16:24] + totals[:, 8:16] + totals[:, 0:8]
    groups = jnp.concatenate([totals[32 * k : 32 * k + 32] for k in range(5)], axis=1)
    sums = dot_exact(gather_runs[:, 0:32], groups)
    rigid = rigid_of(sums[:, 0:8], mgeo)
    for c in range(3):
        fix = rigid[c] - blocks[c]
        for b in range(4):
            lanes = slice(128 * b, 128 * b + 128)
            done = fluid[c, :, :, lanes] + exact_left(hot[b], fix, 3).reshape(16, 16, 128)
            vext[c, 2:18, :, lanes] = done
    stores = [pltpu.make_async_copy(vext.at[c, 2:18], vext_out.at[c, 2:18], store_sem.at[c]) for c in range(3)]
    for store in stores:
        store.start()
    for copy in velocity_halos:
        copy.wait_recv()
    for k in range(4):
        rigid = rigid_of(sums[:, 8 * k + 8 : 8 * k + 16], nbcol[k])
        fix = exact_left(nbhot[k], jnp.concatenate(rigid, axis=1), 3)
        keep = nbkeep[k]
        ref, first = ((vzh, 0), (vzh, 2), (vext, 0), (vext, 18))[k]
        for c in range(3):
            for b in range(4):
                lanes, rows = slice(128 * b, 128 * b + 128), slice(32 * b, 32 * b + 32)
                old = ref[c, first : first + 2, :, lanes].reshape(32, 128)
                new = old * keep[rows] + fix[rows, 128 * c : 128 * c + 128]
                ref[c, first : first + 2, :, lanes] = new.reshape(2, 16, 128)
    late = [
        pltpu.make_async_copy(vext.at[:, 0:2], vext_out.at[:, 0:2], store_sem.at[3]),
        pltpu.make_async_copy(vext.at[:, 18:20], vext_out.at[:, 18:20], store_sem.at[4]),
        pltpu.make_async_copy(vzh, vzh_out, store_sem.at[5]),
    ]
    for store in late:
        store.start()
    stores += late

    for copy in velocity_halos + tile_copies():
        copy.wait_send()
    wait_for(g1.at[pl.ds(0, COLS - 1)], g_send.at[0])
    wait_for(g2.at[pl.ds(0, ROWS - 1)], g_send.at[1])
    wait_for(g3.at[pl.ds(0, COLS - 1)], g_send.at[2])
    wait_for(g4.at[pl.ds(0, ROWS - 1)], g_send.at[3])

    @pl.loop(0, CHUNKS)
    def _(j):
        wait_for(x1.at[j, pl.ds(0, ROWS - 1)], a_send.at[0, j])
        wait_for(y1.at[j, pl.ds(0, COLS - 1)], a_send.at[1, j])
        wait_for(z1.at[j, pl.ds(0, COLS - 1)], a_send.at[2, j])
        wait_for(y2.at[j, pl.ds(0, ROWS - 1)], a_send.at[3, j])

    for store in stores:
        store.wait()


def update(vlow, vhigh, vzh, mult, dzt, bzt, vel, new_aux, new_mult, *, lines):
    rows = 16 * lines
    edge = bzt[...]
    grads = []
    for c in range(3):
        both = jnp.concatenate([vlow[c], vhigh[c]], axis=0)
        field = both[2 : lines + 2]
        vel[c] = field
        dx = along_x(field.reshape(rows, NX))
        near = [both[k : lines + k].reshape(rows, NX) for k in (0, 1, 3, 4)]
        dy = centered(*near)
        dz = exact_left(dzt[...], field.reshape(rows, NX), 3) + exact_left(edge, vzh[c], 3)
        grads.append((dx, dy, dz * (1.0 / 12.0)))
    strain = (
        grads[0][0],
        grads[1][1],
        grads[2][2],
        (grads[0][1] + grads[1][0]) * 0.5,
        (grads[0][2] + grads[2][0]) * 0.5,
        (grads[1][2] + grads[2][1]) * 0.5,
    )
    old = [mult[k].reshape(rows, NX) for k in range(6)]
    q = [old[k] + PEN * strain[k] for k in range(6)]
    norm = jnp.sqrt(
        q[0] * q[0] + q[1] * q[1] + q[2] * q[2] + 2.0 * (q[3] * q[3] + q[4] * q[4] + q[5] * q[5])
    )
    factor = 1.0 - YIELD / jnp.maximum(norm, YIELD)
    for k in range(6):
        aux = factor * q[k] * (1.0 / PEN)
        new_aux[k] = aux.reshape(lines, 16, NX)
        new_mult[k] = (old[k] + PEN * (strain[k] - aux)).reshape(lines, 16, NX)


def local(force, mult, aux, entry_lines, entry_owner, entry_slot):
    t = make_tables()
    vm = pl.BlockSpec(memory_space=pltpu.VMEM)
    hbm = pl.BlockSpec(memory_space=pltpu.HBM)
    sems = pltpu.SemaphoreType.DMA
    names = ("tf", "ti", "kyf", "kyi", "kzf", "kzi", "twy", "twz", "dz", "bz")
    loads = [force, mult, aux] + [jnp.asarray(t[k]) for k in names]
    scratch = [pltpu.VMEM(a.shape, a.dtype) for a in loads] + [
        pltpu.VMEM((3, 20, 16, NX), F32),
        pltpu.VMEM((3, 4, 16, NX), F32),
        pltpu.VMEM((3, 4, 16, NX), F32),
        pltpu.VMEM((3, 20, 16, NX), F32),
        pltpu.VMEM((3, 4, 16, NX), F32),
        pltpu.VMEM((3, 256, NX), F32),
        pltpu.VMEM((2, 3, 256, NX), BF16),
        pltpu.VMEM((3, 16, 16, NX), F32),
        pltpu.VMEM((CHUNKS, ROWS, 3, 2 * MC, 256), F32),
        pltpu.VMEM((CHUNKS, ROWS, 3, 2 * MC, 256), F32),
        pltpu.VMEM((CHUNKS, COLS, 3, 2, MC, 128), F32),
        pltpu.VMEM((CHUNKS, COLS, 3, 2, MC, 128), F32),
        pltpu.VMEM((CHUNKS, COLS, 3, 2, MC, 128), F32),
        pltpu.VMEM((CHUNKS, COLS, 3, 2, MC, 128), F32),
        pltpu.VMEM((CHUNKS, ROWS, 3, 2 * MC, 256), F32),
        pltpu.VMEM((CHUNKS, ROWS, 3, 2 * MC, 256), F32),
        pltpu.VMEM((24 * MC, 512), F32),
        pltpu.VMEM((48 * MC, 256), F32),
        pltpu.VMEM((COLS, 8, 128), F32),
        pltpu.VMEM((ROWS, 8, 512), F32),
        pltpu.VMEM((COLS, 8, 128), F32),
        pltpu.VMEM((ROWS, 8, 512), F32),
        pltpu.VMEM((3, 8, 128), F32),
        pltpu.VMEM((160, 512 * ROWS), BF16),
        pltpu.VMEM((128, 128), F32),
        pltpu.VMEM((4, 256, 128), BF16),
        pltpu.VMEM((4, 128, 256), BF16),
        pltpu.VMEM((4, 8, 128), F32),
        pltpu.VMEM((4, 128, 8), F32),
        pltpu.VMEM((4, 128, 128), BF16),
        pltpu.VMEM((4, 128, 128), F32),
        sems((12,)),
        sems((12,)),
        sems((4, CHUNKS)),
        sems((4, CHUNKS)),
        sems((4,)),
        sems((4,)),
        sems((len(names) + 13,)),
        sems((6,)),
    ]
    vext, vzh = pl.pallas_call(
        kernel,
        out_shape=(
            jax.ShapeDtypeStruct((3, 20, 16, NX), F32),
            jax.ShapeDtypeStruct((3, 4, 16, NX), F32),
        ),
        in_specs=[hbm] * 3 + [vm] * 3 + [hbm] * len(names),
        out_specs=(hbm, hbm),
        scratch_shapes=scratch,
        compiler_params=pltpu.CompilerParams(
            collective_id=0, has_side_effects=True, vmem_limit_bytes=58 * 2**20
        ),
    )(
        force,
        mult,
        aux,
        entry_lines.reshape(1, 128),
        entry_owner.reshape(1, 128),
        entry_slot.reshape(1, 128),
        *loads[3:],
    )

    lines = 4
    whole = lambda *shape: pl.BlockSpec(shape, lambda i: (0,) * len(shape))
    part = lambda n: pl.BlockSpec((n, lines, 16, NX), lambda i: (0, i, 0, 0))
    return tuple(
        pl.pallas_call(
            functools.partial(update, lines=lines),
            grid=(16 // lines,),
            out_shape=tuple(jax.ShapeDtypeStruct((n, 16, 16, NX), F32) for n in (3, 6, 6)),
            in_specs=[
                part(3),
                pl.BlockSpec((3, lines, 16, NX), lambda i: (0, i + 1, 0, 0)),
                whole(3, 64, NX),
                part(6),
                whole(16 * lines, 16 * lines),
                pl.BlockSpec((16 * lines, 64), lambda i: (i, 0)),
            ],
            out_specs=tuple(part(n) for n in (3, 6, 6)),
            compiler_params=pltpu.CompilerParams(vmem_limit_bytes=58 * 2**20),
        )(
            vext,
            vext,
            vzh.reshape(3, 64, NX),
            mult,
            jnp.asarray(deriv_rows(lines).astype(jnp.bfloat16)),
            jnp.asarray(t["bz"]),
        )
    )


def solution(mesh):
    field = P(None, "row", "col", None)
    return jax.shard_map(
        local,
        mesh=mesh,
        in_specs=(field, field, field, P(("row", "col")), P(("row", "col"), None), P(("row", "col"))),
        out_specs=(field, field, field),
        check_vma=False,
    )
```

```python
import functools
import math

import jax
import jax.numpy as jnp
import numpy as np
from jax import lax
from jax.experimental import pallas as pl
from jax.experimental.pallas import tpu as pltpu
from jax.sharding import PartitionSpec as P

MASS, VISC, PEN, YIELD = 0.02, 10.0, 5.0, 2.0
NPD = 72
NX, NY, NZ = 512, 128, 256
ROWS, COLS = 8, 16
CHUNKS = 4
MC = 32 // CHUNKS
F32, BF16 = jnp.float32, jnp.bfloat16
MESH = pl.DeviceIdType.MESH
HIGHEST = lax.Precision.HIGHEST
NN = (((1,), (0,)), ((), ()))
NT = (((1,), (1,)), ((), ()))

FAR = (
    (2, 2), (2, 1), (1, 2), (2, 3), (3, 2), (1, 1), (3, 3), (1, 3), (3, 1),
    (2, 0), (0, 2), (1, 0), (0, 1), (3, 0), (0, 3),
)

YCOMP = (3, 1, 5)
ZCOMP = (4, 5, 2)
XCOMP = (0, 3, 4)


def pieces_np(table, count):
    out = []
    rest = np.asarray(table, np.float64)
    for _ in range(count):
        piece = rest.astype(jnp.bfloat16)
        out.append(piece)
        rest = rest - piece.astype(np.float64)
    return np.stack(out)


def kron_dft(points, batch, sign):
    index = np.arange(points)
    angle = sign * 2 * np.pi * (np.outer(index, index) % points) / points
    eye = np.eye(batch)
    cos, sin = np.kron(np.cos(angle), eye), np.kron(np.sin(angle), eye)
    return np.block([[cos, sin], [-sin, cos]])


def kron_dft_z(sign):
    index = np.arange(16)
    angle = sign * 2 * np.pi * (np.outer(index, index) % 16) / 16
    eye = np.eye(8)
    cos, sin = np.kron(eye, np.cos(angle)), np.kron(eye, np.sin(angle))
    return np.block([[cos, sin], [-sin, cos]])


def mode_table():
    chunk, dest, part, inner = np.meshgrid(
        np.arange(CHUNKS), np.arange(ROWS), np.arange(2), np.arange(MC), indexing="ij"
    )
    mode = 32 * dest + MC * chunk + inner
    return mode.reshape(CHUNKS, -1), part.reshape(CHUNKS, -1)


def make_tables():
    mode, part = mode_table()
    x = np.arange(NX)
    angle = 2 * np.pi * ((mode[..., None] * x) % NX) / NX
    fwd = np.where(part[..., None] == 0, np.cos(angle), -np.sin(angle))
    weight = np.where(mode == 0, 1.0, 2.0)[..., None] / float(NX * NY * NZ)
    inv = weight * fwd
    ky_f = pieces_np(kron_dft(16, 16, -1), 2)
    ky_i = pieces_np(kron_dft(16, 16, 1), INV)
    kz_f = pieces_np(kron_dft_z(-1), 2)
    kz_i = pieces_np(kron_dft_z(1), INV)
    lane = np.arange(256)
    turn_y = 2 * np.pi * np.outer(np.arange(8), lane // 16) / NY
    turn_z = 2 * np.pi * np.outer(np.arange(16), np.arange(128) % 16) / NZ
    two_y = np.stack([np.cos(turn_y), np.sin(turn_y)]).astype(np.float32)
    two_z = np.stack([np.cos(turn_z), np.sin(turn_z)]).astype(np.float32)
    return {
        "tf": pieces_np(fwd, 2),
        "ti": pieces_np(inv, INV),
        "kyf": ky_f,
        "kyi": ky_i,
        "kzf": kz_f,
        "kzi": kz_i,
        "twy": two_y,
        "twz": two_z,
        "dz": deriv_rows(16).astype(jnp.bfloat16),
        "bz": deriv_halo().astype(jnp.bfloat16),
    }


INV = 3


def deriv_rows(lines):
    one = np.zeros((16, 16))
    for offset, coef in ((1, 8), (-1, -8), (2, -1), (-2, 1)):
        one += coef * np.eye(16, k=offset)
    return np.kron(np.eye(lines), one)


def deriv_halo():
    out = np.zeros((16, 16, 4, 16))
    for y in range(16):
        for layer, place in enumerate((-2, -1, 16, 17)):
            for z in range(16):
                out[y, z, layer, y] = {1: 8, -1: -8, 2: -1, -2: 1}.get(place - z, 0)
    return out.reshape(256, 64)


def split(value, count):
    out = []
    for step in range(count):
        piece = value.astype(BF16)
        out.append(piece)
        if step + 1 < count:
            value = value - piece.astype(F32)
    return out


def dot(a, b, dims=NN):
    return lax.dot_general(a, b, dims, preferred_element_type=F32)


def dot_exact(a, b, dims=NN):
    return lax.dot_general(a, b, dims, precision=HIGHEST, preferred_element_type=F32)


def product(a, b, dims=NN):
    count = len(a)
    total = None
    for i in range(count - 1, -1, -1):
        for j in range(count - 1 - i, -1, -1):
            term = dot(a[i], b[j], dims)
            total = term if total is None else total + term
    return total


def exact_left(a, value, count):
    total = None
    for piece in reversed(split(value, count)):
        term = dot(a, piece)
        total = term if total is None else total + term
    return total


def fft(xs, sign):
    count = len(xs)
    if count == 1:
        return xs
    even, odd = fft(xs[0::2], sign), fft(xs[1::2], sign)
    out = [None] * count
    half = count // 2
    for k in range(half):
        re, im = odd[k]
        if k == 0:
            tr, ti = re, im
        elif 4 * k == count:
            tr, ti = (-im, re) if sign > 0 else (im, -re)
        else:
            c = math.cos(2 * math.pi * k / count)
            s = sign * math.sin(2 * math.pi * k / count)
            tr, ti = re * c - im * s, re * s + im * c
        er, ei = even[k]
        out[k] = (er + tr, ei + ti)
        out[k + half] = (er - tr, ei - ti)
    return out


def along_x(field):
    axis = field.ndim - 1
    up1, up2 = pltpu.roll(field, NX - 1, axis), pltpu.roll(field, NX - 2, axis)
    lo1, lo2 = pltpu.roll(field, 1, axis), pltpu.roll(field, 2, axis)
    return (8.0 * (up1 - lo1) - (up2 - lo2)) * (1.0 / 12.0)


def centered(lo2, lo1, up1, up2):
    return (8.0 * (up1 - lo1) - (up2 - lo2)) * (1.0 / 12.0)


def kernel(
    force_in, mult_in, aux_in, lines_in, owner_in, slot_in,
    tf_in, ti_in, kyf_in, kyi_in, kzf_in, kzi_in, twy_in, twz_in, dzt_in, bzt_in,
    vext_out, vzh_out,
    force, mult, aux, tf, ti, kyf, kyi, kzf, kzi, twy, twz, dzt, bzt,
    yext, zf, zh, vext, vzh, rhs, rpieces, fluid,
    x1, r1, y1, r2, z1, r3, y2, r4, ascr, bscr,
    g1, g2, g3, g4, gtile, match, mgeo, hot, hott, nbtile, nbcol, nbhot, nbkeep,
    halo_send, halo_recv, a_send, a_recv, g_send, g_recv, load_sem, store_sem,
):
    row, col = lax.axis_index("row"), lax.axis_index("col")

    def row_peer(off):
        return lax.rem(row + off, ROWS)

    def col_peer(off):
        return lax.rem(col + off, COLS)

    def remote(src, dst, send, recv, device):
        return pltpu.make_async_remote_copy(
            src_ref=src, dst_ref=dst, send_sem=send, recv_sem=recv,
            device_id=device, device_id_type=MESH,
        )

    def wait_for(ref, sem):
        pltpu.make_async_copy(ref, ref, sem).wait()

    loads = {}

    def load(name, src, dst):
        loads[name] = pltpu.make_async_copy(src, dst, load_sem.at[len(loads)])
        loads[name].start()

    for comp in (4, 5, 2, 3, 1):
        load(("mult", comp), mult_in.at[comp], mult.at[comp])
        load(("aux", comp), aux_in.at[comp], aux.at[comp])
    load("dzt", dzt_in, dzt)
    load("bzt", bzt_in, bzt)
    load(("mult", 0), mult_in.at[0], mult.at[0])
    load(("aux", 0), aux_in.at[0], aux.at[0])
    load("force", force_in, force)
    for name, src, dst in (
        ("tf", tf_in, tf), ("twy", twy_in, twy), ("kyf", kyf_in, kyf), ("twz", twz_in, twz),
        ("kzf", kzf_in, kzf), ("kzi", kzi_in, kzi), ("kyi", kyi_in, kyi), ("ti", ti_in, ti),
    ):
        load(name, src, dst)

    def loaded(*names):
        for name in names:
            loads.pop(name).wait()

    barrier = pltpu.get_barrier_semaphore()
    for off in range(1, ROWS):
        pl.semaphore_signal(barrier, inc=1, device_id=(row_peer(off), col), device_id_type=MESH)
    for off in range(1, COLS):
        pl.semaphore_signal(barrier, inc=1, device_id=(row, col_peer(off)), device_id_type=MESH)

    def shifted(comp):
        return mult[comp] - PEN * aux[comp]

    for i, comp in enumerate(ZCOMP):
        loaded(("mult", comp), ("aux", comp))
        for layer, z in enumerate((0, 1, 14, 15)):
            zf[i, layer] = mult[comp, :, z, :] - PEN * aux[comp, :, z, :]
    pl.semaphore_wait(barrier, ROWS + COLS - 2)

    def halo_copies(base, ysrc, high, low, ydst, zsrc, zdst):
        up, down = (row_peer(1), col), (row_peer(ROWS - 1), col)
        right, left = (row, col_peer(1)), (row, col_peer(COLS - 1))
        sems = [(halo_send.at[base + k], halo_recv.at[base + k]) for k in range(4)]
        return [
            remote(zsrc.at[:, 2:4], zdst.at[:, 0:2], *sems[0], right),
            remote(zsrc.at[:, 0:2], zdst.at[:, 2:4], *sems[1], left),
            remote(ysrc.at[:, high : high + 2], ydst.at[:, 0:2], *sems[2], up),
            remote(ysrc.at[:, low : low + 2], ydst.at[:, 18:20], *sems[3], down),
        ]

    stress_halos = halo_copies(0, yext, 16, 2, yext, zf, zh)
    for copy in stress_halos[0:2]:
        copy.start()
    for i, comp in enumerate(YCOMP):
        if comp != 5:
            loaded(("mult", comp), ("aux", comp))
        yext[i, 2:18] = shifted(comp)
    for copy in stress_halos[2:4]:
        copy.start()

    lane128 = lax.broadcasted_iota(jnp.int32, (1, 128), 1)
    lines, block_x = lines_in[...], lines_in[...] & 3
    particle = owner_in[...] * NPD + slot_in[...]
    gy = ((lines >> 6) + row * 16).astype(F32)
    gz = (((lines >> 2) & 15) + col * 16).astype(F32)
    fields = jnp.concatenate(
        [
            particle.astype(F32),
            (block_x * 128).astype(F32),
            gy,
            gz,
            gy * gy,
            gz * gz,
            (lines >> 2).astype(F32),
            block_x.astype(F32),
        ],
        axis=0,
    )
    pair = lax.broadcasted_iota(jnp.int32, (128, 128), 0)
    runs_lane = lax.broadcasted_iota(jnp.int32, (128, 128), 1)
    gather_runs = (pair // 4 == runs_lane).astype(F32)
    spread_runs = (runs_lane // 4 == pair).astype(F32)
    sums = dot_exact(fields, gather_runs)
    mean_y, mean_z = sums[2:3] * 0.25, sums[3:4] * 0.25
    inner = 4.0 * 174752.0 + 128.0 * (
        sums[4:5] - 4.0 * mean_y * mean_y + sums[5:6] - 4.0 * mean_z * mean_z
    )
    gtile[0] = jnp.concatenate(
        [sums[0:1] * 0.25, sums[1:2] * 0.25 + 63.5, mean_y, mean_z, inner, jnp.zeros((3, 128), F32)], axis=0
    )

    def gather_cols(slot, buf):
        buf[col] = gtile[slot]
        for dy, dz in FAR:
            peer = 4 * lax.rem(col // 4 + dz, 4) + lax.rem(col % 4 + dy, 4)
            remote(gtile.at[slot], buf.at[col], g_send.at[2 * slot], g_recv.at[2 * slot], (row, peer)).start()

    def gather_rows(slot, buf, wide):
        wait_for(buf.at[pl.ds(0, COLS - 1)], g_recv.at[2 * slot])
        parts = []
        for q in range(4):
            total = None
            for k in range(4):
                tile = jnp.where(runs_lane[0:8] < 32, buf[4 * q + k], 0.0)
                tile = pltpu.roll(tile, 32 * k, 1) if k else tile
                total = tile if total is None else total + tile
            parts.append(total)
        wide[row] = jnp.concatenate(parts, axis=1)
        for off in range(1, ROWS):
            remote(
                wide.at[row], wide.at[row], g_send.at[2 * slot + 1], g_recv.at[2 * slot + 1], (row_peer(off), col)
            ).start()

    gather_cols(0, g1)

    loaded("dzt", "bzt", ("mult", 0), ("aux", 0), "force")
    for c, comp in enumerate(XCOMP):
        rhs[c] = (force[c] + along_x(shifted(comp))).reshape(256, NX)
    fluid[...] = jnp.zeros_like(fluid)
    for c, comp in enumerate(ZCOMP):
        own = shifted(comp).reshape(256, NX)
        rhs[c] += exact_left(dzt[...], own, 2) * (1.0 / 12.0)
    gather_rows(0, g1, g2)
    for copy in stress_halos:
        copy.wait_recv()
    for c in range(3):
        along_y = centered(yext[c, 0:16], yext[c, 1:17], yext[c, 3:19], yext[c, 4:20]).reshape(256, NX)
        edge = exact_left(bzt[...], zh[c].reshape(64, NX), 2) * (1.0 / 12.0)
        high, low = split(rhs[c] + along_y + edge, 2)
        rpieces[0, c] = high
        rpieces[1, c] = low

    def send_rows(stage, j, src, dst):
        dst[j, row] = src[j, row]
        for off in range(1, ROWS):
            peer = row_peer(off)
            remote(src.at[j, peer], dst.at[j, row], a_send.at[stage, j], a_recv.at[stage, j], (peer, col)).start()

    def send_cols(stage, j, src, dst):
        dst[j, col] = src[j, col]
        for dy, dz in FAR:
            peer = 4 * lax.rem(col // 4 + dz, 4) + lax.rem(col % 4 + dy, 4)
            remote(src.at[j, peer], dst.at[j, col], a_send.at[stage, j], a_recv.at[stage, j], (row, peer)).start()

    def await_all(stage, j, dst, count):
        wait_for(dst.at[j, pl.ds(0, count - 1)], a_recv.at[stage, j])

    def x_forward(j):
        for c in range(3):
            out = product([tf[0, j], tf[1, j]], [rpieces[0, c], rpieces[1, c]], NT)
            x1[j, :, c] = out.reshape(ROWS, 2 * MC, 256)
        send_rows(0, j, x1, r1)

    def y_forward(j):
        await_all(0, j, r1, ROWS)
        for c in range(3):
            xs = [(r1[j, s, c, 0:MC], r1[j, s, c, MC : 2 * MC]) for s in range(8)]
            for k, (re, im) in enumerate(fft(xs, -1)):
                cos, sin = twy[0, k : k + 1], twy[1, k : k + 1]
                at = k * 3 * MC + c * MC
                ascr[at : at + MC, 0:256] = re * cos + im * sin
                ascr[at : at + MC, 256:512] = im * cos - re * sin
        out = product(split(ascr[...], 2), [kyf[0], kyf[1]]).reshape(8, 3, MC, 512)
        for half in range(2):
            for part in range(2):
                at = 256 * part + 128 * half
                y1[j, pl.ds(half, 8, 2), :, part] = out[:, :, :, at : at + 128]
        send_cols(1, j, y1, r2)

    def solve(j):
        await_all(1, j, r2, COLS)
        for c in range(3):
            xs = [(r2[j, s, c, 0], r2[j, s, c, 1]) for s in range(16)]
            for k, (re, im) in enumerate(fft(xs, -1)):
                cos, sin = twz[0, k : k + 1], twz[1, k : k + 1]
                at = k * 3 * MC + c * MC
                bscr[at : at + MC, 0:128] = re * cos + im * sin
                bscr[at : at + MC, 128:256] = im * cos - re * sin
        bscr[...] = product(split(bscr[...], 2), [kzf[0], kzf[1]])
        mode = row * 32 + j * MC + lax.broadcasted_iota(jnp.int32, (MC, 128), 0)
        lanes = lax.broadcasted_iota(jnp.int32, (MC, 128), 1)
        wave_x = mode.astype(F32) * (2.0 * math.pi / NX)
        index_y = col // 2 + 8 * (8 * lax.rem(col, 2) + lanes // 16)
        wave_y = jnp.where(index_y < NY // 2, index_y, index_y - NY).astype(F32) * (2.0 * math.pi / NY)
        keep_y = (index_y != NY // 2).astype(F32)
        for k in range(16):
            index_z = k + 16 * (lanes % 16)
            wave_z = jnp.where(index_z < NZ // 2, index_z, index_z - NZ).astype(F32) * (2.0 * math.pi / NZ)
            keep = keep_y * (index_z != NZ // 2).astype(F32)
            ksq = wave_x * wave_x + wave_y * wave_y + wave_z * wave_z
            inverse = 1.0 / jnp.where(ksq > 0, ksq, 1.0)
            gain = keep / (MASS + VISC * ksq)
            for part in range(2):
                at = 3 * MC * k
                lane = slice(128 * part, 128 * part + 128)
                fx, fy, fz = (bscr[at + MC * c : at + MC * c + MC, lane] for c in range(3))
                dotk = (wave_x * fx + wave_y * fy + wave_z * fz) * inverse
                bscr[at : at + MC, lane] = (fx - wave_x * dotk) * gain
                bscr[at + MC : at + 2 * MC, lane] = (fy - wave_y * dotk) * gain
                bscr[at + 2 * MC : at + 3 * MC, lane] = (fz - wave_z * dotk) * gain
        bscr[...] = product(split(bscr[...], INV), [kzi[p] for p in range(INV)])
        for c in range(3):
            xs = []
            for k in range(16):
                cos, sin = twz[0, k : k + 1], twz[1, k : k + 1]
                at = k * 3 * MC + c * MC
                re, im = bscr[at : at + MC, 0:128], bscr[at : at + MC, 128:256]
                xs.append((re * cos - im * sin, im * cos + re * sin))
            for s, (re, im) in enumerate(fft(xs, 1)):
                z1[j, s, c, 0] = re
                z1[j, s, c, 1] = im
        send_cols(2, j, z1, r3)

    def y_inverse(j):
        await_all(2, j, r3, COLS)
        for half in range(2):
            for part in range(2):
                at = 256 * part + 128 * half
                ascr[:, at : at + 128] = r3[j, pl.ds(half, 8, 2), :, part].reshape(8 * 3 * MC, 128)
        ascr[...] = product(split(ascr[...], INV), [kyi[p] for p in range(INV)])
        for c in range(3):
            xs = []
            for k in range(8):
                cos, sin = twy[0, k : k + 1], twy[1, k : k + 1]
                at = k * 3 * MC + c * MC
                re, im = ascr[at : at + MC, 0:256], ascr[at : at + MC, 256:512]
                xs.append((re * cos - im * sin, im * cos + re * sin))
            for s, (re, im) in enumerate(fft(xs, 1)):
                y2[j, s, c, 0:MC] = re
                y2[j, s, c, MC : 2 * MC] = im
        send_rows(3, j, y2, r4)

    def x_inverse(j):
        await_all(3, j, r4, ROWS)
        for c in range(3):
            spectrum = jnp.transpose(r4[j, :, c].reshape(2 * MC * ROWS, 256))
            out = product(split(spectrum, INV), [ti[p, j] for p in range(INV)])
            fluid[c] += out.reshape(16, 16, NX)

    def tile_copies():
        peers = ((row, col_peer(1)), (row, col_peer(COLS - 1)), (row_peer(1), col), (row_peer(ROWS - 1), col))
        return [
            remote(gtile.at[2], nbtile.at[k], halo_send.at[8 + k], halo_recv.at[8 + k], peer)
            for k, peer in enumerate(peers)
        ]

    def neighbours():
        for copy in tile_copies():
            copy.wait_recv()
        for k in range(4):
            tile = nbtile[k]
            nbcol[k] = dot_exact((pair == runs_lane).astype(F32), tile, NT)
            ids = dot_exact(spread_runs[0:32], tile, NT)[:, 5:6] * 0.25
            for r in range(ROWS):
                same = (ids == g2[r, 0:1]).astype(F32)
                match[32 + 32 * k : 64 + 32 * k, 512 * r : 512 * r + 512] = same.astype(BF16)
            line, block = tile[3:4], tile[4:5]
            y = jnp.floor(line * (1.0 / 16.0))
            z = line - 16.0 * y
            layer, along = (z, y) if k < 2 else (y, z)
            layer = layer - (14.0 if k % 2 == 0 else 0.0)
            inside = (layer >= 0.0) & (layer <= 1.0)
            target = jnp.where(inside, block * 32.0 + layer * 16.0 + along, -1.0)
            hits = (target == pair.astype(F32)).astype(F32)
            nbhot[k] = hits.astype(BF16)
            nbkeep[k] = jnp.broadcast_to(1.0 - jnp.sum(hits, axis=1, keepdims=True), (128, 128))

    def rigid_of(sums, cols):
        rx, ry, rz, mean, turn = (cols[:, k : k + 1] for k in (0, 1, 2, 6, 7))
        vx, vy, vz = (sums[:, k : k + 1] * mean for k in range(3))
        wx, wy, wz = (sums[:, k : k + 1] * turn for k in range(3, 6))
        cell_x = rx + (lane128.astype(F32) - 63.5)
        return (
            jnp.broadcast_to(vx + wy * rz - wz * ry, (128, 128)),
            vy + wz * cell_x - wx * rz,
            vz + wx * ry - wy * cell_x,
        )

    def geometry():
        wait_for(g2.at[pl.ds(0, ROWS - 1)], g_recv.at[1])
        own = dot_exact(spread_runs[0:32], fields, NT) * 0.25
        ids = own[:, 0:1]
        count = jnp.zeros((32, 1), F32)
        cx, cy, cz = count, count, count
        sames = []
        for r in range(ROWS):
            block = g2[r]
            same = (ids == block[0:1]).astype(F32)
            match[0:32, 512 * r : 512 * r + 512] = same.astype(BF16)
            sames.append(same)
            count += jnp.sum(same, axis=1, keepdims=True)
            cx += jnp.sum(same * block[1:2], axis=1, keepdims=True)
            cy += jnp.sum(same * block[2:3], axis=1, keepdims=True)
            cz += jnp.sum(same * block[3:4], axis=1, keepdims=True)
        safe = jnp.maximum(count, 1.0)
        cx, cy, cz = cx / safe, cy / safe, cz / safe
        spread = jnp.zeros((32, 1), F32)
        for r in range(ROWS):
            block = g2[r]
            dx, dy, dz = block[1:2] - cx, block[2:3] - cy, block[3:4] - cz
            inner_spread = block[4:5] + 512.0 * (dx * dx + dy * dy + dz * dz)
            spread += jnp.sum(sames[r] * inner_spread, axis=1, keepdims=True)
        inertia = jnp.maximum(spread * (2.0 / 3.0), 1.0)
        place = lane128
        packed = jnp.where(place == 0, 1.0 / jnp.maximum(512.0 * count, 1.0), 0.0)
        for at, value in ((1, cx), (2, cy), (3, cz), (4, 1.0 / inertia)):
            packed = jnp.where(place == at, value, packed)
        mine = dot_exact((pair == runs_lane).astype(F32), fields, NT)
        centers = dot_exact(gather_runs[:, 0:32], packed)
        rel = jnp.where(place == 0, mine[:, 1:2] + 63.5 - centers[:, 1:2], 0.0)
        rel = jnp.where(place == 1, mine[:, 2:3] - centers[:, 2:3], rel)
        rel = jnp.where(place == 2, mine[:, 3:4] - centers[:, 3:4], rel)
        for at, value in enumerate((mine[:, 6:7], mine[:, 7:8], mine[:, 0:1], centers[:, 0:1], centers[:, 4:5])):
            rel = jnp.where(place == 3 + at, value, rel)
        mgeo[...] = rel
        gtile[2] = jnp.transpose(rel)[0:8]
        for copy in tile_copies():
            copy.start()
        rows256 = lax.broadcasted_iota(jnp.int32, (256, 128), 0).astype(F32)
        cols256 = lax.broadcasted_iota(jnp.int32, (128, 256), 1).astype(F32)
        for b in range(4):
            hot[b] = ((fields[6:7] == rows256) & (fields[7:8] == float(b))).astype(F32).astype(BF16)
            hott[b] = ((mine[:, 6:7] == cols256) & (mine[:, 7:8] == float(b))).astype(F32).astype(BF16)

    loaded("tf")
    x_forward(0)
    x_forward(1)
    geometry()
    loaded("twy", "kyf", "twz", "kzf", "kzi", "kyi", "ti")

    @pl.loop(0, CHUNKS + 5)
    def _(t):
        pl.when(t < CHUNKS)(lambda: y_forward(t))
        pl.when(t + 2 < CHUNKS)(lambda: x_forward(t + 2))
        pl.when((t >= 2) & (t < CHUNKS + 2))(lambda: solve(t - 2))
        pl.when((t >= 4) & (t < CHUNKS + 4))(lambda: y_inverse(t - 4))
        pl.when(t == CHUNKS + 3)(neighbours)
        pl.when(t >= 5)(lambda: x_inverse(t - 5))

    for copy in stress_halos:
        copy.wait_send()
    for c in range(3):
        for layer, z in enumerate((0, 1, 14, 15)):
            zf[c, layer] = fluid[c, :, z, :]
    velocity_halos = halo_copies(4, fluid, 14, 0, vext, zf, vzh)
    for copy in velocity_halos:
        copy.start()

    inside = lane128.astype(F32) - 63.5
    blocks = []
    firsts, seconds = [], []
    for c in range(3):
        block = jnp.zeros((128, 128), F32)
        for b in range(4):
            block += exact_left(hott[b], fluid[c, :, :, 128 * b : 128 * b + 128].reshape(256, 128), 3)
        blocks.append(block)
        firsts.append(jnp.sum(block, axis=1, keepdims=True))
        seconds.append(jnp.sum(block * inside, axis=1, keepdims=True))
    rx, ry, rz = mgeo[:, 0:1], mgeo[:, 1:2], mgeo[:, 2:3]
    moments = jnp.zeros((128, 128), F32)
    for at, value in enumerate(
        (
            firsts[0],
            firsts[1],
            firsts[2],
            ry * firsts[2] - rz * firsts[1],
            rz * firsts[0] - (rx * firsts[2] + seconds[2]),
            rx * firsts[1] + seconds[1] - ry * firsts[0],
        )
    ):
        moments = jnp.where(lane128 == at, value, moments)
    gtile[1] = dot_exact(jnp.transpose(moments)[0:8], gather_runs)
    gather_cols(1, g3)
    gather_rows(1, g3, g4)
    wait_for(g4.at[pl.ds(0, ROWS - 1)], g_recv.at[3])
    parts = split(jnp.concatenate([g4[r] for r in range(ROWS)], axis=1), 3)
    parts = jnp.concatenate([part.astype(F32) for part in parts], axis=0).astype(BF16)
    totals = dot(match[...], parts, NT)
    totals = totals[:, 16:24] + totals[:, 8:16] + totals[:, 0:8]
    groups = jnp.concatenate([totals[32 * k : 32 * k + 32] for k in range(5)], axis=1)
    sums = dot_exact(gather_runs[:, 0:32], groups)
    rigid = rigid_of(sums[:, 0:8], mgeo)
    for c in range(3):
        fix = rigid[c] - blocks[c]
        for b in range(4):
            lanes = slice(128 * b, 128 * b + 128)
            done = fluid[c, :, :, lanes] + exact_left(hot[b], fix, 3).reshape(16, 16, 128)
            vext[c, 2:18, :, lanes] = done
    stores = [pltpu.make_async_copy(vext.at[c, 2:18], vext_out.at[c, 2:18], store_sem.at[c]) for c in range(3)]
    for store in stores:
        store.start()
    for copy in velocity_halos:
        copy.wait_recv()
    for k in range(4):
        rigid = rigid_of(sums[:, 8 * k + 8 : 8 * k + 16], nbcol[k])
        fix = exact_left(nbhot[k], jnp.concatenate(rigid, axis=1), 3)
        keep = nbkeep[k]
        ref, first = ((vzh, 0), (vzh, 2), (vext, 0), (vext, 18))[k]
        for c in range(3):
            for b in range(4):
                lanes, rows = slice(128 * b, 128 * b + 128), slice(32 * b, 32 * b + 32)
                old = ref[c, first : first + 2, :, lanes].reshape(32, 128)
                new = old * keep[rows] + fix[rows, 128 * c : 128 * c + 128]
                ref[c, first : first + 2, :, lanes] = new.reshape(2, 16, 128)
    late = [
        pltpu.make_async_copy(vext.at[:, 0:2], vext_out.at[:, 0:2], store_sem.at[3]),
        pltpu.make_async_copy(vext.at[:, 18:20], vext_out.at[:, 18:20], store_sem.at[4]),
        pltpu.make_async_copy(vzh, vzh_out, store_sem.at[5]),
    ]
    for store in late:
        store.start()
    stores += late

    for copy in velocity_halos + tile_copies():
        copy.wait_send()
    wait_for(g1.at[pl.ds(0, COLS - 1)], g_send.at[0])
    wait_for(g2.at[pl.ds(0, ROWS - 1)], g_send.at[1])
    wait_for(g3.at[pl.ds(0, COLS - 1)], g_send.at[2])
    wait_for(g4.at[pl.ds(0, ROWS - 1)], g_send.at[3])

    @pl.loop(0, CHUNKS)
    def _(j):
        wait_for(x1.at[j, pl.ds(0, ROWS - 1)], a_send.at[0, j])
        wait_for(y1.at[j, pl.ds(0, COLS - 1)], a_send.at[1, j])
        wait_for(z1.at[j, pl.ds(0, COLS - 1)], a_send.at[2, j])
        wait_for(y2.at[j, pl.ds(0, ROWS - 1)], a_send.at[3, j])

    for store in stores:
        store.wait()


def update(vlow, vhigh, vzh, mult, dzt, bzt, vel, new_aux, new_mult, *, lines):
    rows = 16 * lines
    edge = bzt[...]
    grads = []
    for c in range(3):
        both = jnp.concatenate([vlow[c], vhigh[c]], axis=0)
        field = both[2 : lines + 2]
        vel[c] = field
        dx = along_x(field.reshape(rows, NX))
        near = [both[k : lines + k].reshape(rows, NX) for k in (0, 1, 3, 4)]
        dy = centered(*near)
        dz = exact_left(dzt[...], field.reshape(rows, NX), 3) + exact_left(edge, vzh[c], 3)
        grads.append((dx, dy, dz * (1.0 / 12.0)))
    strain = (
        grads[0][0],
        grads[1][1],
        grads[2][2],
        (grads[0][1] + grads[1][0]) * 0.5,
        (grads[0][2] + grads[2][0]) * 0.5,
        (grads[1][2] + grads[2][1]) * 0.5,
    )
    old = [mult[k].reshape(rows, NX) for k in range(6)]
    q = [old[k] + PEN * strain[k] for k in range(6)]
    norm = jnp.sqrt(
        q[0] * q[0] + q[1] * q[1] + q[2] * q[2] + 2.0 * (q[3] * q[3] + q[4] * q[4] + q[5] * q[5])
    )
    factor = 1.0 - YIELD / jnp.maximum(norm, YIELD)
    for k in range(6):
        aux = factor * q[k] * (1.0 / PEN)
        new_aux[k] = aux.reshape(lines, 16, NX)
        new_mult[k] = (old[k] + PEN * (strain[k] - aux)).reshape(lines, 16, NX)


def local(force, mult, aux, entry_lines, entry_owner, entry_slot):
    t = make_tables()
    vm = pl.BlockSpec(memory_space=pltpu.VMEM)
    hbm = pl.BlockSpec(memory_space=pltpu.HBM)
    sems = pltpu.SemaphoreType.DMA
    names = ("tf", "ti", "kyf", "kyi", "kzf", "kzi", "twy", "twz", "dz", "bz")
    loads = [force, mult, aux] + [jnp.asarray(t[k]) for k in names]
    scratch = [pltpu.VMEM(a.shape, a.dtype) for a in loads] + [
        pltpu.VMEM((3, 20, 16, NX), F32),
        pltpu.VMEM((3, 4, 16, NX), F32),
        pltpu.VMEM((3, 4, 16, NX), F32),
        pltpu.VMEM((3, 20, 16, NX), F32),
        pltpu.VMEM((3, 4, 16, NX), F32),
        pltpu.VMEM((3, 256, NX), F32),
        pltpu.VMEM((2, 3, 256, NX), BF16),
        pltpu.VMEM((3, 16, 16, NX), F32),
        pltpu.VMEM((CHUNKS, ROWS, 3, 2 * MC, 256), F32),
        pltpu.VMEM((CHUNKS, ROWS, 3, 2 * MC, 256), F32),
        pltpu.VMEM((CHUNKS, COLS, 3, 2, MC, 128), F32),
        pltpu.VMEM((CHUNKS, COLS, 3, 2, MC, 128), F32),
        pltpu.VMEM((CHUNKS, COLS, 3, 2, MC, 128), F32),
        pltpu.VMEM((CHUNKS, COLS, 3, 2, MC, 128), F32),
        pltpu.VMEM((CHUNKS, ROWS, 3, 2 * MC, 256), F32),
        pltpu.VMEM((CHUNKS, ROWS, 3, 2 * MC, 256), F32),
        pltpu.VMEM((24 * MC, 512), F32),
        pltpu.VMEM((48 * MC, 256), F32),
        pltpu.VMEM((COLS, 8, 128), F32),
        pltpu.VMEM((ROWS, 8, 512), F32),
        pltpu.VMEM((COLS, 8, 128), F32),
        pltpu.VMEM((ROWS, 8, 512), F32),
        pltpu.VMEM((3, 8, 128), F32),
        pltpu.VMEM((160, 512 * ROWS), BF16),
        pltpu.VMEM((128, 128), F32),
        pltpu.VMEM((4, 256, 128), BF16),
        pltpu.VMEM((4, 128, 256), BF16),
        pltpu.VMEM((4, 8, 128), F32),
        pltpu.VMEM((4, 128, 8), F32),
        pltpu.VMEM((4, 128, 128), BF16),
        pltpu.VMEM((4, 128, 128), F32),
        sems((12,)),
        sems((12,)),
        sems((4, CHUNKS)),
        sems((4, CHUNKS)),
        sems((4,)),
        sems((4,)),
        sems((len(names) + 13,)),
        sems((6,)),
    ]
    vext, vzh = pl.pallas_call(
        kernel,
        out_shape=(
            jax.ShapeDtypeStruct((3, 20, 16, NX), F32),
            jax.ShapeDtypeStruct((3, 4, 16, NX), F32),
        ),
        in_specs=[hbm] * 3 + [vm] * 3 + [hbm] * len(names),
        out_specs=(hbm, hbm),
        scratch_shapes=scratch,
        compiler_params=pltpu.CompilerParams(
            collective_id=0, has_side_effects=True, vmem_limit_bytes=58 * 2**20
        ),
    )(
        force,
        mult,
        aux,
        entry_lines.reshape(1, 128),
        entry_owner.reshape(1, 128),
        entry_slot.reshape(1, 128),
        *loads[3:],
    )

    lines = 4
    whole = lambda *shape: pl.BlockSpec(shape, lambda i: (0,) * len(shape))
    part = lambda n: pl.BlockSpec((n, lines, 16, NX), lambda i: (0, i, 0, 0))
    return tuple(
        pl.pallas_call(
            functools.partial(update, lines=lines),
            grid=(16 // lines,),
            out_shape=tuple(jax.ShapeDtypeStruct((n, 16, 16, NX), F32) for n in (3, 6, 6)),
            in_specs=[
                part(3),
                pl.BlockSpec((3, lines, 16, NX), lambda i: (0, i + 1, 0, 0)),
                whole(3, 64, NX),
                part(6),
                whole(16 * lines, 16 * lines),
                pl.BlockSpec((16 * lines, 64), lambda i: (i, 0)),
            ],
            out_specs=tuple(part(n) for n in (3, 6, 6)),
            compiler_params=pltpu.CompilerParams(vmem_limit_bytes=58 * 2**20),
        )(
            vext,
            vext,
            vzh.reshape(3, 64, NX),
            mult,
            jnp.asarray(deriv_rows(lines).astype(jnp.bfloat16)),
            jnp.asarray(t["bz"]),
        )
    )


def solution(mesh):
    field = P(None, "row", "col", None)
    return jax.shard_map(
        local,
        mesh=mesh,
        in_specs=(field, field, field, P(("row", "col")), P(("row", "col"), None), P(("row", "col"))),
        out_specs=(field, field, field),
        check_vma=False,
    )
```
